128 devices in a mesh: expert: 16 (over z, x), tensor: 8 (over y, core).
Axes of the slice: x: 4, y: 4, z: 4, core: 2. Of those that a mesh axis runs over, the one named last changes fastest.
Arguments:
- inputs: bfloat16 [4096, 2048], P(('expert', 'tensor')), may hold values from -6 to 6
- gain_attn: float32 [2048], P('expert'), may hold values from 0.5 to 1.5
- w_q: float32 [2048, 3072], P('expert', 'tensor'), may hold values from -0.125 to 0.125
- w_dkv: float32 [2048, 576], P('expert'), may hold values from -0.125 to 0.125
- gain_latent: float32 [512], P('expert'), may hold values from 0.5 to 1.5
- w_uk: float32 [512, 2048], P('expert', 'tensor'), may hold values from -0.25 to 0.25
- w_uv: float32 [512, 2048], P('expert', 'tensor'), may hold values from -0.25 to 0.25
- w_o: float32 [2048, 2048], P('tensor', 'expert'), may hold values from -1 to 1
- gain_ffn: float32 [2048], P('expert'), may hold values from 0.5 to 1.5
- w_router: float32 [2048, 64], P('expert'), may hold values from -0.0625 to 0.0625
- w_sg: float32 [2048, 2816], P('expert', 'tensor'), may hold values from -0.125 to 0.125
- w_su: float32 [2048, 2816], P('expert', 'tensor'), may hold values from -0.125 to 0.125
- w_sd: float32 [2816, 2048], P('tensor', 'expert'), may hold values from -0.109375 to 0.109375
- w_eg: float32 [64, 1408, 2048], P('expert', 'tensor'), may hold values from -0.125 to 0.125
- w_eu: float32 [64, 1408, 2048], P('expert', 'tensor'), may hold values from -0.125 to 0.125
- w_ed: float32 [64, 1408, 2048], P('expert', 'tensor'), may hold values from -4 to 4
- routes: int32 [4096, 6], P('expert'), may hold values from 0 to 63, all different within a row; in each aligned block of 256 rows (0 to 255, 256 to 511, ...) at most 36 rows name the same one
- seq_lengths: int32 [3], replicated, may hold values from 1 to 3968, 4096 in all
- piece_starts: int32 [8], replicated, may hold values from 0 to 3840, as said below
- out_grad: bfloat16 [4096, 2048], P(('expert', 'tensor')), may hold values from -6 to 6
Outputs:
- layer_out: bfloat16 [4096, 2048], P(('expert', 'tensor'))
- grad_inputs: bfloat16 [4096, 2048], P(('expert', 'tensor'))
- grad_gain_attn: float32 [2048], P('expert')
- grad_w_q: float32 [2048, 3072], P('expert', 'tensor')
- grad_w_dkv: float32 [2048, 576], P('expert')
- grad_gain_latent: float32 [512], P('expert')
- grad_w_uk: float32 [512, 2048], P('expert', 'tensor')
- grad_w_uv: float32 [512, 2048], P('expert', 'tensor')
- grad_w_o: float32 [2048, 2048], P('tensor', 'expert')
- grad_gain_ffn: float32 [2048], P('expert')
- grad_w_router: float32 [2048, 64], P('expert')
- grad_w_sg: float32 [2048, 2816], P('expert', 'tensor')
- grad_w_su: float32 [2048, 2816], P('expert', 'tensor')
- grad_w_sd: float32 [2816, 2048], P('tensor', 'expert')
- grad_w_eg: float32 [64, 1408, 2048], P('expert', 'tensor')
- grad_w_eu: float32 [64, 1408, 2048], P('expert', 'tensor')
- grad_w_ed: float32 [64, 1408, 2048], P('expert', 'tensor')
The draws below stay inside these ranges and needn't reach their ends.
Inputs may be any that keep to these rules, and one draw needn't show every extreme that they name: `routes`: each row names 6 different experts; in the 256 rows of one index of the expert axis no expert is named more than 36 times, and in some such block one expert is named exactly 36 times. `seq_lengths`: the lengths sum to 4096; the longest is 3968. `piece_starts`: piece p starts within positions 2 * 256 * p to 2 * 256 * (p + 1) - 256, so pieces are disjoint and in order.
All inputs are finite; a program needn't handle non-finite values.
Results may differ from the reference program's by a relative error of at most 0.033.
Values may be sent and summed in bfloat16 or wider, within the bound.
No kernel may reach another device: no remote copies, remote signals or barrier semaphores. Data moves between devices by JAX's collectives and lax.ppermute only.
A program may use at most 320 MiB of HBM per device.

```python
import math
import jax
import jax.numpy as jnp
import numpy as np
from jax import lax

D = 2048
H = 16
DN = 128
DR = 64
DV = 128
KVL = 512
FF = 1408
SH = 2816
TOP = 6
TOK_DEV = 256
SEQS = 3
PIECE = 256
EXPERTS = 64
TOKENS = 4096
PIECES = 8
CAP = 36


def draw_piece_starts(key, part):
    key = jax.random.fold_in(key, 11)
    slot_len = 2 * TOK_DEV
    offsets = jax.random.randint(key, (PIECES,), 0, slot_len - PIECE + 1)
    return (jnp.arange(PIECES, dtype=jnp.int32) * slot_len + offsets).astype(jnp.int32)


def shard_levels(rng, extent, pieces, smallest, largest):
    factor_of = 1.0
    for dim, shards_of in pieces:
        steps = jax.random.uniform(jax.random.fold_in(jax.random.fold_in(rng, 6), dim), (shards_of,), jnp.float32, smallest / len(pieces), largest / len(pieces))
        factor_of = factor_of * jnp.repeat(jnp.exp(steps), extent[dim] // shards_of).reshape((-1,) + (1,) * (len(extent) - 1 - dim))
    return factor_of


def profile(count, total, limit, lean):
    portions = [(1 << 20) // math.isqrt(rank ** lean) + 1 for rank in range(2, count + 1)]
    surplus, holding = total - limit - (count - 1), [1] * (count - 1)
    while surplus > 0:
        movable = [i for i in range(count - 1) if holding[i] < limit]
        pool, left = sum([portions[i] for i in movable]), surplus
        for i in movable:
            more = min(limit - holding[i], max(1, left * portions[i] // pool), surplus)
            holding[i] = holding[i] + more
            surplus = surplus - more
    return np.array([limit] + holding)


def uneven(own_key, count, total, limit, lean):
    if count == 2:
        one = jax.random.randint(own_key, (), max(1, total - limit), min(limit, total - 1) + 1)
        return jnp.stack([one, total - one])
    lengths = jnp.asarray(profile(count, total, limit, lean), jnp.int32)
    pairs = (count - 1) // 2
    giver, receiver = lengths[1:1 + 2 * pairs:2], lengths[2:2 + 2 * pairs:2]
    slack = jnp.minimum(giver - 1, limit - receiver)
    passed = jax.random.randint(jax.random.fold_in(own_key, 1), (pairs,), 0, 1 << 20) % (slack + 1)
    lengths = lengths.at[1:1 + 2 * pairs:2].set(giver - passed).at[2:2 + 2 * pairs:2].set(receiver + passed)
    return lengths[jax.random.permutation(jax.random.fold_in(own_key, 2), count)]


def routed_block(stream_key, own, number, rows, amount, top, bound, skew):
    sequence = jax.random.permutation(stream_key, amount)
    heavy_load, common = shares(amount, rows * top, bound, skew, True), shares(amount, rows * top, bound, skew, False)
    places = jnp.arange(amount)

    def named(tallies, offset_by):
        used = int((tallies > 0).sum())
        fixed = max(1, used // 4)
        passed = fixed + (places - fixed + offset_by * (used - fixed)) % max(1, amount - fixed)
        return jnp.zeros((amount,), jnp.int32).at[sequence[jnp.where(places < fixed, places, passed)]].set(jnp.asarray(tallies, jnp.int32))

    tallies = jnp.where(number % 4 == 0, named(heavy_load, number // 4), named(common, number - number // 4 - 1))
    mixed = jax.random.permutation(jax.random.fold_in(own, 3), amount)
    source_of, receiver = mixed[0:amount // 2 * 2:2], mixed[1:amount // 2 * 2:2]
    room = jnp.minimum(tallies[source_of] - 1, bound - tallies[receiver]) // 2
    room = jnp.where((source_of == sequence[0]) | (receiver == sequence[0]) | (tallies[receiver] == 0), 0, jnp.maximum(room, 0))
    passed = jax.random.randint(jax.random.fold_in(own, 4), (amount // 2,), 0, 1 << 20) % (room + 1)
    tallies = tallies.at[source_of].add(-passed).at[receiver].add(passed)
    members = jnp.searchsorted(jnp.cumsum(tallies), jnp.arange(rows * top), side="right").astype(jnp.int32)
    listing = members.reshape(top, rows).T
    listing = listing[jax.random.permutation(jax.random.fold_in(own, 1), rows)]
    offset_by = jax.random.randint(jax.random.fold_in(own, 2), (rows, 1), 0, top)
    return jnp.take_along_axis(listing, (jnp.arange(top)[None, :] + offset_by) % top, axis=1)


def shares(number_of, total, reach, lean, full):
    portions = [(1 << 20) // math.isqrt(grade ** lean) + 1 for grade in range(1, number_of + 1)]
    largest = reach if full else min(reach, max(-(-total // number_of), total * portions[0] // sum(portions)))
    least = 1 if total - largest >= number_of - 1 else 0
    holding, surplus = [largest] + [least] * (number_of - 1), total - largest - least * (number_of - 1)
    while surplus > 0:
        candidates = [i for i in range(1, number_of) if holding[i] < largest] or [i for i in range(1, number_of) if holding[i] < reach]
        whole, left = sum([portions[i] for i in candidates]), surplus
        for i in candidates:
            addition = min(reach - holding[i], max(1, left * portions[i] // whole), surplus)
            holding[i] = holding[i] + addition
            surplus = surplus - addition
    return np.array(holding)


def bell_draw(key, shape, width, reach, pieces=(), kind=jnp.bfloat16):
    gain = shard_levels(key, shape, pieces, -0.22, 0.18) if pieces else 1.0
    values = jax.random.normal(key, shape, jnp.float32) * width * gain
    return jnp.minimum(jnp.maximum(values, -reach), reach).astype(kind)


def setup_inputs(seed: int = 0) -> dict:
    key_list = jax.random.split(jax.random.key(seed), 21)
    inputs = bell_draw(key_list[0], (TOKENS, D), 1.0, 6.0, ((0, 128),))
    gain_attn = jnp.clip(1.0 + 0.1 * jax.random.normal(key_list[1], (D,), jnp.float32), 0.5, 1.5)
    w_q = bell_draw(key_list[2], (D, H * (DN + DR)), D ** -0.5, 0.125, ((0, 16), (1, 8)), jnp.float32)
    w_dkv = bell_draw(key_list[3], (D, KVL + DR), D ** -0.5, 0.125, ((0, 16),), jnp.float32)
    gain_latent = jnp.clip(1.0 + 0.1 * jax.random.normal(key_list[4], (KVL,), jnp.float32), 0.5, 1.5)
    w_uk = bell_draw(key_list[5], (KVL, H * DN), KVL ** -0.5, 0.25, ((0, 16), (1, 8)), jnp.float32)
    w_uv = bell_draw(key_list[6], (KVL, H * DV), KVL ** -0.5, 0.25, ((0, 16), (1, 8)), jnp.float32)
    w_o = bell_draw(key_list[7], (H * DV, D), (H * DV // 64) ** -0.5, 1.0, ((0, 8), (1, 16)), jnp.float32)
    gain_ffn = jnp.clip(1.0 + 0.1 * jax.random.normal(key_list[8], (D,), jnp.float32), 0.5, 1.5)
    w_router = bell_draw(key_list[9], (D, EXPERTS), (4 * D) ** -0.5, 0.0625, ((0, 16),), jnp.float32)
    w_sg = bell_draw(key_list[10], (D, SH), D ** -0.5, 0.125, ((0, 16), (1, 8)), jnp.float32)
    w_su = bell_draw(key_list[11], (D, SH), D ** -0.5, 0.125, ((0, 16), (1, 8)), jnp.float32)
    w_sd = bell_draw(key_list[12], (SH, D), SH ** -0.5, 0.109375, ((0, 8), (1, 16)), jnp.float32)
    w_eg = bell_draw(key_list[13], (EXPERTS, FF, D), D ** -0.5, 0.125, ((0, 16), (1, 8)), jnp.float32)
    w_eu = bell_draw(key_list[14], (EXPERTS, FF, D), D ** -0.5, 0.125, ((0, 16), (1, 8)), jnp.float32)
    w_ed = bell_draw(key_list[15], (EXPERTS, FF, D), (FF // 1024 + 1) ** -0.5, 4.0, ((0, 16), (1, 8)), jnp.float32)
    routes_keys = jax.random.split(jax.random.fold_in(key_list[16], 1), TOKENS // TOK_DEV)
    routes_turns = jax.random.permutation(jax.random.fold_in(key_list[16], 3), TOKENS // TOK_DEV)
    routes = jax.vmap(lambda own, number: routed_block(jax.random.fold_in(key_list[16], 2), own, number, TOK_DEV, EXPERTS, TOP, CAP, 1))(routes_keys, routes_turns).reshape((TOKENS, TOP))
    seq_lengths = uneven(key_list[17], SEQS, TOKENS, TOKENS - TOK_DEV // 2, 0).astype(jnp.int32)
    piece_starts = draw_piece_starts(jax.random.fold_in(key_list[20], 71), 0)
    out_grad = bell_draw(key_list[19], (TOKENS, D), 1.0, 6.0, ((0, 128),))
    return dict(inputs=inputs, gain_attn=gain_attn, w_q=w_q, w_dkv=w_dkv, gain_latent=gain_latent, w_uk=w_uk, w_uv=w_uv, w_o=w_o, gain_ffn=gain_ffn, w_router=w_router, w_sg=w_sg, w_su=w_su, w_sd=w_sd, w_eg=w_eg, w_eu=w_eu, w_ed=w_ed, routes=routes, seq_lengths=seq_lengths, piece_starts=piece_starts, out_grad=out_grad)


EPS = 1e-06
NEG = -1e+30
HIGH = lax.Precision.HIGHEST

@jax.custom_vjp
def low(v):
    return lax.optimization_barrier(v.astype(jnp.bfloat16)).astype(jnp.float32)

@jax.custom_vjp
def low_back(v):
    return v

def low_keep(v):
    return (low(v), None)

def low_pass(kept, grad):
    return (grad,)

def back_keep(v):
    return (v, None)

def back_low(kept, grad):
    return (low(grad),)
low.defvjp(low_keep, low_pass)
low_back.defvjp(back_keep, back_low)

def low_both(values):
    return low_back(low(values))

def matmul_high(left, right):
    return jnp.dot(left, right, precision=HIGH, preferred_element_type=jnp.float32)

def matmul_high_nt(left, right):
    return lax.dot_general(left, right, (((1,), (1,)), ((), ())), precision=HIGH, preferred_element_type=jnp.float32)

def rms_scaled(values):
    return values * lax.rsqrt(lax.optimization_barrier(jnp.mean(values * values, axis=-1, keepdims=True)) + EPS)

def rotate(values, cosine, sine):
    half_dim = values.shape[-1] // 2
    first_half = values[..., :half_dim]
    second = values[..., half_dim:]
    return jnp.concatenate([first_half * cosine - second * sine, second * cosine + first_half * sine], axis=-1)

def tables(position):
    inv_freq = 10000.0 ** (-(2.0 * jnp.arange(DR // 2, dtype=jnp.float32)) / DR)
    angles = position.astype(jnp.float32)[:, None] * inv_freq[None, :]
    return (jnp.cos(angles), jnp.sin(angles))

def locate(row_ids, seq_lengths, piece_starts):
    seq_ends = jnp.cumsum(seq_lengths).astype(jnp.int32)
    starts = seq_ends - seq_lengths
    member = ((row_ids[:, None] >= starts[None, :]) & (row_ids[:, None] < seq_ends[None, :])).astype(jnp.int32)
    seq_id = lax.optimization_barrier(jnp.sum(member * jnp.arange(seq_lengths.shape[0], dtype=jnp.int32)[None, :], axis=1))
    position = row_ids - lax.optimization_barrier(jnp.sum(member * starts[None, :], axis=1))
    inside = ((row_ids[:, None] >= piece_starts[None, :]) & (row_ids[:, None] < piece_starts[None, :] + PIECE)).astype(jnp.int32)
    piece_id = lax.optimization_barrier(jnp.sum(inside * (jnp.arange(piece_starts.shape[0], dtype=jnp.int32) + 1)[None, :], axis=1)) - 1
    return (seq_id, position, piece_id)

def allowed(rows_q, seq_q, piece_q, rows_k, seq_k, piece_k):
    same_seq = seq_q[:, None] == seq_k[None, :]
    before = rows_k[None, :] <= rows_q[:, None]
    picture = (piece_q[:, None] == piece_k[None, :]) & (piece_q[:, None] >= 0)
    return same_seq & (before | picture)

def slot_tables(routes):
    groups = TOKENS // TOK_DEV
    flat_routes = routes.reshape(groups, TOK_DEV * TOP)
    one_hot = (flat_routes[:, :, None] == jnp.arange(EXPERTS, dtype=jnp.int32)[None, None, :]).astype(jnp.int32)
    slot_rank = lax.optimization_barrier(jnp.sum((jnp.cumsum(one_hot, axis=1) - 1) * one_hot, axis=2))
    group_of = jnp.arange(groups, dtype=jnp.int32)[:, None]
    pair_slot = ((group_of * EXPERTS + flat_routes) * CAP + slot_rank).reshape(-1).astype(jnp.int32)
    pair_token = jnp.arange(TOKENS * TOP, dtype=jnp.int32) // TOP
    slot_token = jnp.full((groups * EXPERTS * CAP,), TOKENS, jnp.int32).at[pair_slot].set(pair_token)
    return (pair_slot, slot_token)

def reference(inputs, gain_attn, w_q, w_dkv, gain_latent, w_uk, w_uv, w_o, gain_ffn, w_router, w_sg, w_su, w_sd, w_eg, w_eu, w_ed, routes, seq_lengths, piece_starts, out_grad):
    row_ids = jnp.arange(TOKENS, dtype=jnp.int32)
    seq_id, position, piece_id = locate(row_ids, seq_lengths, piece_starts)
    cosine, sine = tables(position)
    pair_slot, slot_token = slot_tables(routes)
    groups = TOKENS // TOK_DEV
    query_block = TOKENS if TOKENS <= 512 else math.gcd(TOKENS, 512)
    block_count = TOKENS // query_block
    score_scale = (DN + DR) ** (-0.5)

    def forward(inputs, gain_attn, w_q, w_dkv, gain_latent, w_uk, w_uv, w_o, gain_ffn, w_router, w_sg, w_su, w_sd, w_eg, w_eu, w_ed):
        h_one = low(rms_scaled(inputs) * low(gain_attn))
        latent_all = low_back(matmul_high(h_one, low(w_dkv)))
        c_norm = low(rms_scaled(latent_all[:, :KVL]) * low(gain_latent))
        k_rot = low(rotate(latent_all[:, KVL:], cosine, sine))
        q_raw = low_back(matmul_high(h_one, low(w_q))).reshape(TOKENS, H, DN + DR)
        queries = low(jnp.concatenate([q_raw[:, :, :DN], rotate(q_raw[:, :, DN:], cosine[:, None, :], sine[:, None, :])], axis=-1))
        keys = low_both(matmul_high(c_norm, low(w_uk))).reshape(TOKENS, H, DN)
        vals = low_both(matmul_high(c_norm, low(w_uv))).reshape(TOKENS, H, DV)
        full_keys = jnp.concatenate([keys, jnp.broadcast_to(k_rot[:, None, :], (TOKENS, H, DR))], axis=-1)

        def attend(block_item):
            q_blk, rows_blk, seq_blk, piece_blk = block_item
            raw_scores = jnp.einsum('qhd,khd->hqk', q_blk, full_keys, precision=HIGH)
            scores = low_back(score_scale * raw_scores)
            key_mask = allowed(rows_blk, seq_blk, piece_blk, row_ids, seq_id, piece_id)[None]
            row_top = lax.optimization_barrier(jnp.max(jnp.where(key_mask, scores, NEG), axis=-1, keepdims=True))
            sum_total = lax.optimization_barrier(jnp.sum(jnp.where(key_mask, jnp.exp(scores - row_top), 0.0), axis=-1, keepdims=True))
            log_total = row_top + jnp.log(sum_total)
            weights = low(jnp.where(key_mask, jnp.exp(scores - log_total), 0.0))
            return jnp.einsum('hqk,khd->qhd', weights, vals, precision=HIGH)
        attn_raw = lax.map(jax.checkpoint(attend), (queries.reshape(block_count, query_block, H, DN + DR), row_ids.reshape(block_count, query_block), seq_id.reshape(block_count, query_block), piece_id.reshape(block_count, query_block)))
        attn_heads = low_both(attn_raw.reshape(TOKENS, H * DV))
        mid = inputs + low_back(matmul_high(attn_heads, low(w_o)))
        h_two = low(rms_scaled(mid) * low(gain_ffn))
        logits = low_back(matmul_high(h_two, low(w_router)))
        router_probs = jax.nn.softmax(logits, axis=-1)
        gate_values = low(jnp.take_along_axis(router_probs, routes, axis=1))
        shared_gate = low_back(matmul_high(h_two, low(w_sg)))
        shared_up = low_back(matmul_high(h_two, low(w_su)))
        shared_hidden = low(jax.nn.silu(shared_gate) * shared_up)
        shared_out = matmul_high(shared_hidden, low(w_sd))
        padded = jnp.concatenate([h_two, jnp.zeros((1, D), jnp.float32)], axis=0)
        expert_in = padded[slot_token].reshape(groups, EXPERTS, CAP, D).transpose(1, 0, 2, 3)

        def expert(block_item):
            rows_in, gate_w, up_w, down_w = block_item
            flat_rows = rows_in.reshape(groups * CAP, D)
            expert_gate = low_back(matmul_high_nt(flat_rows, low(gate_w)))
            expert_up = low_back(matmul_high_nt(flat_rows, low(up_w)))
            expert_hidden = low(jax.nn.silu(expert_gate) * expert_up)
            return low_back(matmul_high(expert_hidden, low(down_w))).reshape(groups, CAP, D)
        expert_out = lax.map(jax.checkpoint(expert), (expert_in, w_eg, w_eu, w_ed))
        slot_out = expert_out.transpose(1, 0, 2, 3).reshape(groups * EXPERTS * CAP, D)
        pair_out = slot_out[pair_slot].reshape(TOKENS, TOP, D)
        routed_out = lax.optimization_barrier(jnp.sum(gate_values[:, :, None] * pair_out, axis=1))
        return mid + shared_out + routed_out
    layer_value, pullback = jax.vjp(forward, inputs.astype(jnp.float32), gain_attn, w_q, w_dkv, gain_latent, w_uk, w_uv, w_o, gain_ffn, w_router, w_sg, w_su, w_sd, w_eg, w_eu, w_ed)
    grads = pullback(out_grad.astype(jnp.float32))
    return (layer_value.astype(jnp.bfloat16), grads[0].astype(jnp.bfloat16), grads[1], grads[2], grads[3], grads[4], grads[5], grads[6], grads[7], grads[8], grads[9], grads[10], grads[11], grads[12], grads[13], grads[14], grads[15])
```

```python
import jax
import jax.numpy as jnp
from jax import lax
from jax.experimental import pallas as pl
from jax.experimental.pallas import tpu as pltpu
from jax.sharding import Mesh, PartitionSpec as P

D = 2048
H_DEV = 2
DN = 128
DR = 64
KVL = 512
PIECE = 256
EXPERTS = 64
ROWS = 256
OWN = 32
SLOTS = 40
FFH = 704
SHP = 384
KEYS = 4096
CHUNK = 512
EPS = 1e-06
NEG = -1e30
SCALE = (DN + DR) ** (-0.5)
EX = ("z", "x")
HALF = jnp.bfloat16
WIDE = jnp.float32


def dot_nn(left, right):
    return jnp.dot(left, right, preferred_element_type=WIDE)


def dot_nt(left, right):
    return lax.dot_general(left, right, (((1,), (1,)), ((), ())), preferred_element_type=WIDE)


def dot_tn(left, right):
    return lax.dot_general(left, right, (((0,), (0,)), ((), ())), preferred_element_type=WIDE)


def inv_rms(values):
    return lax.rsqrt(jnp.mean(values * values, axis=-1, keepdims=True) + EPS)


def norm_back(grad, normed, row_scale, gain):
    scaled = grad * gain
    inner_mean = jnp.mean(scaled * normed, axis=-1, keepdims=True)
    return (row_scale * (scaled - normed * inner_mean), jnp.sum(grad * normed, axis=0))


def swap_core(value):
    return lax.ppermute(value, "c", [(0, 1), (1, 0)])


def shift_y(value, by):
    return lax.ppermute(value, "y", [(i, (i + by) % 4) for i in range(4)])


def spread(value, axes):
    return lax.all_to_all(value, axes, split_axis=0, concat_axis=0, tiled=True)


def gather_rows(value, yi, ci):
    n = value.shape[1]
    block = jnp.zeros((4, OWN, n), value.dtype)
    block = lax.dynamic_update_slice(block, value[None], (yi, 0, 0))
    for by in (1, 2, 3):
        block = lax.dynamic_update_slice(block, shift_y(value, by)[None], ((yi - by) % 4, 0, 0))
    other = swap_core(block)
    first = jnp.where(ci == 0, block, other)
    second = jnp.where(ci == 0, other, block)
    return jnp.stack([first, second], axis=1).reshape(ROWS, n)


def sum_rows(value, ci):
    n = value.shape[1]
    parts = value.reshape(4, 2, OWN, n)
    mine = lax.dynamic_index_in_dim(parts, ci, 1, keepdims=False)
    theirs = lax.dynamic_index_in_dim(parts, 1 - ci, 1, keepdims=False)
    pair = (mine.astype(WIDE) + swap_core(theirs).astype(WIDE)).astype(HALF)
    return jnp.sum(spread(pair, "y").astype(WIDE), axis=0)


def sum_experts(value):
    rows, width = value.shape
    parts = spread(value.reshape(16, rows // 16, width), EX)
    return jnp.sum(parts.astype(WIDE), axis=0)


def spans(row_ids, seq_lengths, piece_starts):
    ends = jnp.cumsum(seq_lengths)
    starts = ends - seq_lengths
    member = (row_ids[:, None] >= starts[None, :]) & (row_ids[:, None] < ends[None, :])
    member = member.astype(jnp.int32)
    low = jnp.sum(member * starts[None, :], axis=1)
    end = jnp.sum(member * ends[None, :], axis=1)
    inside = (row_ids[:, None] >= piece_starts[None, :]) & (
        row_ids[:, None] < piece_starts[None, :] + PIECE
    )
    piece_last = jnp.max(jnp.where(inside, piece_starts[None, :] + (PIECE - 1), -1), axis=1)
    high = jnp.where(piece_last >= 0, jnp.minimum(piece_last, end - 1), row_ids)
    return row_ids - low, low, high


def head_query(q_ref, head):
    lane = lax.broadcasted_iota(jnp.int32, (ROWS, 128), 1)
    rot = q_ref[:, 256:384]
    rot = jnp.where((lane // 32) % 2 == head, rot, jnp.zeros_like(rot))
    return jnp.concatenate([q_ref[:, 128 * head : 128 * head + 128], rot], axis=1)


def attend_kernel(q_ref, kv_ref, low_ref, high_ref, p_ref, o_ref, s_ref):
    low = low_ref[...]
    high = high_ref[...]
    for head in range(H_DEV):
        query = head_query(q_ref, head)

        def scores_step(i, top):
            at = pl.multiple_of(i * CHUNK, CHUNK)
            key = jnp.concatenate(
                [
                    kv_ref[pl.ds(at, CHUNK), 128 * head : 128 * head + 128],
                    kv_ref[pl.ds(at, CHUNK), 512:640],
                ],
                axis=1,
            )
            scores = dot_nt(key, query) * SCALE
            col = lax.broadcasted_iota(jnp.int32, (CHUNK, ROWS), 0) + at
            scores = jnp.where((col >= low) & (col <= high), scores, NEG)
            s_ref[pl.ds(at, CHUNK), :] = scores
            return jnp.maximum(top, jnp.max(scores.reshape(CHUNK // 8, 8, ROWS), axis=0))

        top = lax.fori_loop(
            0, KEYS // CHUNK, scores_step, jnp.full((8, ROWS), NEG, WIDE)
        )
        top = jnp.max(top, axis=0, keepdims=True)

        def exp_step(i, total):
            at = pl.multiple_of(i * CHUNK, CHUNK)
            weights = jnp.exp(s_ref[pl.ds(at, CHUNK), :] - top)
            s_ref[pl.ds(at, CHUNK), :] = weights
            return total + jnp.sum(weights.reshape(CHUNK // 8, 8, ROWS), axis=0)

        total = lax.fori_loop(0, KEYS // CHUNK, exp_step, jnp.zeros((8, ROWS), WIDE))
        inverse = 1.0 / jnp.sum(total, axis=0, keepdims=True)

        def value_step(i, acc):
            at = pl.multiple_of(i * CHUNK, CHUNK)
            probs = (s_ref[pl.ds(at, CHUNK), :] * inverse).astype(HALF)
            p_ref[head, pl.ds(at, CHUNK), :] = probs
            value = kv_ref[pl.ds(at, CHUNK), 256 + 128 * head : 384 + 128 * head]
            return acc + dot_tn(value, probs)

        out = lax.fori_loop(0, KEYS // CHUNK, value_step, jnp.zeros((DN, ROWS), WIDE))
        o_ref[:, 128 * head : 128 * head + 128] = out.T


def attend(queries, kv_all, low, high):
    vmem = pl.BlockSpec(memory_space=pltpu.VMEM)
    return pl.pallas_call(
        attend_kernel,
        out_shape=(
            jax.ShapeDtypeStruct((H_DEV, KEYS, ROWS), HALF),
            jax.ShapeDtypeStruct((ROWS, H_DEV * DN), WIDE),
        ),
        in_specs=[vmem] * 4,
        out_specs=(vmem, vmem),
        scratch_shapes=[pltpu.VMEM((KEYS, ROWS), WIDE)],
        compiler_params=pltpu.CompilerParams(vmem_limit_bytes=40 * 1024 * 1024),
        cost_estimate=pl.CostEstimate(
            flops=2 * H_DEV * ROWS * KEYS * 384, bytes_accessed=12 << 20, transcendentals=2 << 20
        ),
    )(queries, kv_all, low, high)


def attend_back_kernel(q_ref, kv_ref, p_ref, do_ref, delta_ref, dkv_ref, dq_ref, acc_ref):
    acc_ref[...] = jnp.zeros_like(acc_ref)
    query = [head_query(q_ref, head) for head in range(H_DEV)]

    def step(i, carry):
        at = pl.multiple_of(i * CHUNK, CHUNK)
        rot = kv_ref[pl.ds(at, CHUNK), 512:640]
        d_rot = jnp.zeros((CHUNK, 128), WIDE)
        for head in range(H_DEV):
            d_out = do_ref[:, 128 * head : 128 * head + 128]
            value = kv_ref[pl.ds(at, CHUNK), 256 + 128 * head : 384 + 128 * head]
            probs = p_ref[head, pl.ds(at, CHUNK), :]
            d_probs = dot_nt(value, d_out)
            d_scores = (
                probs.astype(WIDE) * (d_probs - delta_ref[head : head + 1, :])
            ).astype(HALF)
            d_key = dot_nn(d_scores, query[head]) * SCALE
            dkv_ref[pl.ds(at, CHUNK), 128 * head : 128 * head + 128] = d_key[:, :128].astype(HALF)
            d_rot = d_rot + d_key[:, 128:]
            dkv_ref[pl.ds(at, CHUNK), 256 + 128 * head : 384 + 128 * head] = dot_nn(
                probs, d_out
            ).astype(HALF)
            key = jnp.concatenate(
                [kv_ref[pl.ds(at, CHUNK), 128 * head : 128 * head + 128], rot], axis=1
            )
            acc_ref[head] += dot_tn(key, d_scores)
        dkv_ref[pl.ds(at, CHUNK), 512:640] = d_rot.astype(HALF)
        return carry

    lax.fori_loop(0, KEYS // CHUNK, step, 0)
    lane = lax.broadcasted_iota(jnp.int32, (ROWS, 128), 1)
    d_rot = jnp.zeros((ROWS, 128), WIDE)
    for head in range(H_DEV):
        d_query = acc_ref[head].T * SCALE
        dq_ref[:, 128 * head : 128 * head + 128] = d_query[:, :128]
        d_rot = jnp.where((lane // 32) % 2 == head, d_query[:, 128:], d_rot)
    dq_ref[:, 256:384] = d_rot


def attend_back(queries, kv_all, probs, d_heads, delta):
    vmem = pl.BlockSpec(memory_space=pltpu.VMEM)
    return pl.pallas_call(
        attend_back_kernel,
        out_shape=(
            jax.ShapeDtypeStruct((KEYS, 640), HALF),
            jax.ShapeDtypeStruct((ROWS, 384), WIDE),
        ),
        in_specs=[vmem] * 5,
        out_specs=(vmem, vmem),
        scratch_shapes=[pltpu.VMEM((H_DEV, 256, ROWS), WIDE)],
        compiler_params=pltpu.CompilerParams(vmem_limit_bytes=40 * 1024 * 1024),
        cost_estimate=pl.CostEstimate(
            flops=2 * H_DEV * ROWS * KEYS * 768, bytes_accessed=16 << 20, transcendentals=0
        ),
    )(queries, kv_all, probs, d_heads, delta)


def pack_query_columns(w):
    return jnp.concatenate(
        [w[:, 0:128], w[:, 192:320], w[:, 128:160], w[:, 320:352], w[:, 160:192], w[:, 352:384]],
        axis=1,
    )


def unpack_query_columns(w):
    return jnp.concatenate(
        [w[:, 0:128], w[:, 256:288], w[:, 320:352], w[:, 128:256], w[:, 288:320], w[:, 352:384]],
        axis=1,
    )


def pad_cols(w, width):
    return jnp.pad(w, ((0, 0), (0, width - w.shape[1])))


def silu_parts(gate):
    sig = jax.nn.sigmoid(gate)
    return gate * sig, sig * (1.0 + gate * (1.0 - sig))


def body(
    inputs,
    gain_attn,
    w_q,
    w_dkv,
    gain_latent,
    w_uk,
    w_uv,
    w_o,
    gain_ffn,
    w_router,
    w_sg,
    w_su,
    w_sd,
    w_eg,
    w_eu,
    w_ed,
    routes,
    seq_lengths,
    piece_starts,
    out_grad,
):
    zi, xi, yi, ci = (lax.axis_index(name) for name in ("z", "x", "y", "c"))
    ei = zi * 4 + xi
    ti = yi * 2 + ci

    gain_cols = jnp.stack([gain_attn, gain_ffn, jnp.pad(gain_latent, (0, 96))], axis=1)
    w_router_perm = w_router.reshape(128, 16, 4).transpose(0, 2, 1).reshape(128, EXPERTS)
    first_pack = jnp.concatenate(
        [
            pack_query_columns(w_q),
            w_dkv,
            w_router_perm,
            jnp.concatenate([w_uk, w_uv], axis=1).reshape(128, 128),
            w_o.T,
            pad_cols(gain_cols, 128),
        ],
        axis=1,
    ).astype(HALF)
    first_all = lax.all_gather(first_pack, EX, axis=0, tiled=True)
    second_pack = jnp.concatenate(
        [pad_cols(w_sg, SHP), pad_cols(w_su, SHP), pad_cols(w_sd.T, SHP)], axis=1
    ).astype(HALF)

    in_rows = gather_rows(inputs, yi, ci)
    g_rows = gather_rows(out_grad, yi, ci)

    weg_b = spread(w_eg.astype(HALF), "y").reshape(FFH, D)
    weu_b = spread(w_eu.astype(HALF), "y").reshape(FFH, D)
    wed_b = spread(w_ed.astype(HALF), "y").reshape(FFH, D)

    wq_b = first_all[:, 0:384]
    blk_b = first_all[:, 384:1024]
    wkv_b = first_all[:, 1024:1152].reshape(KVL, 512)
    wot_b = first_all[:, 1152:1408]
    pick = jnp.eye(8, 128, dtype=HALF)
    gains = dot_nt(pick, first_all[:, 1408:1536])
    gain_one = gains[0]
    gain_two = gains[1]
    gain_lat = gains[2].reshape(16, 128)[:, :32].reshape(KVL)

    routes_t = routes.T
    expert_ids = 4 * lax.broadcasted_iota(jnp.int32, (16, 1, ROWS), 0) + yi
    named = jnp.max((routes_t[None] == expert_ids).astype(WIDE), axis=1)
    earlier = (
        lax.broadcasted_iota(jnp.int32, (ROWS, ROWS), 0)
        < lax.broadcasted_iota(jnp.int32, (ROWS, ROWS), 1)
    ).astype(HALF)
    rank = dot_nn(named.astype(HALF), earlier)
    slot_ids = lax.broadcasted_iota(jnp.int32, (16, SLOTS, ROWS), 1).astype(WIDE)
    picked = (named[:, None, :] > 0.5) & (rank[:, None, :] == slot_ids)
    select = picked.astype(HALF).reshape(16 * SLOTS, ROWS)

    def half_cols(value):
        return lax.dynamic_slice_in_dim(value, ci * (D // 2), D // 2, value.ndim - 1)

    def join_halves(mine):
        other = swap_core(mine)
        return jnp.concatenate(
            [jnp.where(ci == 0, mine, other), jnp.where(ci == 0, other, mine)], axis=1
        )

    g_half = half_cols(g_rows)
    g_sent = dot_nn(select, g_half).astype(HALF).reshape(16, SLOTS, D // 2)
    g_slots = join_halves(spread(g_sent, EX).reshape(16 * SLOTS, D // 2))

    row_ids = ei * ROWS + jnp.arange(ROWS, dtype=jnp.int32)
    position, low, high = spans(row_ids, seq_lengths, piece_starts)
    inv_freq = 10000.0 ** (-(2.0 * jnp.arange(DR // 2, dtype=WIDE)) / DR)
    angles = position.astype(WIDE)[:, None] * inv_freq[None, :]
    cosine, sine = jnp.cos(angles), jnp.sin(angles)
    cos4 = jnp.concatenate([cosine] * 4, axis=1)
    sin4 = jnp.concatenate([-sine, -sine, sine, sine], axis=1)

    def swap_halves(v):
        return jnp.concatenate([v[:, 64:], v[:, :64]], axis=1)

    in_wide = in_rows.astype(WIDE)
    h_one = (in_wide * inv_rms(in_wide) * gain_one).astype(HALF)
    latent_all = dot_nn(h_one, blk_b)
    lat_part = latent_all[:, :KVL]
    scale_lat = inv_rms(lat_part)
    normed_lat = lat_part * scale_lat
    c_norm = (normed_lat * gain_lat).astype(HALF)
    rope_a, rope_b = latent_all[:, 512:544], latent_all[:, 544:576]
    rope = jnp.concatenate([rope_a, rope_a, rope_b, rope_b], axis=1)
    k_rot = rope * cos4 + swap_halves(rope) * sin4
    kv_local = jnp.concatenate([dot_nn(c_norm, wkv_b), k_rot], axis=1).astype(HALF)
    kv_all = lax.all_gather(kv_local, EX, axis=0, tiled=True)
    q_raw = dot_nn(h_one, wq_b)
    q_rot = q_raw[:, 256:]
    q_rot = q_rot * cos4 + swap_halves(q_rot) * sin4
    queries = jnp.concatenate([q_raw[:, :256], q_rot], axis=1).astype(HALF)
    second_all = lax.all_gather(second_pack, EX, axis=0, tiled=True)
    probs, heads_wide = attend(queries, kv_all, low[None, :], high[None, :])
    attn_heads = heads_wide.astype(HALF)
    attn_own = sum_rows(dot_nt(attn_heads, wot_b).astype(HALF), ci)

    in_own = inputs.astype(WIDE)
    g_own = out_grad.astype(WIDE)
    mid_own = in_own + attn_own
    scale_two = inv_rms(mid_own)
    normed_two = mid_own * scale_two
    h_two_own = (normed_two * gain_two).astype(HALF)
    h_two = gather_rows(h_two_own, yi, ci)

    rope_router_b = blk_b[:, 512:640]
    logits_t = lax.dot_general(
        rope_router_b, h_two, (((0,), (1,)), ((), ())), preferred_element_type=WIDE
    )[64:]
    probs_t = jax.nn.softmax(logits_t, axis=0)
    gate_t = lax.dynamic_slice_in_dim(probs_t, yi * 16, 16, 0).astype(HALF).astype(WIDE)
    gated = jnp.where(picked, gate_t[:, None, :], 0.0)
    slot_gate = jnp.sum(gated, axis=2)
    gated = gated.astype(HALF).reshape(16 * SLOTS, ROWS)

    x_sent = dot_nn(select, half_cols(h_two)).astype(HALF).reshape(16, SLOTS, D // 2)
    x_sent = jnp.concatenate(
        [x_sent, jnp.broadcast_to(slot_gate[:, :, None], (16, SLOTS, 128)).astype(HALF)], axis=2
    )
    x_recv = spread(x_sent, EX).reshape(16 * SLOTS, D // 2 + 128)
    x_slots = join_halves(x_recv[:, : D // 2])
    gate_slots = x_recv[:, D // 2 : D // 2 + 1].astype(WIDE)

    wgu_b = second_all[:, : 2 * SHP]
    wsdt_b = second_all[:, 2 * SHP :]
    shared_pre = dot_nn(h_two, wgu_b)
    shared_gate, shared_up = shared_pre[:, :SHP], shared_pre[:, SHP:]
    shared_silu, shared_slope = silu_parts(shared_gate)
    shared_hidden = (shared_silu * shared_up).astype(HALF)
    shared_out = dot_nt(shared_hidden, wsdt_b)
    d_shared_hidden = dot_nn(g_rows, wsdt_b)
    d_shared_pre = jnp.concatenate(
        [d_shared_hidden * shared_up * shared_slope, d_shared_hidden * shared_silu], axis=1
    ).astype(HALF)
    d_shared_in = dot_nt(d_shared_pre, wgu_b)
    shared_grads = jnp.concatenate(
        [
            dot_tn(h_two, d_shared_pre).astype(HALF),
            dot_tn(g_rows, shared_hidden).astype(HALF),
        ],
        axis=1,
    )

    expert_gate = dot_nt(x_slots, weg_b)
    expert_up = dot_nt(x_slots, weu_b)
    expert_silu, expert_slope = silu_parts(expert_gate)
    expert_hidden = (expert_silu * expert_up).astype(HALF)
    expert_out = dot_nn(expert_hidden, wed_b).astype(HALF)

    def pair_sum(value):
        mine = half_cols(value)
        theirs = lax.dynamic_slice_in_dim(value, (1 - ci) * (D // 2), D // 2, 1)
        total = mine.astype(WIDE) + swap_core(theirs).astype(WIDE)
        return total.astype(HALF).reshape(16, SLOTS, D // 2)

    out_back = spread(pair_sum(expert_out), EX).reshape(16 * SLOTS, D // 2)
    d_slot_out = (g_slots.astype(WIDE) * gate_slots).astype(HALF)
    d_expert_hidden = dot_nt(d_slot_out, wed_b)
    d_expert_gate = (d_expert_hidden * expert_up * expert_slope).astype(HALF)
    d_expert_up = (d_expert_hidden * expert_silu).astype(HALF)
    d_expert_in = (dot_nn(d_expert_gate, weg_b) + dot_nn(d_expert_up, weu_b)).astype(HALF)
    in_back = spread(pair_sum(d_expert_in), EX).reshape(16 * SLOTS, D // 2)

    def expert_grad(left, right):
        grad = dot_tn(left, right).astype(HALF).reshape(4, FFH // 4, D)
        return spread(grad, "y").astype(WIDE)

    grad_ed = expert_grad(expert_hidden, d_slot_out)
    grad_eg = expert_grad(d_expert_gate, x_slots)
    grad_eu = expert_grad(d_expert_up, x_slots)

    def place_half(value):
        zero = jnp.zeros_like(value)
        return jnp.concatenate(
            [jnp.where(ci == 0, value, zero), jnp.where(ci == 0, zero, value)], axis=1
        )

    routed_out = dot_tn(gated, out_back)
    ffn_part = (shared_out + place_half(routed_out)).astype(HALF)
    slot_dots = dot_nt(out_back, g_half).reshape(16, SLOTS, ROWS)
    d_route_t = jnp.sum(jnp.where(picked, slot_dots, 0.0), axis=1).astype(HALF)
    lane_at = (
        lax.broadcasted_iota(jnp.int32, (16, 128), 0) + yi * 16
        == lax.broadcasted_iota(jnp.int32, (16, 128), 1)
    ).astype(HALF)
    d_route_part = dot_tn(d_route_t, lane_at)
    d_h_part = d_shared_in + place_half(dot_tn(select, in_back))
    back_own = sum_rows(jnp.concatenate([d_h_part, d_route_part], axis=1).astype(HALF), ci)
    layer_out = (mid_own + sum_rows(ffn_part, ci)).astype(HALF)

    logits_own = dot_nn(h_two_own, rope_router_b)[:, 64:]
    probs_own = jax.nn.softmax(logits_own, axis=-1)
    d_route = back_own[:, D : D + EXPERTS]
    d_logits = (
        probs_own * (d_route - jnp.sum(probs_own * d_route, axis=-1, keepdims=True))
    ).astype(HALF)
    d_logits_pad = jnp.pad(d_logits, ((0, 0), (64, 0)))
    d_h_two = back_own[:, :D] + dot_nt(d_logits_pad, rope_router_b)
    d_mid_norm, gain_two_part = norm_back(d_h_two, normed_two, scale_two, gain_two)
    d_mid_own = d_mid_norm + g_own
    mid_all = gather_rows(
        jnp.concatenate([d_mid_own.astype(HALF), d_logits_pad], axis=1), yi, ci
    )
    d_attn_b = mid_all[:, :D]
    d_logits_all = mid_all[:, D + 64 :]

    grad_ot = dot_tn(d_attn_b, attn_heads).astype(HALF)
    d_heads = dot_nn(d_attn_b, wot_b).astype(HALF)
    delta = jnp.sum(
        (d_heads.astype(WIDE) * heads_wide).reshape(ROWS, H_DEV, DN), axis=2
    ).T
    shared_sum = lax.psum_scatter(
        jnp.concatenate([shared_grads, grad_ot], axis=1), EX, scatter_dimension=0, tiled=True
    ).astype(WIDE)
    d_kv, d_q = attend_back(queries, kv_all, probs, d_heads, delta)
    d_kv_rows = sum_experts(d_kv)
    d_q_rot = d_q[:, 256:]
    d_q_rot = d_q_rot * cos4 - swap_halves(d_q_rot) * sin4
    d_queries = jnp.concatenate([d_q[:, :256], d_q_rot], axis=1).astype(HALF)
    grad_q = sum_experts(dot_tn(h_one, d_queries).astype(HALF))
    d_one_own = sum_rows(dot_nt(d_queries, wq_b).astype(HALF), ci)
    d_kv_b = d_kv_rows[:, :512].astype(HALF)
    grad_kv = sum_experts(dot_tn(c_norm, d_kv_b).astype(HALF))
    d_lat_part = jnp.concatenate([dot_nt(d_kv_b, wkv_b), d_kv_rows[:, 512:]], axis=1)
    d_lat_own = sum_rows(d_lat_part.astype(HALF), ci)

    def own_rows(value):
        return lax.dynamic_slice_in_dim(value, ti * OWN, OWN, 0)

    cos_own, sin_own = own_rows(cos4), own_rows(sin4)
    d_rope = d_lat_own[:, 512:]
    d_rope = d_rope * cos_own - swap_halves(d_rope) * sin_own
    d_rope = jnp.concatenate(
        [d_rope[:, 0:32] + d_rope[:, 32:64], d_rope[:, 64:96] + d_rope[:, 96:128]], axis=1
    )
    d_lat, gain_lat_part = norm_back(
        d_lat_own[:, :512], own_rows(normed_lat), own_rows(scale_lat), gain_lat
    )
    d_latent = jnp.concatenate([d_lat, d_rope], axis=1).astype(HALF)
    d_latent_pad = jnp.pad(d_latent, ((0, 0), (0, 64)))
    d_h_one = d_one_own + dot_nt(d_latent_pad, blk_b)
    scale_one = inv_rms(in_own)
    normed_one = in_own * scale_one
    d_in_norm, gain_one_part = norm_back(d_h_one, normed_one, scale_one, gain_one)
    grad_inputs = (d_mid_own + d_in_norm).astype(HALF)

    d_latent_all = gather_rows(d_latent_pad, yi, ci)
    grad_dkv = dot_tn(h_one, lax.dynamic_slice_in_dim(d_latent_all, ti * 72, 72, 1))
    grad_router = dot_tn(h_two, lax.dynamic_slice_in_dim(d_logits_all, ti * 8, 8, 1))
    gain_lat_wide = jnp.pad(gain_lat_part.reshape(16, 32), ((0, 0), (0, 96))).reshape(D)
    gain_rows = jnp.stack([gain_one_part, gain_two_part, gain_lat_wide], axis=0).astype(HALF)
    gain_at = (
        lax.broadcasted_iota(jnp.int32, (3, 48), 0) == lax.broadcasted_iota(jnp.int32, (3, 48), 1)
    ).astype(HALF)
    last_part = jnp.concatenate([grad_dkv, grad_router, dot_tn(gain_rows, gain_at)], axis=1)
    last_sum = sum_experts(last_part.astype(HALF))
    last_all = spread(
        jnp.broadcast_to(last_sum.astype(HALF)[None], (8, 128, 128)), ("y", "c")
    )
    sum_dkv = last_all[:, :, :72].transpose(1, 0, 2).reshape(128, 576).astype(WIDE)
    sum_router = last_all[:, :, 72:80].transpose(1, 0, 2).reshape(128, 4, 16)
    sum_router = sum_router.transpose(0, 2, 1).reshape(128, EXPERTS).astype(WIDE)
    gain_sums = jnp.sum(last_all[:, :, 80:83].astype(WIDE), axis=0)

    return (
        layer_out,
        grad_inputs,
        gain_sums[:, 0],
        unpack_query_columns(grad_q),
        sum_dkv,
        gain_sums[:32, 2],
        grad_kv[:, :256],
        grad_kv[:, 256:],
        shared_sum[:, 3 * SHP :].T,
        gain_sums[:, 1],
        sum_router,
        shared_sum[:, :352],
        shared_sum[:, SHP : SHP + 352],
        shared_sum[:, 2 * SHP : 2 * SHP + 352].T,
        grad_eg,
        grad_eu,
        grad_ed,
    )


def solution(mesh):
    grid = Mesh(mesh.devices.reshape(4, 4, 4, 2), ("z", "x", "y", "c"))
    ten = ("y", "c")
    rows = P(("z", "x", "y", "c"), None)
    wide = P(EX, ten)
    tall = P(ten, EX)
    expert = P(EX, ten, None)
    return jax.shard_map(
        body,
        mesh=grid,
        in_specs=(
            rows,
            P(EX),
            wide,
            P(EX, None),
            P(EX),
            wide,
            wide,
            tall,
            P(EX),
            P(EX, None),
            wide,
            wide,
            tall,
            expert,
            expert,
            expert,
            P(EX, None),
            P(),
            P(),
            rows,
        ),
        out_specs=(
            rows,
            rows,
            P(EX),
            wide,
            P(EX, None),
            P(EX),
            wide,
            wide,
            tall,
            P(EX),
            P(EX, None),
            wide,
            wide,
            tall,
            expert,
            expert,
            expert,
        ),
        check_vma=False,
    )
```

```python
import jax
import jax.numpy as jnp
from jax import lax
from jax.experimental import pallas as pl
from jax.experimental.layout import Layout, with_layout_constraint
from jax.experimental.pallas import tpu as pltpu
from jax.sharding import Mesh, PartitionSpec as P

D = 2048
H_DEV = 2
DN = 128
DV = 128
DR = 64
KVL = 512
PIECE = 256
EXPERTS = 64
ROWS = 256
OWN = 32
SLOTS = 40
FFH = 704
FFS = 176
FFP = 768
SHP = 384
KEYS = 4096
CHUNK = 512
EPS = 1e-06
NEG = -1e30
SCALE = (DN + DR) ** (-0.5)
EX = ("z", "x")
HALF = jnp.bfloat16
WIDE = jnp.float32


def dot_nn(left, right):
    return jnp.dot(left, right, preferred_element_type=WIDE)


def dot_nt(left, right):
    return lax.dot_general(left, right, (((1,), (1,)), ((), ())), preferred_element_type=WIDE)


def dot_tn(left, right):
    return lax.dot_general(left, right, (((0,), (0,)), ((), ())), preferred_element_type=WIDE)


def inv_rms(values):
    return lax.rsqrt(jnp.mean(values * values, axis=-1, keepdims=True) + EPS)


def norm_back(grad, normed, row_scale, gain):
    scaled = grad * gain
    inner_mean = jnp.mean(scaled * normed, axis=-1, keepdims=True)
    return (row_scale * (scaled - normed * inner_mean), jnp.sum(grad * normed, axis=0))


def row_major(value):
    return with_layout_constraint(value, Layout(major_to_minor=(0, 1)))


def swap_core(value):
    return lax.ppermute(value, "c", [(0, 1), (1, 0)])


def shift_y(value, by):
    return lax.ppermute(value, "y", [(i, (i + by) % 4) for i in range(4)])


def spread(value, axes):
    return lax.all_to_all(value, axes, split_axis=0, concat_axis=0, tiled=True)


def gather_rows(value, yi, ci):
    n = value.shape[1]
    block = jnp.zeros((4, OWN, n), value.dtype)
    block = lax.dynamic_update_slice(block, value[None], (yi, 0, 0))
    for by in (1, 2, 3):
        block = lax.dynamic_update_slice(block, shift_y(value, by)[None], ((yi - by) % 4, 0, 0))
    other = swap_core(block)
    first = jnp.where(ci == 0, block, other)
    second = jnp.where(ci == 0, other, block)
    return jnp.stack([first, second], axis=1).reshape(ROWS, n)


def core_sum(value, ci):
    parts = value.reshape(4, 2, OWN, value.shape[1])
    mine = lax.dynamic_index_in_dim(parts, ci, 1, keepdims=False)
    theirs = lax.dynamic_index_in_dim(parts, 1 - ci, 1, keepdims=False)
    return (mine.astype(WIDE) + swap_core(theirs).astype(WIDE)).astype(HALF)


def row_sum(pair, yi):
    total = lax.dynamic_index_in_dim(pair, yi, 0, keepdims=False).astype(WIDE)
    for by in (1, 2, 3):
        piece = lax.dynamic_index_in_dim(pair, (yi + by) % 4, 0, keepdims=False)
        total = total + shift_y(piece, by).astype(WIDE)
    return total


def sum_rows(value, yi, ci):
    return row_sum(core_sum(value, ci), yi)


def sum_experts(value):
    rows, width = value.shape
    parts = spread(value.reshape(16, rows // 16, width), EX)
    return jnp.sum(parts.astype(WIDE), axis=0)


def spans(row_ids, seq_lengths, piece_starts):
    ends = jnp.cumsum(seq_lengths)
    starts = ends - seq_lengths
    member = (row_ids[:, None] >= starts[None, :]) & (row_ids[:, None] < ends[None, :])
    member = member.astype(jnp.int32)
    low = jnp.sum(member * starts[None, :], axis=1)
    end = jnp.sum(member * ends[None, :], axis=1)
    inside = (row_ids[:, None] >= piece_starts[None, :]) & (
        row_ids[:, None] < piece_starts[None, :] + PIECE
    )
    piece_last = jnp.max(jnp.where(inside, piece_starts[None, :] + (PIECE - 1), -1), axis=1)
    high = jnp.where(piece_last >= 0, jnp.minimum(piece_last, end - 1), row_ids)
    return row_ids - low, low, high


def head_query(q_ref, head):
    lane = lax.broadcasted_iota(jnp.int32, (ROWS, 128), 1)
    rot = q_ref[:, 256:384]
    rot = jnp.where((lane // 32) % 2 == head, rot, jnp.zeros_like(rot))
    return jnp.concatenate([q_ref[:, 128 * head : 128 * head + 128], rot], axis=1)


def attend_kernel(q_ref, kv_ref, rot_ref, low_ref, high_ref, p_ref, o_ref, s_ref):
    low = low_ref[...]
    high = high_ref[...]
    for head in range(H_DEV):
        query = head_query(q_ref, head)

        def scores_step(i, top):
            at = pl.multiple_of(i * CHUNK, CHUNK)
            key = jnp.concatenate(
                [
                    kv_ref[pl.ds(at, CHUNK), 128 * head : 128 * head + 128],
                    rot_ref[pl.ds(at, CHUNK), :],
                ],
                axis=1,
            )
            scores = dot_nt(key, query) * SCALE
            col = lax.broadcasted_iota(jnp.int32, (CHUNK, ROWS), 0) + at
            scores = jnp.where((col >= low) & (col <= high), scores, NEG)
            s_ref[pl.ds(at, CHUNK), :] = scores
            return jnp.maximum(top, jnp.max(scores.reshape(CHUNK // 8, 8, ROWS), axis=0))

        top = lax.fori_loop(
            0, KEYS // CHUNK, scores_step, jnp.full((8, ROWS), NEG, WIDE)
        )
        top = jnp.max(top, axis=0, keepdims=True)

        def exp_step(i, total):
            at = pl.multiple_of(i * CHUNK, CHUNK)
            weights = jnp.exp(s_ref[pl.ds(at, CHUNK), :] - top)
            s_ref[pl.ds(at, CHUNK), :] = weights
            return total + jnp.sum(weights.reshape(CHUNK // 8, 8, ROWS), axis=0)

        total = lax.fori_loop(0, KEYS // CHUNK, exp_step, jnp.zeros((8, ROWS), WIDE))
        inverse = 1.0 / jnp.sum(total, axis=0, keepdims=True)

        def value_step(i, acc):
            at = pl.multiple_of(i * CHUNK, CHUNK)
            probs = (s_ref[pl.ds(at, CHUNK), :] * inverse).astype(HALF)
            p_ref[head, pl.ds(at, CHUNK), :] = probs
            value = kv_ref[pl.ds(at, CHUNK), 256 + 128 * head : 384 + 128 * head]
            return acc + dot_tn(value, probs)

        out = lax.fori_loop(0, KEYS // CHUNK, value_step, jnp.zeros((DN, ROWS), WIDE))
        o_ref[:, 128 * head : 128 * head + 128] = out.T


def attend(queries, kv_all, rot_all, low, high):
    vmem = pl.BlockSpec(memory_space=pltpu.VMEM)
    return pl.pallas_call(
        attend_kernel,
        out_shape=(
            jax.ShapeDtypeStruct((H_DEV, KEYS, ROWS), HALF),
            jax.ShapeDtypeStruct((ROWS, H_DEV * DN), WIDE),
        ),
        in_specs=[vmem] * 5,
        out_specs=(vmem, vmem),
        scratch_shapes=[pltpu.VMEM((KEYS, ROWS), WIDE)],
        compiler_params=pltpu.CompilerParams(vmem_limit_bytes=40 * 1024 * 1024),
        cost_estimate=pl.CostEstimate(
            flops=2 * H_DEV * ROWS * KEYS * 384, bytes_accessed=12 << 20, transcendentals=2 << 20
        ),
    )(queries, kv_all, rot_all, low, high)


def attend_back_kernel(
    core_ref, q_ref, kv_ref, rot_ref, p_ref, dmid_ref, wot_ref, wkv_ref, o_ref,
    keep_ref, send_ref, dkv_ref, dq_ref, acc_ref, do_ref, delta_ref, qf_ref,
):
    step = pl.program_id(0)

    @pl.when(step == 0)
    def _():
        acc_ref[...] = jnp.zeros_like(acc_ref)
        d_heads = dot_nn(dmid_ref[...], wot_ref[...]).astype(HALF)
        do_ref[...] = d_heads
        product = d_heads.astype(WIDE) * o_ref[...]
        for head in range(H_DEV):
            delta_ref[8 * head : 8 * head + 8, :] = lax.dot_general(
                jnp.ones((8, 128), WIDE),
                product[:, 128 * head : 128 * head + 128],
                (((1,), (1,)), ((), ())),
                precision=lax.Precision.HIGHEST,
                preferred_element_type=WIDE,
            )
            qf_ref[head] = head_query(q_ref, head)

    rot = rot_ref[...]
    d_rot = jnp.zeros((CHUNK, 128), WIDE)
    for head in range(H_DEV):
        d_out = do_ref[:, 128 * head : 128 * head + 128]
        value = kv_ref[:, 256 + 128 * head : 384 + 128 * head]
        probs = p_ref[head]
        d_probs = dot_nt(value, d_out)
        d_scores = (
            probs.astype(WIDE) * (d_probs - delta_ref[8 * head : 8 * head + 1, :])
        ).astype(HALF)
        d_key = dot_nn(d_scores, qf_ref[head]) * SCALE
        dkv_ref[:, 128 * head : 128 * head + 128] = d_key[:, :128].astype(HALF)
        d_rot = d_rot + d_key[:, 128:]
        dkv_ref[:, 256 + 128 * head : 384 + 128 * head] = dot_nn(probs, d_out).astype(HALF)
        key = jnp.concatenate([kv_ref[:, 128 * head : 128 * head + 128], rot], axis=1)
        acc_ref[head] += dot_tn(key, d_scores)
    d_lat = dot_nt(dkv_ref[...], wkv_ref[...]).astype(HALF)
    d_rot = d_rot.astype(HALF)

    def write(target, core):
        for block in range(CHUNK // ROWS):
            for y in range(4):
                row = ROWS * block + OWN * (2 * y + core)
                target[y, block, :, :512] = d_lat[row : row + OWN]
                target[y, block, :, 512:] = d_rot[row : row + OWN]

    @pl.when(core_ref[0] == 0)
    def _():
        write(keep_ref, 0)
        write(send_ref, 1)

    @pl.when(core_ref[0] != 0)
    def _():
        write(keep_ref, 1)
        write(send_ref, 0)

    @pl.when(step == KEYS // CHUNK - 1)
    def _():
        lane = lax.broadcasted_iota(jnp.int32, (ROWS, 128), 1)
        d_q_rot = jnp.zeros((ROWS, 128), WIDE)
        for head in range(H_DEV):
            d_query = acc_ref[head].T * SCALE
            dq_ref[:, 128 * head : 128 * head + 128] = d_query[:, :128]
            d_q_rot = jnp.where((lane // 32) % 2 == head, d_query[:, 128:], d_q_rot)
        dq_ref[:, 256:384] = d_q_rot


def attend_back(ci, queries, kv_all, rot_all, probs, d_mid, wot, wkv, heads):
    def whole(*shape):
        return pl.BlockSpec(shape, lambda i, core: (0,) * len(shape))

    share = jax.ShapeDtypeStruct((4, 16, OWN, 640), HALF)
    share_spec = pl.BlockSpec((4, CHUNK // ROWS, OWN, 640), lambda i, core: (0, i, 0, 0))
    return pl.pallas_call(
        attend_back_kernel,
        out_shape=(
            share,
            share,
            jax.ShapeDtypeStruct((KEYS, 512), HALF),
            jax.ShapeDtypeStruct((ROWS, 384), WIDE),
        ),
        grid_spec=pltpu.PrefetchScalarGridSpec(
            num_scalar_prefetch=1,
            grid=(KEYS // CHUNK,),
            in_specs=[
                whole(ROWS, 384),
                pl.BlockSpec((CHUNK, 512), lambda i, core: (i, 0)),
                pl.BlockSpec((CHUNK, 128), lambda i, core: (i, 0)),
                pl.BlockSpec((H_DEV, CHUNK, ROWS), lambda i, core: (0, i, 0)),
                whole(ROWS, D),
                whole(D, 256),
                whole(KVL, 512),
                whole(ROWS, 256),
            ],
            out_specs=(
                share_spec,
                share_spec,
                pl.BlockSpec((CHUNK, 512), lambda i, core: (i, 0)),
                whole(ROWS, 384),
            ),
            scratch_shapes=[
                pltpu.VMEM((H_DEV, 256, ROWS), WIDE),
                pltpu.VMEM((ROWS, H_DEV * DV), HALF),
                pltpu.VMEM((8 * H_DEV, ROWS), WIDE),
                pltpu.VMEM((H_DEV, ROWS, 256), HALF),
            ],
        ),
        compiler_params=pltpu.CompilerParams(vmem_limit_bytes=32 * 1024 * 1024),
        cost_estimate=pl.CostEstimate(
            flops=2 * H_DEV * ROWS * KEYS * 768 + 2 * KEYS * 512 * 512,
            bytes_accessed=24 << 20,
            transcendentals=0,
        ),
    )(ci.reshape(1), queries, kv_all, rot_all, probs, d_mid, wot, wkv, heads)


def expert_kernel(at_ref, x_ref, xo_ref, g_ref, go_ref, *rest):
    pieces = rest[:12]
    keep_in, send_in, keep_out, send_out, x_out, dso_out, hid_out, dpre_out = rest[12:20]
    wg_ref, wu_ref, wd_ref, dots_ref, sems = rest[20:]
    copies = []
    for part, target in enumerate((wg_ref, wu_ref, wd_ref)):
        for k in range(4):
            copy = pltpu.make_async_copy(
                pieces[4 * part + k],
                target.at[pl.ds(FFS * k, FFS), :],
                sems.at[4 * part + k],
            )
            copy.start()
            copies.append(copy)
        target[FFH:, :] = jnp.zeros((FFP - FFH, D), HALF)
    first = at_ref[0] == 0
    half = D // 2
    own = x_ref[:, :half]
    other = xo_ref[:, :half]
    x_out[:, :half] = jnp.where(first, own, other)
    x_out[:, half:] = jnp.where(first, other, own)
    gate = x_ref[:, half : half + 1].astype(WIDE)
    own = (g_ref[...].astype(WIDE) * gate).astype(HALF)
    other = (go_ref[...].astype(WIDE) * gate).astype(HALF)
    dso_out[:, :half] = jnp.where(first, own, other)
    dso_out[:, half:] = jnp.where(first, other, own)
    for copy in copies:
        copy.wait()

    def hidden_step(i, carry):
        at = pl.multiple_of(i * 256, 256)
        x = x_out[...]
        pre_gate = dot_nt(x, wg_ref[pl.ds(at, 256), :])
        pre_up = dot_nt(x, wu_ref[pl.ds(at, 256), :])
        d_hidden = dot_nt(dso_out[...], wd_ref[pl.ds(at, 256), :])
        sig = 1.0 / (1.0 + jnp.exp(-pre_gate))
        act = pre_gate * sig
        hid_out[:, pl.ds(at, 256)] = (act * pre_up).astype(HALF)
        slope = sig * (1.0 + pre_gate * (1.0 - sig))
        dpre_out[:, pl.ds(at, 256)] = (d_hidden * pre_up * slope).astype(HALF)
        dpre_out[:, pl.ds(pl.multiple_of(at + FFP, 256), 256)] = (d_hidden * act).astype(HALF)
        return carry

    lax.fori_loop(0, FFP // 256, hidden_step, 0)

    dots_ref[...] = jnp.zeros_like(dots_ref)

    def output_step(i, carry):
        at = pl.multiple_of(i * 256, 256)
        to = pl.multiple_of((i % 4) * 256, 256)
        own_side = (i // 4) == at_ref[0]
        d_in = dot_nn(dpre_out[:, :FFP], wg_ref[:, pl.ds(at, 256)])
        d_in = d_in + dot_nn(dpre_out[:, FFP:], wu_ref[:, pl.ds(at, 256)])
        d_in = d_in.astype(HALF)
        out = dot_nn(hid_out[...], wd_ref[:, pl.ds(at, 256)])
        g = jnp.where(own_side, g_ref[:, pl.ds(to, 256)], go_ref[:, pl.ds(to, 256)])
        dots = out * g.astype(WIDE)
        dots_ref[...] += dots[:, :128] + dots[:, 128:]
        out = out.astype(HALF)

        @pl.when(own_side)
        def _():
            keep_in[:, pl.ds(to, 256)] = d_in
            keep_out[:, pl.ds(to, 256)] = out

        @pl.when(jnp.logical_not(own_side))
        def _():
            send_in[:, pl.ds(to, 256)] = d_in
            send_out[:, pl.ds(to, 256)] = out

        return carry

    lax.fori_loop(0, D // 256, output_step, 0)
    total = jnp.sum(dots_ref[...], axis=1, keepdims=True)
    keep_in[:, half:] = jnp.broadcast_to(total, (16 * SLOTS, 128)).astype(HALF)
    send_in[:, half:] = jnp.zeros((16 * SLOTS, 128), HALF)


def run_expert(ci, x_own, x_other, g_own, g_other, pieces):
    rows = 16 * SLOTS
    vmem = pl.BlockSpec(memory_space=pltpu.VMEM)
    return pl.pallas_call(
        expert_kernel,
        out_shape=(
            jax.ShapeDtypeStruct((rows, D // 2 + 128), HALF),
            jax.ShapeDtypeStruct((rows, D // 2 + 128), HALF),
            jax.ShapeDtypeStruct((rows, D // 2), HALF),
            jax.ShapeDtypeStruct((rows, D // 2), HALF),
            jax.ShapeDtypeStruct((rows, D), HALF),
            jax.ShapeDtypeStruct((rows, D), HALF),
            jax.ShapeDtypeStruct((rows, FFP), HALF),
            jax.ShapeDtypeStruct((rows, 2 * FFP), HALF),
        ),
        in_specs=[pl.BlockSpec(memory_space=pltpu.SMEM)]
        + [vmem] * 4
        + [pl.BlockSpec(memory_space=pl.ANY)] * 12,
        out_specs=(vmem,) * 8,
        scratch_shapes=[pltpu.VMEM((FFP, D), HALF)] * 3
        + [pltpu.VMEM((rows, 128), WIDE), pltpu.SemaphoreType.DMA((12,))],
        compiler_params=pltpu.CompilerParams(vmem_limit_bytes=52 * 1024 * 1024),
        cost_estimate=pl.CostEstimate(
            flops=12 * rows * D * FFP, bytes_accessed=28 << 20, transcendentals=rows * FFP
        ),
    )(ci.reshape(1), x_own, x_other, g_own, g_other, *pieces)


def place_kernel(at_ref, *refs):
    out_ref = refs[4]
    step = pl.program_id(0)
    for k in range(4):

        @pl.when(step == k)
        def _():
            out_ref[0] = refs[k][...].astype(WIDE)


def place_pieces(yi, pieces):
    return pl.pallas_call(
        place_kernel,
        out_shape=jax.ShapeDtypeStruct((4, FFS, D), WIDE),
        grid_spec=pltpu.PrefetchScalarGridSpec(
            num_scalar_prefetch=1,
            grid=(4,),
            in_specs=[pl.BlockSpec((FFS, D), lambda k, at: (0, 0))] * 4,
            out_specs=pl.BlockSpec((1, FFS, D), lambda k, at: ((at[0] + k) % 4, 0, 0)),
        ),
        compiler_params=pltpu.CompilerParams(vmem_limit_bytes=24 * 1024 * 1024),
        cost_estimate=pl.CostEstimate(flops=1, bytes_accessed=1, transcendentals=0),
    )(yi.reshape(1), *pieces)


def late_kernel(dq_ref, wq_ref, so_ref, gated_ref, out_ref, core_ref, late_ref):
    late_ref[:, :D] = dot_nt(dq_ref[...], wq_ref[...]).astype(HALF)
    routed = dot_tn(gated_ref[...], out_ref[...])
    half = D // 2
    first = (core_ref[0] == 0).astype(WIDE)
    late_ref[:, D : D + half] = (so_ref[:, :half] + routed * first).astype(HALF)
    late_ref[:, D + half :] = (so_ref[:, half:] + routed * (1.0 - first)).astype(HALF)


def late_products(ci, d_queries, wq, shared_out, gated, out_back):
    vmem = pl.BlockSpec(memory_space=pltpu.VMEM)
    return pl.pallas_call(
        late_kernel,
        out_shape=jax.ShapeDtypeStruct((ROWS, 2 * D), HALF),
        in_specs=[vmem] * 5 + [pl.BlockSpec(memory_space=pltpu.SMEM)],
        out_specs=vmem,
        compiler_params=pltpu.CompilerParams(vmem_limit_bytes=32 * 1024 * 1024),
        cost_estimate=pl.CostEstimate(flops=1, bytes_accessed=1, transcendentals=0),
    )(d_queries, wq, shared_out, gated, out_back, ci.reshape(1))


def rest_kernel(
    h_two_ref, dsp_ref, g_ref, sh_ref, h_one_ref, dq_ref, dmid_ref, heads_ref, c_ref, dkv_ref,
    out_ref, kv_ref,
):
    def step(i, carry):
        at = pl.multiple_of(i * 256, 256)
        rows = pl.ds(at, 256)
        out_ref[rows, 0:768] = dot_tn(h_two_ref[:, rows], dsp_ref[...]).astype(HALF)
        out_ref[rows, 768:1152] = dot_tn(g_ref[:, rows], sh_ref[...]).astype(HALF)
        out_ref[rows, 1152:1536] = dot_tn(h_one_ref[:, rows], dq_ref[...]).astype(HALF)
        out_ref[rows, 1536:1792] = dot_tn(dmid_ref[:, rows], heads_ref[...]).astype(HALF)
        return carry

    lax.fori_loop(0, D // 256, step, 0)
    kv_ref[...] = jnp.zeros_like(kv_ref)

    def kv_step(i, carry):
        rows = pl.ds(pl.multiple_of(i * CHUNK, CHUNK), CHUNK)
        kv_ref[...] += dot_tn(c_ref[rows, 0:KVL], dkv_ref[rows, :])
        return carry

    lax.fori_loop(0, KEYS // CHUNK, kv_step, 0)
    for e in range(16):
        for block in range(4):
            row = 128 * e + 32 * block
            out_ref[row : row + 32, 1792:1920] = kv_ref[
                32 * e : 32 * e + 32, 128 * block : 128 * block + 128
            ].astype(HALF)


def rest_products(*operands):
    vmem = pl.BlockSpec(memory_space=pltpu.VMEM)
    return pl.pallas_call(
        rest_kernel,
        out_shape=jax.ShapeDtypeStruct((D, 1920), HALF),
        in_specs=[vmem] * 10,
        out_specs=vmem,
        scratch_shapes=[pltpu.VMEM((KVL, 512), WIDE)],
        compiler_params=pltpu.CompilerParams(vmem_limit_bytes=48 * 1024 * 1024),
        cost_estimate=pl.CostEstimate(flops=1, bytes_accessed=1, transcendentals=0),
    )(*operands)


def pack_query_columns(w):
    return jnp.concatenate(
        [w[:, 0:128], w[:, 192:320], w[:, 128:160], w[:, 320:352], w[:, 160:192], w[:, 352:384]],
        axis=1,
    )


def unpack_query_columns(w):
    return jnp.concatenate(
        [w[:, 0:128], w[:, 256:288], w[:, 320:352], w[:, 128:256], w[:, 288:320], w[:, 352:384]],
        axis=1,
    )


def pad_cols(w, width):
    return jnp.pad(w, ((0, 0), (0, width - w.shape[1])))


def silu_parts(gate):
    sig = jax.nn.sigmoid(gate)
    return gate * sig, sig * (1.0 + gate * (1.0 - sig))


def body(
    inputs,
    gain_attn,
    w_q,
    w_dkv,
    gain_latent,
    w_uk,
    w_uv,
    w_o,
    gain_ffn,
    w_router,
    w_sg,
    w_su,
    w_sd,
    w_eg,
    w_eu,
    w_ed,
    routes,
    seq_lengths,
    piece_starts,
    out_grad,
):
    zi, xi, yi, ci = (lax.axis_index(name) for name in ("z", "x", "y", "c"))
    ei = zi * 4 + xi
    ti = yi * 2 + ci

    def half_cols(value):
        return lax.dynamic_slice_in_dim(value, ci * (D // 2), D // 2, value.ndim - 1)

    def place_half(value):
        zero = jnp.zeros_like(value)
        return jnp.concatenate(
            [jnp.where(ci == 0, value, zero), jnp.where(ci == 0, zero, value)], axis=1
        )

    def swap_halves(v):
        return jnp.concatenate([v[:, 64:], v[:, :64]], axis=1)

    def own_rows(value):
        return lax.dynamic_slice_in_dim(value, ti * OWN, OWN, 0)

    def sent_pieces(weight):
        return [
            lax.dynamic_index_in_dim(weight, (yi + by) % 4, 0, keepdims=False).astype(HALF)
            for by in range(4)
        ]

    def moved_pieces(sent):
        return [sent[0]] + [shift_y(sent[by], by) for by in (1, 2, 3)]

    def own_pieces(grad):
        return [grad[FFS * by : FFS * (by + 1)] for by in range(4)]

    gain_cols = jnp.stack([gain_attn, gain_ffn, jnp.pad(gain_latent, (0, 96))], axis=1)
    w_router_perm = w_router.reshape(128, 16, 4).transpose(0, 2, 1).reshape(128, EXPERTS)
    first_pack = jnp.concatenate(
        [
            w_dkv,
            w_router_perm,
            jnp.concatenate([w_uk, w_uv], axis=1).reshape(128, 128),
            pad_cols(gain_cols, 128),
            pack_query_columns(w_q),
            w_o.T,
        ],
        axis=1,
    ).astype(HALF)
    first_all = lax.all_gather(first_pack, EX, axis=0, tiled=True)
    gate_sent, up_sent, down_sent = sent_pieces(w_eg), sent_pieces(w_eu), sent_pieces(w_ed)
    gate_sent, up_sent, inputs_b, out_grad_b = lax.optimization_barrier(
        (gate_sent, up_sent, inputs, out_grad)
    )
    gate_pieces = moved_pieces(gate_sent)
    in_rows = gather_rows(inputs_b, yi, ci)
    g_rows = gather_rows(out_grad_b, yi, ci)
    second_pack = jnp.concatenate(
        [pad_cols(w_sg, SHP), pad_cols(w_su, SHP), pad_cols(w_sd.T, SHP)], axis=1
    ).astype(HALF)

    row_ids = ei * ROWS + jnp.arange(ROWS, dtype=jnp.int32)
    position, low, high = spans(row_ids, seq_lengths, piece_starts)
    inv_freq = 10000.0 ** (-(2.0 * jnp.arange(DR // 2, dtype=WIDE)) / DR)
    angles = position.astype(WIDE)[:, None] * inv_freq[None, :]
    cosine, sine = jnp.cos(angles), jnp.sin(angles)
    cos4 = jnp.concatenate([cosine] * 4, axis=1)
    sin4 = jnp.concatenate([-sine, -sine, sine, sine], axis=1)

    routes_t = routes.T
    expert_ids = 4 * lax.broadcasted_iota(jnp.int32, (16, 1, ROWS), 0) + yi
    named = jnp.max((routes_t[None] == expert_ids).astype(WIDE), axis=1)
    earlier = (
        lax.broadcasted_iota(jnp.int32, (ROWS, ROWS), 0)
        < lax.broadcasted_iota(jnp.int32, (ROWS, ROWS), 1)
    ).astype(HALF)
    rank = dot_nn(named.astype(HALF), earlier)
    slot_ids = lax.broadcasted_iota(jnp.int32, (16, SLOTS, ROWS), 1).astype(WIDE)
    picked = (named[:, None, :] > 0.5) & (rank[:, None, :] == slot_ids)
    select = picked.astype(HALF).reshape(16 * SLOTS, ROWS)

    in_wide = in_rows.astype(WIDE)
    normed_in = in_wide * inv_rms(in_wide)
    first_all, gate_pieces, up_sent, down_sent, second_pack = lax.optimization_barrier(
        (first_all, gate_pieces, up_sent, down_sent, second_pack)
    )
    normed_in, cos4, sin4, select = lax.optimization_barrier((normed_in, cos4, sin4, select))

    blk_b = first_all[:, 0:640]
    wkv_b = first_all[:, 640:768]
    pick = jnp.eye(8, 128, dtype=HALF)
    gains = dot_nt(pick, first_all[:, 768:896])
    wq_b = first_all[:, 896:1280]
    wot_b = first_all[:, 1280:1536]
    gain_one = gains[0]
    gain_two = gains[1]
    gain_lat = gains[2].reshape(16, 128)[:, :32].reshape(KVL)
    h_one = (normed_in * gain_one).astype(HALF)
    latent_all = dot_nn(h_one, blk_b)
    lat_part = latent_all[:, :KVL]
    scale_lat = inv_rms(lat_part)
    normed_lat = lat_part * scale_lat
    c_norm = (normed_lat * gain_lat).astype(HALF)
    rope_a, rope_b = latent_all[:, 512:544], latent_all[:, 544:576]
    rope = jnp.concatenate([rope_a, rope_a, rope_b, rope_b], axis=1)
    k_rot = rope * cos4 + swap_halves(rope) * sin4
    c_local = jnp.concatenate([c_norm, k_rot.astype(HALF)], axis=1)
    g_half = half_cols(g_rows)
    g_sent = dot_nn(select, g_half).astype(HALF).reshape(16, SLOTS, D // 2)
    c_local, up_sent, down_sent, g_sent, wq_b, wkv_b = lax.optimization_barrier(
        (c_local, up_sent, down_sent, g_sent, wq_b, wkv_b)
    )
    g_recv = spread(g_sent, EX).reshape(16 * SLOTS, D // 2)
    c_all = lax.all_gather(c_local, EX, axis=0, tiled=True)
    up_pieces = moved_pieces(up_sent)
    down_first = [down_sent[0], shift_y(down_sent[1], 1), None, shift_y(down_sent[3], 3)]
    wkv_b = wkv_b.reshape(KVL, 512)
    q_raw = dot_nn(h_one, wq_b)
    q_rot = q_raw[:, 256:]
    q_rot = q_rot * cos4 + swap_halves(q_rot) * sin4
    queries = jnp.concatenate([q_raw[:, :256], q_rot], axis=1).astype(HALF)
    c_all, queries, wot_b, wkv_b, up_pieces, down_first, g_recv, second_pack, down_sent = (
        lax.optimization_barrier(
            (c_all, queries, wot_b, wkv_b, up_pieces, down_first, g_recv, second_pack, down_sent)
        )
    )

    second_all = lax.all_gather(second_pack, EX, axis=0, tiled=True)
    kv_all = dot_nn(c_all[:, :KVL], wkv_b).astype(HALF)
    rot_all = c_all[:, KVL:]
    probs, heads_wide = attend(queries, kv_all, rot_all, low[None, :], high[None, :])
    attn_heads = heads_wide.astype(HALF)
    attn_own = sum_rows(dot_nt(attn_heads, wot_b).astype(HALF), yi, ci)

    in_own = inputs.astype(WIDE)
    mid_own = in_own + attn_own
    scale_two = inv_rms(mid_own)
    normed_two = mid_own * scale_two
    h_two_own = (normed_two * gain_two).astype(HALF)
    h_two = gather_rows(h_two_own, yi, ci)

    rope_router_b = blk_b[:, 512:640]
    logits_t = lax.dot_general(
        rope_router_b, h_two, (((0,), (1,)), ((), ())), preferred_element_type=WIDE
    )[64:]
    probs_t = jax.nn.softmax(logits_t, axis=0)
    gate_t = lax.dynamic_slice_in_dim(probs_t, yi * 16, 16, 0).astype(HALF).astype(WIDE)
    gated = jnp.where(picked, gate_t[:, None, :], 0.0)
    slot_gate = jnp.sum(gated, axis=2)
    gated = gated.astype(HALF).reshape(16 * SLOTS, ROWS)
    x_sent = dot_nn(select, half_cols(h_two)).astype(HALF).reshape(16, SLOTS, D // 2)
    slot_gate = jnp.broadcast_to(slot_gate[:, :, None], (16, SLOTS, 128)).astype(HALF)
    x_sent = jnp.concatenate([x_sent, slot_gate], axis=2)
    x_sent, g_own, down_sent, h_two = lax.optimization_barrier((x_sent, g_recv, down_sent, h_two))
    x_own = spread(x_sent, EX).reshape(16 * SLOTS, D // 2 + 128)
    g_other = swap_core(g_own)
    down_pieces = [down_first[0], down_first[1], shift_y(down_sent[2], 2), down_first[3]]

    wgu_b = second_all[:, : 2 * SHP]
    wsdt_b = second_all[:, 2 * SHP :]
    shared_pre = dot_nn(h_two, wgu_b)
    shared_gate, shared_up = shared_pre[:, :SHP], shared_pre[:, SHP:]
    shared_silu, shared_slope = silu_parts(shared_gate)
    shared_hidden = (shared_silu * shared_up).astype(HALF)
    shared_out = dot_nt(shared_hidden, wsdt_b)
    d_shared_hidden = dot_nn(g_rows, wsdt_b)
    d_shared_pre = jnp.concatenate(
        [d_shared_hidden * shared_up * shared_slope, d_shared_hidden * shared_silu], axis=1
    ).astype(HALF)
    d_shared_in = dot_nt(d_shared_pre, wgu_b)
    x_own, g_other, down_pieces, shared_out, d_shared_in, d_shared_pre, shared_hidden = (
        lax.optimization_barrier(
            (x_own, g_other, down_pieces, shared_out, d_shared_in, d_shared_pre, shared_hidden)
        )
    )

    x_other = swap_core(x_own)
    keep_in, send_in, keep_out, send_out, x_slots, d_slot_out, expert_hidden, d_expert_pre = (
        run_expert(
            ci, x_own, x_other, g_own, g_other, gate_pieces + up_pieces + down_pieces
        )
    )

    def pair(keep, send):
        return (keep.astype(WIDE) + swap_core(send).astype(WIDE)).astype(HALF)

    in_sent = pair(keep_in, send_in)
    gate_parts = own_pieces(dot_tn(d_expert_pre[:, :FFP], x_slots).astype(HALF))
    in_sent, gate_parts, keep_out, send_out, d_slot_out, expert_hidden, d_expert_pre = (
        lax.optimization_barrier(
            (in_sent, gate_parts, keep_out, send_out, d_slot_out, expert_hidden, d_expert_pre)
        )
    )
    in_recv = spread(in_sent.reshape(16, SLOTS, D // 2 + 128), EX)
    gate_back = [gate_parts[0], shift_y(gate_parts[1], -1), None, shift_y(gate_parts[3], -3)]
    out_sent = pair(keep_out, send_out)
    up_parts = own_pieces(dot_tn(d_expert_pre[:, FFP:], x_slots).astype(HALF))
    down_parts = own_pieces(dot_tn(expert_hidden, d_slot_out).astype(HALF))
    in_recv, out_sent, gate_parts, gate_back, up_parts, down_parts = lax.optimization_barrier(
        (in_recv, out_sent, gate_parts, gate_back, up_parts, down_parts)
    )

    in_back = in_recv[:, :, : D // 2].reshape(16 * SLOTS, D // 2)
    slot_dots = in_recv[:, :, D // 2 : D // 2 + 1].astype(WIDE)
    d_route_t = jnp.sum(jnp.where(picked, slot_dots, 0.0), axis=1).astype(HALF)
    lane_at = (
        lax.broadcasted_iota(jnp.int32, (16, 128), 0) + yi * 16
        == lax.broadcasted_iota(jnp.int32, (16, 128), 1)
    ).astype(HALF)
    d_route_part = dot_tn(d_route_t, lane_at)
    d_h_part = d_shared_in + place_half(dot_tn(select, in_back))
    back_part = jnp.concatenate([d_h_part, d_route_part], axis=1).astype(HALF)
    back_own = sum_rows(back_part, yi, ci)

    logits_own = dot_nn(h_two_own, rope_router_b)[:, 64:]
    probs_own = jax.nn.softmax(logits_own, axis=-1)
    d_route = back_own[:, D : D + EXPERTS]
    d_logits = (
        probs_own * (d_route - jnp.sum(probs_own * d_route, axis=-1, keepdims=True))
    ).astype(HALF)
    d_logits_pad = jnp.pad(d_logits, ((0, 0), (64, 0)))
    d_h_two = back_own[:, :D] + dot_nt(d_logits_pad, rope_router_b)
    d_mid_norm, gain_two_part = norm_back(d_h_two, normed_two, scale_two, gain_two)
    d_mid_own = d_mid_norm + out_grad.astype(WIDE)
    d_attn_b = gather_rows(d_mid_own.astype(HALF), yi, ci)
    d_attn_b, up_parts = lax.optimization_barrier((d_attn_b, up_parts))

    up_back = [up_parts[0], shift_y(up_parts[1], -1), None, shift_y(up_parts[3], -3)]
    lat_keep, lat_send, d_kv, d_q = attend_back(
        ci, queries, kv_all, rot_all, probs, d_attn_b, wot_b, wkv_b, heads_wide
    )
    lat_keep, lat_send, d_kv, d_q, up_parts, up_back = lax.optimization_barrier(
        (lat_keep, lat_send, d_kv, d_q, up_parts, up_back)
    )
    lat_pair = pair(lat_keep, lat_send)
    lat_pair, d_kv, d_q, d_attn_b, d_shared_pre, shared_hidden, out_sent = lax.optimization_barrier(
        (lat_pair, d_kv, d_q, d_attn_b, d_shared_pre, shared_hidden, out_sent)
    )
    out_back = spread(out_sent.reshape(16, SLOTS, D // 2), EX).reshape(16 * SLOTS, D // 2)
    lat_total = lax.dynamic_index_in_dim(lat_pair, yi, 0, keepdims=False).astype(WIDE)
    lat_pieces = [
        shift_y(lax.dynamic_index_in_dim(lat_pair, (yi + by) % 4, 0, keepdims=False), by)
        for by in (1, 2, 3)
    ]

    d_q_rot = d_q[:, 256:]
    d_q_rot = d_q_rot * cos4 - swap_halves(d_q_rot) * sin4
    d_queries = jnp.concatenate([d_q[:, :256], d_q_rot], axis=1).astype(HALF)
    rest_grads = rest_products(
        h_two, d_shared_pre, g_rows, shared_hidden, h_one, d_queries, d_attn_b, attn_heads, c_all, d_kv
    )
    for piece in lat_pieces:
        lat_total = lat_total + piece.astype(WIDE)
    lat_total, d_queries, out_back, down_parts, up_parts, rest_grads = lax.optimization_barrier(
        (lat_total.astype(HALF), d_queries, out_back, down_parts, up_parts, rest_grads)
    )
    rest_sum = lax.psum_scatter(rest_grads, EX, scatter_dimension=0, tiled=True)
    lat_parts = spread(lat_total, EX)
    down_back = [down_parts[0], shift_y(down_parts[1], -1), None, shift_y(down_parts[3], -3)]
    late_parts = late_products(ci, d_queries, wq_b, shared_out, gated, out_back)
    late_own = sum_rows(late_parts, yi, ci)
    lat_parts, down_parts, down_back, late_own = lax.optimization_barrier(
        (lat_parts, down_parts, down_back, late_own)
    )
    d_one_own = late_own[:, :D]
    layer_out = (mid_own + late_own[:, D:]).astype(HALF)
    d_lat_own = jnp.sum(lat_parts.astype(WIDE), axis=0)

    cos_own, sin_own = own_rows(cos4), own_rows(sin4)
    d_rope = d_lat_own[:, 512:]
    d_rope = d_rope * cos_own - swap_halves(d_rope) * sin_own
    d_rope = jnp.concatenate(
        [d_rope[:, 0:32] + d_rope[:, 32:64], d_rope[:, 64:96] + d_rope[:, 96:128]], axis=1
    )
    d_lat, grad_gain_lat = norm_back(
        d_lat_own[:, :512], own_rows(normed_lat), own_rows(scale_lat), gain_lat
    )
    d_latent_pad = jnp.pad(jnp.concatenate([d_lat, d_rope], axis=1).astype(HALF), ((0, 0), (0, 64)))
    d_both = jnp.concatenate([d_latent_pad, d_logits_pad], axis=1)
    d_both = spread(jnp.broadcast_to(d_both[None], (8, OWN, 768)), ("y", "c")).reshape(ROWS, 768)
    d_both, up_parts, down_parts, down_back, gate_parts = lax.optimization_barrier(
        (d_both, up_parts, down_parts, down_back, gate_parts)
    )
    d_latent = d_both[:, :576]
    d_logits_all = d_both[:, 704:768]
    down_back[2] = shift_y(down_parts[2], -2)
    gate_back[2] = shift_y(gate_parts[2], -2)
    up_back[2] = shift_y(up_parts[2], -2)
    d_h_one = d_one_own + dot_nt(d_latent_pad, blk_b)
    scale_one = inv_rms(in_own)
    normed_one = in_own * scale_one
    d_in_norm, gain_one_part = norm_back(d_h_one, normed_one, scale_one, gain_one)
    grad_inputs = (d_mid_own + d_in_norm).astype(HALF)

    grad_router = dot_tn(h_two, lax.dynamic_slice_in_dim(d_logits_all, ti * 8, 8, 1))
    grad_dkv = dot_tn(h_one, lax.dynamic_slice_in_dim(d_latent, ti * 72, 72, 1))
    gain_lat_wide = jnp.pad(grad_gain_lat.reshape(16, 32), ((0, 0), (0, 96))).reshape(D)
    gain_rows = jnp.stack([gain_one_part, gain_two_part, gain_lat_wide], axis=0).astype(HALF)
    gain_at = (
        lax.broadcasted_iota(jnp.int32, (3, 48), 0) == lax.broadcasted_iota(jnp.int32, (3, 48), 1)
    ).astype(HALF)
    last_part = jnp.concatenate([grad_dkv, grad_router, dot_tn(gain_rows, gain_at)], axis=1)
    last_parts = spread(last_part.astype(HALF).reshape(16, 128, 128), EX)
    last_parts, down_back = lax.optimization_barrier((last_parts, down_back))
    grad_ed = place_pieces(yi, down_back)
    last_sum = jnp.sum(last_parts.astype(WIDE), axis=0)
    last_all = spread(
        jnp.broadcast_to(last_sum.astype(HALF)[None], (8, 128, 128)), ("y", "c")
    )
    last_all, gate_back, up_back = lax.optimization_barrier((last_all, gate_back, up_back))
    grad_eg = place_pieces(yi, gate_back)
    grad_eu = place_pieces(yi, up_back)
    rest_sum = rest_sum.astype(WIDE)
    sum_kv = rest_sum[:, 1792:].reshape(4, 32, 128).transpose(1, 0, 2).reshape(32, 512)
    sum_dkv = last_all[:, :, :72].transpose(1, 0, 2).reshape(128, 576).astype(WIDE)
    sum_router = last_all[:, :, 72:80].transpose(1, 0, 2).reshape(128, 4, 16)
    sum_router = sum_router.transpose(0, 2, 1).reshape(128, EXPERTS).astype(WIDE)
    gain_sums = jnp.sum(last_all[:, :, 80:83].astype(WIDE), axis=0)

    return (
        layer_out,
        grad_inputs,
        gain_sums[:, 0],
        unpack_query_columns(rest_sum[:, 1152:1536]),
        sum_dkv,
        gain_sums[:32, 2],
        sum_kv[:, :256],
        sum_kv[:, 256:],
        rest_sum[:, 1536:1792].T,
        gain_sums[:, 1],
        sum_router,
        rest_sum[:, :352],
        rest_sum[:, SHP : SHP + 352],
        rest_sum[:, 2 * SHP : 2 * SHP + 352].T,
        grad_eg,
        grad_eu,
        grad_ed,
    )


def solution(mesh):
    grid = Mesh(mesh.devices.reshape(4, 4, 4, 2), ("z", "x", "y", "c"))
    ten = ("y", "c")
    rows = P(("z", "x", "y", "c"), None)
    wide = P(EX, ten)
    tall = P(ten, EX)
    expert = P(EX, ten, None)
    return jax.shard_map(
        body,
        mesh=grid,
        in_specs=(
            rows,
            P(EX),
            wide,
            P(EX, None),
            P(EX),
            wide,
            wide,
            tall,
            P(EX),
            P(EX, None),
            wide,
            wide,
            tall,
            expert,
            expert,
            expert,
            P(EX, None),
            P(),
            P(),
            rows,
        ),
        out_specs=(
            rows,
            rows,
            P(EX),
            wide,
            P(EX, None),
            P(EX),
            wide,
            wide,
            tall,
            P(EX),
            P(EX, None),
            wide,
            wide,
            tall,
            expert,
            expert,
            expert,
        ),
        check_vma=False,
    )
```

```python
import jax
import jax.numpy as jnp
from jax import lax
from jax.experimental import pallas as pl
from jax.experimental.layout import Layout, with_layout_constraint
from jax.experimental.pallas import tpu as pltpu
from jax.sharding import Mesh, PartitionSpec as P

D = 2048
H_DEV = 2
DN = 128
DV = 128
DR = 64
KVL = 512
PIECE = 256
EXPERTS = 64
ROWS = 256
OWN = 32
SLOTS = 40
FFH = 704
FFS = 176
FFP = 768
SHP = 384
KEYS = 4096
CHUNK = 512
EPS = 1e-06
NEG = -1e30
SCALE = (DN + DR) ** (-0.5)
EX = ("z", "x")
HALF = jnp.bfloat16
WIDE = jnp.float32


def dot_nn(left, right):
    return jnp.dot(left, right, preferred_element_type=WIDE)


def dot_nt(left, right):
    return lax.dot_general(left, right, (((1,), (1,)), ((), ())), preferred_element_type=WIDE)


def dot_tn(left, right):
    return lax.dot_general(left, right, (((0,), (0,)), ((), ())), preferred_element_type=WIDE)


def inv_rms(values):
    return lax.rsqrt(jnp.mean(values * values, axis=-1, keepdims=True) + EPS)


def norm_back(grad, normed, row_scale, gain):
    scaled = grad * gain
    inner_mean = jnp.mean(scaled * normed, axis=-1, keepdims=True)
    return (row_scale * (scaled - normed * inner_mean), jnp.sum(grad * normed, axis=0))


def row_major(value):
    return with_layout_constraint(value, Layout(major_to_minor=(0, 1)))


def swap_core(value):
    return lax.ppermute(value, "c", [(0, 1), (1, 0)])


def shift_y(value, by):
    return lax.ppermute(value, "y", [(i, (i + by) % 4) for i in range(4)])


def spread(value, axes):
    return lax.all_to_all(value, axes, split_axis=0, concat_axis=0, tiled=True)


def gather_rows(value, yi, ci):
    n = value.shape[1]
    block = jnp.zeros((4, OWN, n), value.dtype)
    block = lax.dynamic_update_slice(block, value[None], (yi, 0, 0))
    for by in (1, 2, 3):
        block = lax.dynamic_update_slice(block, shift_y(value, by)[None], ((yi - by) % 4, 0, 0))
    other = swap_core(block)
    first = jnp.where(ci == 0, block, other)
    second = jnp.where(ci == 0, other, block)
    return jnp.stack([first, second], axis=1).reshape(ROWS, n)


def pair_pieces(keep, send, yi):
    other = swap_core(send)
    pieces = []
    for by in range(4):
        at = (yi + by) % 4
        mine = lax.dynamic_index_in_dim(keep, at, 0, keepdims=False).astype(WIDE)
        theirs = lax.dynamic_index_in_dim(other, at, 0, keepdims=False).astype(WIDE)
        pieces.append((mine + theirs).astype(HALF))
    return pieces


def add_pieces(pieces):
    total = pieces[0].astype(WIDE)
    for by in (1, 2, 3):
        total = total + shift_y(pieces[by], by).astype(WIDE)
    return total


def sum_rows(value, yi, ci):
    parts = value.reshape(4, 2, OWN, value.shape[1])
    mine = lax.dynamic_index_in_dim(parts, ci, 1, keepdims=False)
    theirs = lax.dynamic_index_in_dim(parts, 1 - ci, 1, keepdims=False)
    return add_pieces(pair_pieces(mine, theirs, yi))


def sum_experts(value):
    rows, width = value.shape
    parts = spread(value.reshape(16, rows // 16, width), EX)
    return jnp.sum(parts.astype(WIDE), axis=0)


def spans(row_ids, seq_lengths, piece_starts):
    ends = jnp.cumsum(seq_lengths)
    starts = ends - seq_lengths
    member = (row_ids[:, None] >= starts[None, :]) & (row_ids[:, None] < ends[None, :])
    member = member.astype(jnp.int32)
    low = jnp.sum(member * starts[None, :], axis=1)
    end = jnp.sum(member * ends[None, :], axis=1)
    inside = (row_ids[:, None] >= piece_starts[None, :]) & (
        row_ids[:, None] < piece_starts[None, :] + PIECE
    )
    piece_last = jnp.max(jnp.where(inside, piece_starts[None, :] + (PIECE - 1), -1), axis=1)
    high = jnp.where(piece_last >= 0, jnp.minimum(piece_last, end - 1), row_ids)
    return row_ids - low, low, high


def head_query(q_ref, head):
    lane = lax.broadcasted_iota(jnp.int32, (ROWS, 128), 1)
    rot = q_ref[:, 256:384]
    rot = jnp.where((lane // 32) % 2 == head, rot, jnp.zeros_like(rot))
    return jnp.concatenate([q_ref[:, 128 * head : 128 * head + 128], rot], axis=1)


def attend_kernel(q_ref, kv_ref, rot_ref, low_ref, high_ref, p_ref, o_ref, s_ref):
    low = low_ref[...]
    high = high_ref[...]
    for head in range(H_DEV):
        query = head_query(q_ref, head)

        def scores_step(i, top):
            at = pl.multiple_of(i * CHUNK, CHUNK)
            key = jnp.concatenate(
                [
                    kv_ref[pl.ds(at, CHUNK), 128 * head : 128 * head + 128],
                    rot_ref[pl.ds(at, CHUNK), :],
                ],
                axis=1,
            )
            scores = dot_nt(key, query) * SCALE
            col = lax.broadcasted_iota(jnp.int32, (CHUNK, ROWS), 0) + at
            scores = jnp.where((col >= low) & (col <= high), scores, NEG)
            s_ref[pl.ds(at, CHUNK), :] = scores
            return jnp.maximum(top, jnp.max(scores.reshape(CHUNK // 8, 8, ROWS), axis=0))

        top = lax.fori_loop(
            0, KEYS // CHUNK, scores_step, jnp.full((8, ROWS), NEG, WIDE)
        )
        top = jnp.max(top, axis=0, keepdims=True)

        def exp_step(i, total):
            at = pl.multiple_of(i * CHUNK, CHUNK)
            weights = jnp.exp(s_ref[pl.ds(at, CHUNK), :] - top)
            s_ref[pl.ds(at, CHUNK), :] = weights
            return total + jnp.sum(weights.reshape(CHUNK // 8, 8, ROWS), axis=0)

        total = lax.fori_loop(0, KEYS // CHUNK, exp_step, jnp.zeros((8, ROWS), WIDE))
        inverse = 1.0 / jnp.sum(total, axis=0, keepdims=True)

        def value_step(i, acc):
            at = pl.multiple_of(i * CHUNK, CHUNK)
            probs = (s_ref[pl.ds(at, CHUNK), :] * inverse).astype(HALF)
            p_ref[head, pl.ds(at, CHUNK), :] = probs
            value = kv_ref[pl.ds(at, CHUNK), 256 + 128 * head : 384 + 128 * head]
            return acc + dot_tn(value, probs)

        out = lax.fori_loop(0, KEYS // CHUNK, value_step, jnp.zeros((DN, ROWS), WIDE))
        o_ref[:, 128 * head : 128 * head + 128] = out.T


def attend(queries, kv_all, rot_all, low, high):
    vmem = pl.BlockSpec(memory_space=pltpu.VMEM)
    return pl.pallas_call(
        attend_kernel,
        out_shape=(
            jax.ShapeDtypeStruct((H_DEV, KEYS, ROWS), HALF),
            jax.ShapeDtypeStruct((ROWS, H_DEV * DN), WIDE),
        ),
        in_specs=[vmem] * 5,
        out_specs=(vmem, vmem),
        scratch_shapes=[pltpu.VMEM((KEYS, ROWS), WIDE)],
        compiler_params=pltpu.CompilerParams(vmem_limit_bytes=40 * 1024 * 1024),
        cost_estimate=pl.CostEstimate(
            flops=2 * H_DEV * ROWS * KEYS * 384, bytes_accessed=12 << 20, transcendentals=2 << 20
        ),
    )(queries, kv_all, rot_all, low, high)


def attend_back_kernel(
    core_ref, q_ref, kv_ref, rot_ref, p_ref, dmid_ref, wot_ref, wkv_ref, o_ref,
    keep_ref, send_ref, dkv_ref, dq_ref, acc_ref, do_ref, delta_ref, qf_ref,
):
    step = pl.program_id(0)

    @pl.when(step == 0)
    def _():
        acc_ref[...] = jnp.zeros_like(acc_ref)
        d_heads = dot_nn(dmid_ref[...], wot_ref[...]).astype(HALF)
        do_ref[...] = d_heads
        product = d_heads.astype(WIDE) * o_ref[...]
        for head in range(H_DEV):
            delta_ref[8 * head : 8 * head + 8, :] = lax.dot_general(
                jnp.ones((8, 128), WIDE),
                product[:, 128 * head : 128 * head + 128],
                (((1,), (1,)), ((), ())),
                precision=lax.Precision.HIGHEST,
                preferred_element_type=WIDE,
            )
            qf_ref[head] = head_query(q_ref, head)

    rot = rot_ref[...]
    d_rot = jnp.zeros((CHUNK, 128), WIDE)
    for head in range(H_DEV):
        d_out = do_ref[:, 128 * head : 128 * head + 128]
        value = kv_ref[:, 256 + 128 * head : 384 + 128 * head]
        probs = p_ref[head]
        d_probs = dot_nt(value, d_out)
        d_scores = (
            probs.astype(WIDE) * (d_probs - delta_ref[8 * head : 8 * head + 1, :])
        ).astype(HALF)
        d_key = dot_nn(d_scores, qf_ref[head]) * SCALE
        dkv_ref[:, 128 * head : 128 * head + 128] = d_key[:, :128].astype(HALF)
        d_rot = d_rot + d_key[:, 128:]
        dkv_ref[:, 256 + 128 * head : 384 + 128 * head] = dot_nn(probs, d_out).astype(HALF)
        key = jnp.concatenate([kv_ref[:, 128 * head : 128 * head + 128], rot], axis=1)
        acc_ref[head] += dot_tn(key, d_scores)
    d_lat = dot_nt(dkv_ref[...], wkv_ref[...]).astype(HALF)
    d_rot = d_rot.astype(HALF)

    def write(target, core):
        for block in range(CHUNK // ROWS):
            for y in range(4):
                row = ROWS * block + OWN * (2 * y + core)
                target[y, block, :, :512] = d_lat[row : row + OWN]
                target[y, block, :, 512:] = d_rot[row : row + OWN]

    @pl.when(core_ref[0] == 0)
    def _():
        write(keep_ref, 0)
        write(send_ref, 1)

    @pl.when(core_ref[0] != 0)
    def _():
        write(keep_ref, 1)
        write(send_ref, 0)

    @pl.when(step == KEYS // CHUNK - 1)
    def _():
        lane = lax.broadcasted_iota(jnp.int32, (ROWS, 128), 1)
        d_q_rot = jnp.zeros((ROWS, 128), WIDE)
        for head in range(H_DEV):
            d_query = acc_ref[head].T * SCALE
            dq_ref[:, 128 * head : 128 * head + 128] = d_query[:, :128]
            d_q_rot = jnp.where((lane // 32) % 2 == head, d_query[:, 128:], d_q_rot)
        dq_ref[:, 256:384] = d_q_rot


def attend_back(ci, queries, kv_all, rot_all, probs, d_mid, wot, wkv, heads):
    def whole(*shape):
        return pl.BlockSpec(shape, lambda i, core: (0,) * len(shape))

    share = jax.ShapeDtypeStruct((4, 16, OWN, 640), HALF)
    share_spec = pl.BlockSpec((4, CHUNK // ROWS, OWN, 640), lambda i, core: (0, i, 0, 0))
    return pl.pallas_call(
        attend_back_kernel,
        out_shape=(
            share,
            share,
            jax.ShapeDtypeStruct((KEYS, 512), HALF),
            jax.ShapeDtypeStruct((ROWS, 384), WIDE),
        ),
        grid_spec=pltpu.PrefetchScalarGridSpec(
            num_scalar_prefetch=1,
            grid=(KEYS // CHUNK,),
            in_specs=[
                whole(ROWS, 384),
                pl.BlockSpec((CHUNK, 512), lambda i, core: (i, 0)),
                pl.BlockSpec((CHUNK, 128), lambda i, core: (i, 0)),
                pl.BlockSpec((H_DEV, CHUNK, ROWS), lambda i, core: (0, i, 0)),
                whole(ROWS, D),
                whole(D, 256),
                whole(KVL, 512),
                whole(ROWS, 256),
            ],
            out_specs=(
                share_spec,
                share_spec,
                pl.BlockSpec((CHUNK, 512), lambda i, core: (i, 0)),
                whole(ROWS, 384),
            ),
            scratch_shapes=[
                pltpu.VMEM((H_DEV, 256, ROWS), WIDE),
                pltpu.VMEM((ROWS, H_DEV * DV), HALF),
                pltpu.VMEM((8 * H_DEV, ROWS), WIDE),
                pltpu.VMEM((H_DEV, ROWS, 256), HALF),
            ],
        ),
        compiler_params=pltpu.CompilerParams(vmem_limit_bytes=32 * 1024 * 1024),
        cost_estimate=pl.CostEstimate(
            flops=2 * H_DEV * ROWS * KEYS * 768 + 2 * KEYS * 512 * 512,
            bytes_accessed=24 << 20,
            transcendentals=0,
        ),
    )(ci.reshape(1), queries, kv_all, rot_all, probs, d_mid, wot, wkv, heads)


def expert_kernel(at_ref, x_ref, xo_ref, g_ref, go_ref, *rest):
    pieces = rest[:12]
    keep_in, send_in, keep_out, send_out, x_out, dso_out, hid_out, dpre_out = rest[12:20]
    wg_ref, wu_ref, wd_ref, dots_ref, sems = rest[20:]
    copies = []
    for part, target in enumerate((wg_ref, wu_ref, wd_ref)):
        for k in range(4):
            copy = pltpu.make_async_copy(
                pieces[4 * part + k],
                target.at[pl.ds(FFS * k, FFS), :],
                sems.at[4 * part + k],
            )
            copy.start()
            copies.append(copy)
        target[FFH:, :] = jnp.zeros((FFP - FFH, D), HALF)
    first = at_ref[0] == 0
    half = D // 2
    own = x_ref[:, :half]
    other = xo_ref[:, :half]
    x_out[:, :half] = jnp.where(first, own, other)
    x_out[:, half:] = jnp.where(first, other, own)
    gate = x_ref[:, half : half + 1].astype(WIDE)
    own = (g_ref[...].astype(WIDE) * gate).astype(HALF)
    other = (go_ref[...].astype(WIDE) * gate).astype(HALF)
    dso_out[:, :half] = jnp.where(first, own, other)
    dso_out[:, half:] = jnp.where(first, other, own)
    for copy in copies:
        copy.wait()

    def hidden_step(i, carry):
        at = pl.multiple_of(i * 256, 256)
        x = x_out[...]
        pre_gate = dot_nt(x, wg_ref[pl.ds(at, 256), :])
        pre_up = dot_nt(x, wu_ref[pl.ds(at, 256), :])
        d_hidden = dot_nt(dso_out[...], wd_ref[pl.ds(at, 256), :])
        sig = 1.0 / (1.0 + jnp.exp(-pre_gate))
        act = pre_gate * sig
        hid_out[:, pl.ds(at, 256)] = (act * pre_up).astype(HALF)
        slope = sig * (1.0 + pre_gate * (1.0 - sig))
        dpre_out[:, pl.ds(at, 256)] = (d_hidden * pre_up * slope).astype(HALF)
        dpre_out[:, pl.ds(pl.multiple_of(at + FFP, 256), 256)] = (d_hidden * act).astype(HALF)
        return carry

    lax.fori_loop(0, FFP // 256, hidden_step, 0)

    dots_ref[...] = jnp.zeros_like(dots_ref)

    def output_step(i, carry):
        at = pl.multiple_of(i * 256, 256)
        to = pl.multiple_of((i % 4) * 256, 256)
        own_side = (i // 4) == at_ref[0]
        d_in = dot_nn(dpre_out[:, :FFP], wg_ref[:, pl.ds(at, 256)])
        d_in = d_in + dot_nn(dpre_out[:, FFP:], wu_ref[:, pl.ds(at, 256)])
        d_in = d_in.astype(HALF)
        out = dot_nn(hid_out[...], wd_ref[:, pl.ds(at, 256)])
        g = jnp.where(own_side, g_ref[:, pl.ds(to, 256)], go_ref[:, pl.ds(to, 256)])
        dots = out * g.astype(WIDE)
        dots_ref[...] += dots[:, :128] + dots[:, 128:]
        out = out.astype(HALF)

        @pl.when(own_side)
        def _():
            keep_in[:, pl.ds(to, 256)] = d_in
            keep_out[:, pl.ds(to, 256)] = out

        @pl.when(jnp.logical_not(own_side))
        def _():
            send_in[:, pl.ds(to, 256)] = d_in
            send_out[:, pl.ds(to, 256)] = out

        return carry

    lax.fori_loop(0, D // 256, output_step, 0)
    total = jnp.sum(dots_ref[...], axis=1, keepdims=True)
    keep_in[:, half:] = jnp.broadcast_to(total, (16 * SLOTS, 128)).astype(HALF)
    send_in[:, half:] = jnp.zeros((16 * SLOTS, 128), HALF)


def run_expert(ci, x_own, x_other, g_own, g_other, pieces):
    rows = 16 * SLOTS
    vmem = pl.BlockSpec(memory_space=pltpu.VMEM)
    return pl.pallas_call(
        expert_kernel,
        out_shape=(
            jax.ShapeDtypeStruct((rows, D // 2 + 128), HALF),
            jax.ShapeDtypeStruct((rows, D // 2 + 128), HALF),
            jax.ShapeDtypeStruct((rows, D // 2), HALF),
            jax.ShapeDtypeStruct((rows, D // 2), HALF),
            jax.ShapeDtypeStruct((rows, D), HALF),
            jax.ShapeDtypeStruct((rows, D), HALF),
            jax.ShapeDtypeStruct((rows, FFP), HALF),
            jax.ShapeDtypeStruct((rows, 2 * FFP), HALF),
        ),
        in_specs=[pl.BlockSpec(memory_space=pltpu.SMEM)]
        + [vmem] * 4
        + [pl.BlockSpec(memory_space=pl.ANY)] * 12,
        out_specs=(vmem,) * 8,
        scratch_shapes=[pltpu.VMEM((FFP, D), HALF)] * 3
        + [pltpu.VMEM((rows, 128), WIDE), pltpu.SemaphoreType.DMA((12,))],
        compiler_params=pltpu.CompilerParams(vmem_limit_bytes=52 * 1024 * 1024),
        cost_estimate=pl.CostEstimate(
            flops=12 * rows * D * FFP, bytes_accessed=28 << 20, transcendentals=rows * FFP
        ),
    )(ci.reshape(1), x_own, x_other, g_own, g_other, *pieces)


def place_kernel(at_ref, *refs):
    out_ref = refs[4]
    step = pl.program_id(0)
    for k in range(4):

        @pl.when(step == k)
        def _():
            out_ref[0] = refs[k][...].astype(WIDE)


def place_pieces(yi, pieces, part):
    return pl.pallas_call(
        place_kernel,
        out_shape=jax.ShapeDtypeStruct((4, FFS, D), WIDE),
        grid_spec=pltpu.PrefetchScalarGridSpec(
            num_scalar_prefetch=1,
            grid=(4,),
            in_specs=[
                pl.BlockSpec((FFS, D), lambda k, at, i=i: (part if i == 2 else 0, 0))
                for i in range(4)
            ],
            out_specs=pl.BlockSpec((1, FFS, D), lambda k, at: ((at[0] + k) % 4, 0, 0)),
        ),
        compiler_params=pltpu.CompilerParams(vmem_limit_bytes=24 * 1024 * 1024),
        cost_estimate=pl.CostEstimate(flops=1, bytes_accessed=1, transcendentals=0),
    )(yi.reshape(1), *pieces)


def expert_grad_kernel(x_ref, dso_ref, hid_ref, dpre_ref, gate_ref, *rest):
    outs, far_ref = rest[:6], rest[6]
    targets, sems = rest[7:9], rest[9]
    copies = []

    def copy(source, target):
        moved = pltpu.make_async_copy(source, target, sems.at[len(copies)])
        moved.start()
        copies.append(moved)

    copy(gate_ref.at[pl.ds(2 * FFS, FFS), :], far_ref.at[pl.ds(0, FFS), :])
    for part, right in enumerate((x_ref, dso_ref)):
        target = targets[part]
        for c in range(FFP // 256):
            if part == 0:
                left = dpre_ref[:, FFP + 256 * c : FFP + 256 * c + 256]
            else:
                left = hid_ref[:, 256 * c : 256 * c + 256]
            target[256 * c : 256 * c + 256, :] = dot_tn(left, right[...]).astype(HALF)
        for i, k in enumerate((0, 1, 3)):
            copy(target.at[pl.ds(FFS * k, FFS), :], outs[3 * part + i])
        copy(target.at[pl.ds(2 * FFS, FFS), :], far_ref.at[pl.ds(FFS * (part + 1), FFS), :])
    for moved in copies:
        moved.wait()


def expert_grads(x_slots, d_slot_out, hidden, d_pre, grad_gate):
    vmem = pl.BlockSpec(memory_space=pltpu.VMEM)
    hbm = pl.BlockSpec(memory_space=pl.ANY)
    outs = pl.pallas_call(
        expert_grad_kernel,
        out_shape=(jax.ShapeDtypeStruct((FFS, D), HALF),) * 6
        + (jax.ShapeDtypeStruct((3 * FFS, D), HALF),),
        in_specs=[vmem] * 4 + [hbm],
        out_specs=(hbm,) * 7,
        scratch_shapes=[pltpu.VMEM((FFP, D), HALF)] * 2 + [pltpu.SemaphoreType.DMA((9,))],
        compiler_params=pltpu.CompilerParams(vmem_limit_bytes=40 * 1024 * 1024),
        cost_estimate=pl.CostEstimate(flops=1, bytes_accessed=1, transcendentals=0),
    )(x_slots, d_slot_out, hidden, d_pre, grad_gate)
    up_parts = [outs[0], outs[1], None, outs[2]]
    down_parts = [outs[3], outs[4], None, outs[5]]
    return up_parts, down_parts, outs[6]


def late_kernel(one_ref, so_ref, gated_ref, out_ref, core_ref, late_ref):
    late_ref[:, :D] = one_ref[...]
    routed = dot_tn(gated_ref[...], out_ref[...])
    half = D // 2
    first = (core_ref[0] == 0).astype(WIDE)
    late_ref[:, D : D + half] = (so_ref[:, :half] + routed * first).astype(HALF)
    late_ref[:, D + half :] = (so_ref[:, half:] + routed * (1.0 - first)).astype(HALF)


def late_products(ci, d_one, shared_out, gated, out_back):
    vmem = pl.BlockSpec(memory_space=pltpu.VMEM)
    return pl.pallas_call(
        late_kernel,
        out_shape=jax.ShapeDtypeStruct((ROWS, 2 * D), HALF),
        in_specs=[vmem] * 4 + [pl.BlockSpec(memory_space=pltpu.SMEM)],
        out_specs=vmem,
        compiler_params=pltpu.CompilerParams(vmem_limit_bytes=32 * 1024 * 1024),
        cost_estimate=pl.CostEstimate(flops=1, bytes_accessed=1, transcendentals=0),
    )(d_one, shared_out, gated, out_back, ci.reshape(1))


def rest_kernel(
    h_two_ref, dsp_ref, g_ref, sh_ref, h_one_ref, dq_ref, dmid_ref, heads_ref, c_ref, dkv_ref,
    wq_ref, norm_ref, out_ref, one_ref, gain_ref, kv_ref,
):
    d_one = dot_nt(dq_ref[...], wq_ref[...])
    one_ref[...] = d_one.astype(HALF)
    gain_ref[...] = jnp.sum(d_one * norm_ref[...], axis=0, keepdims=True)

    def step(i, carry):
        rows = pl.ds(pl.multiple_of(i * 256, 256), 256)
        out_ref[rows, 0:768] = dot_tn(h_two_ref[:, rows], dsp_ref[...]).astype(HALF)
        out_ref[rows, 768:1152] = dot_tn(g_ref[:, rows], sh_ref[...]).astype(HALF)
        out_ref[rows, 1152:1536] = dot_tn(h_one_ref[:, rows], dq_ref[...]).astype(HALF)
        out_ref[rows, 1536:1792] = dot_tn(dmid_ref[:, rows], heads_ref[...]).astype(HALF)
        return carry

    lax.fori_loop(0, D // 256, step, 0)
    kv_ref[...] = jnp.zeros_like(kv_ref)

    def kv_step(i, carry):
        rows = pl.ds(pl.multiple_of(i * CHUNK, CHUNK), CHUNK)
        kv_ref[...] += dot_tn(c_ref[rows, 0:KVL], dkv_ref[rows, :])
        return carry

    lax.fori_loop(0, KEYS // CHUNK, kv_step, 0)
    for e in range(16):
        for block in range(4):
            row = 128 * e + 32 * block
            out_ref[row : row + 32, 1792:1920] = kv_ref[
                32 * e : 32 * e + 32, 128 * block : 128 * block + 128
            ].astype(HALF)


def rest_products(*operands):
    vmem = pl.BlockSpec(memory_space=pltpu.VMEM)
    return pl.pallas_call(
        rest_kernel,
        out_shape=(
            jax.ShapeDtypeStruct((D, 1920), HALF),
            jax.ShapeDtypeStruct((ROWS, D), HALF),
            jax.ShapeDtypeStruct((1, D), WIDE),
        ),
        in_specs=[vmem] * 12,
        out_specs=(vmem,) * 3,
        scratch_shapes=[pltpu.VMEM((KVL, 512), WIDE)],
        compiler_params=pltpu.CompilerParams(vmem_limit_bytes=48 * 1024 * 1024),
        cost_estimate=pl.CostEstimate(flops=1, bytes_accessed=1, transcendentals=0),
    )(*operands)


def pack_query_columns(w):
    return jnp.concatenate(
        [w[:, 0:128], w[:, 192:320], w[:, 128:160], w[:, 320:352], w[:, 160:192], w[:, 352:384]],
        axis=1,
    )


def unpack_query_columns(w):
    return jnp.concatenate(
        [w[:, 0:128], w[:, 256:288], w[:, 320:352], w[:, 128:256], w[:, 288:320], w[:, 352:384]],
        axis=1,
    )


def pad_cols(w, width):
    return jnp.pad(w, ((0, 0), (0, width - w.shape[1])))


def silu_parts(gate):
    sig = jax.nn.sigmoid(gate)
    return gate * sig, sig * (1.0 + gate * (1.0 - sig))


def body(
    inputs,
    gain_attn,
    w_q,
    w_dkv,
    gain_latent,
    w_uk,
    w_uv,
    w_o,
    gain_ffn,
    w_router,
    w_sg,
    w_su,
    w_sd,
    w_eg,
    w_eu,
    w_ed,
    routes,
    seq_lengths,
    piece_starts,
    out_grad,
):
    zi, xi, yi, ci = (lax.axis_index(name) for name in ("z", "x", "y", "c"))
    ei = zi * 4 + xi
    ti = yi * 2 + ci

    def half_cols(value):
        return lax.dynamic_slice_in_dim(value, ci * (D // 2), D // 2, value.ndim - 1)

    def place_half(value):
        zero = jnp.zeros_like(value)
        return jnp.concatenate(
            [jnp.where(ci == 0, value, zero), jnp.where(ci == 0, zero, value)], axis=1
        )

    def swap_halves(v):
        return jnp.concatenate([v[:, 64:], v[:, :64]], axis=1)

    def ordered_cores(mine, other, axis):
        return jnp.concatenate(
            [jnp.where(ci == 0, mine, other), jnp.where(ci == 0, other, mine)], axis=axis
        )

    def both_cores(value, axis):
        return ordered_cores(value, swap_core(value), axis)

    def own_rows(value):
        return lax.dynamic_slice_in_dim(value, ti * OWN, OWN, 0)

    def sent_pieces(weight):
        return [
            lax.dynamic_index_in_dim(weight, (yi + by) % 4, 0, keepdims=False).astype(HALF)
            for by in range(4)
        ]

    def moved_pieces(sent):
        return [sent[0]] + [shift_y(sent[by], by) for by in (1, 2, 3)]

    gain_cols = jnp.stack([gain_attn, gain_ffn, jnp.pad(gain_latent, (0, 96))], axis=1)
    w_router_perm = w_router.reshape(128, 16, 4).transpose(0, 2, 1).reshape(128, EXPERTS)
    first_pack = jnp.concatenate(
        [
            w_dkv,
            w_router_perm,
            jnp.concatenate([w_uk, w_uv], axis=1).reshape(128, 128),
            pad_cols(gain_cols, 128),
            pack_query_columns(w_q),
            w_o.T,
        ],
        axis=1,
    ).astype(HALF)
    first_all = lax.all_gather(first_pack, EX, axis=0, tiled=True)
    gate_sent, up_sent, down_sent = sent_pieces(w_eg), sent_pieces(w_eu), sent_pieces(w_ed)
    gate_sent, up_sent, inputs_b, out_grad_b = lax.optimization_barrier(
        (gate_sent, up_sent, inputs, out_grad)
    )
    gate_pieces = moved_pieces(gate_sent)
    in_rows = gather_rows(inputs_b, yi, ci)
    g_rows = gather_rows(out_grad_b, yi, ci)
    second_pack = jnp.concatenate(
        [pad_cols(w_sg, SHP), pad_cols(w_su, SHP), pad_cols(w_sd.T, SHP)], axis=1
    ).astype(HALF)

    row_ids = ei * ROWS + jnp.arange(ROWS, dtype=jnp.int32)
    position, low, high = spans(row_ids, seq_lengths, piece_starts)
    inv_freq = 10000.0 ** (-(2.0 * jnp.arange(DR // 2, dtype=WIDE)) / DR)
    angles = position.astype(WIDE)[:, None] * inv_freq[None, :]
    cosine, sine = jnp.cos(angles), jnp.sin(angles)
    cos4 = jnp.concatenate([cosine] * 4, axis=1)
    sin4 = jnp.concatenate([-sine, -sine, sine, sine], axis=1)

    routes_t = routes.T
    expert_ids = 4 * lax.broadcasted_iota(jnp.int32, (16, 1, ROWS), 0) + yi
    named = jnp.max((routes_t[None] == expert_ids).astype(WIDE), axis=1)
    earlier = (
        lax.broadcasted_iota(jnp.int32, (ROWS, ROWS), 0)
        < lax.broadcasted_iota(jnp.int32, (ROWS, ROWS), 1)
    ).astype(HALF)
    rank = dot_nn(named.astype(HALF), earlier)
    slot_ids = lax.broadcasted_iota(jnp.int32, (16, SLOTS, ROWS), 1).astype(WIDE)
    picked = (named[:, None, :] > 0.5) & (rank[:, None, :] == slot_ids)
    select = picked.astype(HALF).reshape(16 * SLOTS, ROWS)

    in_wide = in_rows.astype(WIDE)
    normed_in = in_wide * inv_rms(in_wide)
    first_all, gate_pieces, up_sent, down_sent, second_pack = lax.optimization_barrier(
        (first_all, gate_pieces, up_sent, down_sent, second_pack)
    )
    normed_in, cos4, sin4, select = lax.optimization_barrier((normed_in, cos4, sin4, select))

    blk_b = first_all[:, 0:640]
    wkv_b = first_all[:, 640:768]
    pick = jnp.eye(8, 128, dtype=HALF)
    gains = dot_nt(pick, first_all[:, 768:896])
    wq_b = first_all[:, 896:1280]
    wot_b = first_all[:, 1280:1536]
    gain_one = gains[0]
    gain_two = gains[1]
    gain_lat = gains[2].reshape(16, 128)[:, :32].reshape(KVL)
    h_one = (normed_in * gain_one).astype(HALF)
    latent_all = dot_nn(h_one, blk_b)
    lat_part = latent_all[:, :KVL]
    scale_lat = inv_rms(lat_part)
    normed_lat = lat_part * scale_lat
    c_norm = (normed_lat * gain_lat).astype(HALF)
    rope_a, rope_b = latent_all[:, 512:544], latent_all[:, 544:576]
    rope = jnp.concatenate([rope_a, rope_a, rope_b, rope_b], axis=1)
    k_rot = rope * cos4 + swap_halves(rope) * sin4
    c_local = jnp.concatenate([c_norm, k_rot.astype(HALF)], axis=1)
    g_half = half_cols(g_rows)
    g_sent = dot_nn(select, g_half).astype(HALF).reshape(16, SLOTS, D // 2)
    c_local, up_sent, down_sent, g_sent, wq_b, wkv_b = lax.optimization_barrier(
        (c_local, up_sent, down_sent, g_sent, wq_b, wkv_b)
    )
    g_recv = spread(g_sent, EX).reshape(16 * SLOTS, D // 2)
    c_all = lax.all_gather(c_local, EX, axis=0, tiled=True)
    up_pieces = moved_pieces(up_sent)
    down_first = [down_sent[0], shift_y(down_sent[1], 1), None, shift_y(down_sent[3], 3)]
    wkv_b = wkv_b.reshape(KVL, 512)
    q_raw = dot_nn(h_one, wq_b)
    q_rot = q_raw[:, 256:]
    q_rot = q_rot * cos4 + swap_halves(q_rot) * sin4
    queries = jnp.concatenate([q_raw[:, :256], q_rot], axis=1).astype(HALF)
    c_all, queries, wot_b, wkv_b, up_pieces, down_first, g_recv, second_pack, down_sent = (
        lax.optimization_barrier(
            (c_all, queries, wot_b, wkv_b, up_pieces, down_first, g_recv, second_pack, down_sent)
        )
    )

    second_all = lax.all_gather(second_pack, EX, axis=0, tiled=True)
    kv_all = dot_nn(c_all[:, :KVL], wkv_b).astype(HALF)
    rot_all = c_all[:, KVL:]
    probs, heads_wide = attend(queries, kv_all, rot_all, low[None, :], high[None, :])
    attn_heads = heads_wide.astype(HALF)
    attn_own = sum_rows(dot_nt(attn_heads, wot_b).astype(HALF), yi, ci)

    in_own = inputs.astype(WIDE)
    mid_own = in_own + attn_own
    scale_two = inv_rms(mid_own)
    normed_two = mid_own * scale_two
    h_two_own = (normed_two * gain_two).astype(HALF)
    h_two = gather_rows(h_two_own, yi, ci)

    rope_router_b = blk_b[:, 512:640]
    logits_t = lax.dot_general(
        rope_router_b, h_two, (((0,), (1,)), ((), ())), preferred_element_type=WIDE
    )[64:]
    probs_t = jax.nn.softmax(logits_t, axis=0)
    gate_t = lax.dynamic_slice_in_dim(probs_t, yi * 16, 16, 0).astype(HALF).astype(WIDE)
    gated = jnp.where(picked, gate_t[:, None, :], 0.0)
    slot_gate = jnp.sum(gated, axis=2)
    gated = gated.astype(HALF).reshape(16 * SLOTS, ROWS)
    x_sent = dot_nn(select, half_cols(h_two)).astype(HALF).reshape(16, SLOTS, D // 2)
    slot_gate = jnp.broadcast_to(slot_gate[:, :, None], (16, SLOTS, 128)).astype(HALF)
    x_sent = jnp.concatenate([x_sent, slot_gate], axis=2)
    x_sent, g_own, down_sent, h_two = lax.optimization_barrier((x_sent, g_recv, down_sent, h_two))
    x_own = spread(x_sent, EX).reshape(16 * SLOTS, D // 2 + 128)
    g_other = swap_core(g_own)
    down_pieces = [down_first[0], down_first[1], shift_y(down_sent[2], 2), down_first[3]]

    wgu_b = second_all[:, : 2 * SHP]
    wsdt_b = second_all[:, 2 * SHP :]
    shared_pre = dot_nn(h_two, wgu_b)
    shared_gate, shared_up = shared_pre[:, :SHP], shared_pre[:, SHP:]
    shared_silu, shared_slope = silu_parts(shared_gate)
    shared_hidden = (shared_silu * shared_up).astype(HALF)
    shared_out = dot_nt(shared_hidden, wsdt_b)
    d_shared_hidden = dot_nn(g_rows, wsdt_b)
    d_shared_pre = jnp.concatenate(
        [d_shared_hidden * shared_up * shared_slope, d_shared_hidden * shared_silu], axis=1
    ).astype(HALF)
    d_shared_in = dot_nt(d_shared_pre, wgu_b)
    x_own, g_other, down_pieces, shared_out, d_shared_in, d_shared_pre, shared_hidden = (
        lax.optimization_barrier(
            (x_own, g_other, down_pieces, shared_out, d_shared_in, d_shared_pre, shared_hidden)
        )
    )

    x_other = swap_core(x_own)
    keep_in, send_in, keep_out, send_out, x_slots, d_slot_out, expert_hidden, d_expert_pre = (
        run_expert(
            ci, x_own, x_other, g_own, g_other, gate_pieces + up_pieces + down_pieces
        )
    )

    def pair(keep, send):
        return (keep.astype(WIDE) + swap_core(send).astype(WIDE)).astype(HALF)

    in_sent = pair(keep_in, send_in)
    grad_gate = dot_tn(d_expert_pre[:, :FFP], x_slots).astype(HALF)
    in_sent, grad_gate, keep_out, send_out, d_slot_out, expert_hidden, d_expert_pre = (
        lax.optimization_barrier(
            (in_sent, grad_gate, keep_out, send_out, d_slot_out, expert_hidden, d_expert_pre)
        )
    )
    in_recv = spread(in_sent.reshape(16, SLOTS, D // 2 + 128), EX)
    gate_back = [
        grad_gate[:FFS],
        shift_y(grad_gate[FFS : 2 * FFS], -1),
        None,
        shift_y(grad_gate[3 * FFS : FFH], -3),
    ]
    out_sent = pair(keep_out, send_out)
    up_parts, down_parts, far_parts = expert_grads(
        x_slots, d_slot_out, expert_hidden, d_expert_pre, grad_gate
    )
    in_recv, gate_back, up_parts, down_parts, far_parts = lax.optimization_barrier(
        (in_recv, gate_back, up_parts, down_parts, far_parts)
    )

    in_back = in_recv[:, :, : D // 2].reshape(16 * SLOTS, D // 2)
    slot_dots = in_recv[:, :, D // 2 : D // 2 + 1].astype(WIDE)
    d_route_t = jnp.sum(jnp.where(picked, slot_dots, 0.0), axis=1).astype(HALF)
    lane_at = (
        lax.broadcasted_iota(jnp.int32, (16, 128), 0) + yi * 16
        == lax.broadcasted_iota(jnp.int32, (16, 128), 1)
    ).astype(HALF)
    d_route_part = dot_tn(d_route_t, lane_at)
    d_h_part = d_shared_in + place_half(dot_tn(select, in_back))
    back_part = jnp.concatenate([d_h_part, d_route_part], axis=1).astype(HALF)
    back_own = sum_rows(back_part, yi, ci)

    logits_own = dot_nn(h_two_own, rope_router_b)[:, 64:]
    probs_own = jax.nn.softmax(logits_own, axis=-1)
    d_route = back_own[:, D : D + EXPERTS]
    d_logits = (
        probs_own * (d_route - jnp.sum(probs_own * d_route, axis=-1, keepdims=True))
    ).astype(HALF)
    d_logits_pad = jnp.pad(d_logits, ((0, 0), (64, 0)))
    d_h_two = back_own[:, :D] + dot_nt(d_logits_pad, rope_router_b)
    d_mid_norm, gain_two_part = norm_back(d_h_two, normed_two, scale_two, gain_two)
    d_mid_own = d_mid_norm + out_grad.astype(WIDE)
    d_attn_b = gather_rows(d_mid_own.astype(HALF), yi, ci)
    d_attn_b, up_parts = lax.optimization_barrier((d_attn_b, up_parts))

    up_back = [up_parts[0], shift_y(up_parts[1], -1), None, shift_y(up_parts[3], -3)]
    lat_keep, lat_send, d_kv, d_q = attend_back(
        ci, queries, kv_all, rot_all, probs, d_attn_b, wot_b, wkv_b, heads_wide
    )
    lat_keep, lat_send, d_kv, d_q, up_parts, up_back = lax.optimization_barrier(
        (lat_keep, lat_send, d_kv, d_q, up_parts, up_back)
    )
    lat_pieces = pair_pieces(lat_keep, lat_send, yi)
    lat_pieces, d_kv, d_q, d_attn_b, out_sent = lax.optimization_barrier(
        (lat_pieces, d_kv, d_q, d_attn_b, out_sent)
    )
    out_back = spread(out_sent.reshape(16, SLOTS, D // 2), EX).reshape(16 * SLOTS, D // 2)
    lat_total = add_pieces(lat_pieces)

    d_q_rot = d_q[:, 256:]
    d_q_rot = d_q_rot * cos4 - swap_halves(d_q_rot) * sin4
    d_queries = jnp.concatenate([d_q[:, :256], d_q_rot], axis=1).astype(HALF)
    rest_grads, d_one, gain_one_late = rest_products(
        h_two, d_shared_pre, g_rows, shared_hidden, h_one, d_queries, d_attn_b, attn_heads,
        c_all, d_kv, wq_b, normed_in,
    )
    lat_total, out_back, down_parts, far_parts, rest_grads = lax.optimization_barrier(
        (lat_total.astype(HALF), out_back, down_parts, far_parts, rest_grads)
    )
    rest_sum = lax.psum_scatter(rest_grads, EX, scatter_dimension=0, tiled=True)
    lat_parts = spread(lat_total, EX)
    far_back = shift_y(far_parts, -2)
    down_back = [down_parts[0], shift_y(down_parts[1], -1), None, shift_y(down_parts[3], -3)]
    lat_parts, d_one, out_back = lax.optimization_barrier((lat_parts, d_one, out_back))
    d_lat_own = jnp.sum(lat_parts.astype(WIDE), axis=0)

    cos_own, sin_own = own_rows(cos4), own_rows(sin4)
    d_rope = d_lat_own[:, 512:]
    d_rope = d_rope * cos_own - swap_halves(d_rope) * sin_own
    d_rope = jnp.concatenate(
        [d_rope[:, 0:32] + d_rope[:, 32:64], d_rope[:, 64:96] + d_rope[:, 96:128]], axis=1
    )
    d_lat, grad_gain_lat = norm_back(
        d_lat_own[:, :512], own_rows(normed_lat), own_rows(scale_lat), gain_lat
    )
    d_latent = jnp.concatenate([d_lat, d_rope], axis=1).astype(HALF)
    d_latent_pad = jnp.pad(d_latent, ((0, 0), (0, 64)))
    d_chip = both_cores(jnp.concatenate([d_latent, d_logits], axis=1), 0)
    d_chip, d_one, out_back = lax.optimization_barrier((d_chip, d_one, out_back))
    late_parts = late_products(ci, d_one, shared_out, gated, out_back).reshape(4, 2, OWN, 2 * D)
    late_pieces = pair_pieces(
        lax.dynamic_index_in_dim(late_parts, ci, 1, keepdims=False),
        lax.dynamic_index_in_dim(late_parts, 1 - ci, 1, keepdims=False),
        yi,
    )
    d_lat_one = dot_nt(d_latent_pad, blk_b)
    scale_one = inv_rms(in_own)
    normed_one = in_own * scale_one
    gain_one_part = gain_one_late[0] + jnp.sum(d_lat_one * normed_one, axis=0)

    def chip_rows(value):
        return lax.dynamic_slice_in_dim(value, yi * 2 * OWN, 2 * OWN, 0)

    def own_half(value):
        half = value.shape[1] // 2
        return jnp.where(ci == 0, value[:, :half], value[:, half:])

    grad_dkv = dot_tn(chip_rows(h_one), own_half(d_chip[:, :576]))
    grad_router = dot_tn(chip_rows(h_two), own_half(d_chip[:, 576:]))
    gain_lat_wide = jnp.pad(grad_gain_lat.reshape(16, 32), ((0, 0), (0, 96))).reshape(D)
    gain_rows = jnp.stack([gain_one_part, gain_two_part, gain_lat_wide], axis=0).astype(HALF)
    gain_at = (
        lax.broadcasted_iota(jnp.int32, (3, 64), 0) == lax.broadcasted_iota(jnp.int32, (3, 64), 1)
    ).astype(HALF)
    last_part = jnp.concatenate([grad_dkv, grad_router, dot_tn(gain_rows, gain_at)], axis=1)
    last_parts = spread(last_part.astype(HALF).reshape(16, 128, 384), EX)
    last_parts, far_back, down_back, late_pieces = lax.optimization_barrier(
        (last_parts, far_back, down_back, late_pieces)
    )
    last_sum = jnp.sum(last_parts.astype(WIDE), axis=0).astype(HALF)
    last_sum = add_pieces([last_sum] * 4).astype(HALF)
    last_other = swap_core(last_sum)
    sum_dkv = ordered_cores(last_sum[:, :288], last_other[:, :288], 1).astype(WIDE)
    sum_router = ordered_cores(last_sum[:, 288:320], last_other[:, 288:320], 1)
    sum_router = sum_router.reshape(128, 4, 16).transpose(0, 2, 1).reshape(128, EXPERTS).astype(WIDE)
    gain_sums = last_sum[:, 320:323].astype(WIDE) + last_other[:, 320:323].astype(WIDE)
    late_own = add_pieces(late_pieces)
    up_back[2] = gate_back[2] = down_back[2] = far_back
    grad_eg = place_pieces(yi, gate_back, 0)
    grad_eu = place_pieces(yi, up_back, 1)
    grad_ed = place_pieces(yi, down_back, 2)
    layer_out = (mid_own + late_own[:, D:]).astype(HALF)
    d_in_norm, _ = norm_back(late_own[:, :D] + d_lat_one, normed_one, scale_one, gain_one)
    grad_inputs = (d_mid_own + d_in_norm).astype(HALF)
    rest_sum = rest_sum.astype(WIDE)
    sum_kv = rest_sum[:, 1792:].reshape(4, 32, 128).transpose(1, 0, 2).reshape(32, 512)
    return (
        layer_out,
        grad_inputs,
        gain_sums[:, 0],
        unpack_query_columns(rest_sum[:, 1152:1536]),
        sum_dkv,
        gain_sums[:32, 2],
        sum_kv[:, :256],
        sum_kv[:, 256:],
        rest_sum[:, 1536:1792].T,
        gain_sums[:, 1],
        sum_router,
        rest_sum[:, :352],
        rest_sum[:, SHP : SHP + 352],
        rest_sum[:, 2 * SHP : 2 * SHP + 352].T,
        grad_eg,
        grad_eu,
        grad_ed,
    )


def solution(mesh):
    grid = Mesh(mesh.devices.reshape(4, 4, 4, 2), ("z", "x", "y", "c"))
    ten = ("y", "c")
    rows = P(("z", "x", "y", "c"), None)
    wide = P(EX, ten)
    tall = P(ten, EX)
    expert = P(EX, ten, None)
    return jax.shard_map(
        body,
        mesh=grid,
        in_specs=(
            rows,
            P(EX),
            wide,
            P(EX, None),
            P(EX),
            wide,
            wide,
            tall,
            P(EX),
            P(EX, None),
            wide,
            wide,
            tall,
            expert,
            expert,
            expert,
            P(EX, None),
            P(),
            P(),
            rows,
        ),
        out_specs=(
            rows,
            rows,
            P(EX),
            wide,
            P(EX, None),
            P(EX),
            wide,
            wide,
            tall,
            P(EX),
            P(EX, None),
            wide,
            wide,
            tall,
            expert,
            expert,
            expert,
        ),
        check_vma=False,
    )
```

```python
import jax
import jax.numpy as jnp
from jax import lax
from jax.experimental import pallas as pl
from jax.experimental.layout import Layout, with_layout_constraint
from jax.experimental.pallas import tpu as pltpu
from jax.sharding import Mesh, PartitionSpec as P

D = 2048
H_DEV = 2
DN = 128
DV = 128
DR = 64
KVL = 512
PIECE = 256
EXPERTS = 64
ROWS = 256
OWN = 32
SLOTS = 40
FFH = 704
FFS = 176
FFP = 768
SHP = 384
KEYS = 4096
CHUNK = 512
EPS = 1e-06
NEG = -1e30
SCALE = (DN + DR) ** (-0.5)
EX = ("z", "x")
HALF = jnp.bfloat16
WIDE = jnp.float32


def dot_nn(left, right):
    return jnp.dot(left, right, preferred_element_type=WIDE)


def dot_nt(left, right):
    return lax.dot_general(left, right, (((1,), (1,)), ((), ())), preferred_element_type=WIDE)


def dot_tn(left, right):
    return lax.dot_general(left, right, (((0,), (0,)), ((), ())), preferred_element_type=WIDE)


def inv_rms(values):
    return lax.rsqrt(jnp.mean(values * values, axis=-1, keepdims=True) + EPS)


def norm_back(grad, normed, row_scale, gain):
    scaled = grad * gain
    inner_mean = jnp.mean(scaled * normed, axis=-1, keepdims=True)
    return (row_scale * (scaled - normed * inner_mean), jnp.sum(grad * normed, axis=0))


def row_major(value):
    return with_layout_constraint(value, Layout(major_to_minor=(0, 1)))


def swap_core(value):
    return lax.ppermute(value, "c", [(0, 1), (1, 0)])


def shift_y(value, by):
    return lax.ppermute(value, "y", [(i, (i + by) % 4) for i in range(4)])


def spread(value, axes):
    return lax.all_to_all(value, axes, split_axis=0, concat_axis=0, tiled=True)


def gather_rows(value, yi, ci):
    n = value.shape[1]
    block = jnp.zeros((4, OWN, n), value.dtype)
    block = lax.dynamic_update_slice(block, value[None], (yi, 0, 0))
    for by in (1, 2, 3):
        block = lax.dynamic_update_slice(block, shift_y(value, by)[None], ((yi - by) % 4, 0, 0))
    other = swap_core(block)
    first = jnp.where(ci == 0, block, other)
    second = jnp.where(ci == 0, other, block)
    return jnp.stack([first, second], axis=1).reshape(ROWS, n)


def pair_pieces(keep, send, yi):
    other = swap_core(send)
    pieces = []
    for by in range(4):
        at = (yi + by) % 4
        mine = lax.dynamic_index_in_dim(keep, at, 0, keepdims=False).astype(WIDE)
        theirs = lax.dynamic_index_in_dim(other, at, 0, keepdims=False).astype(WIDE)
        pieces.append((mine + theirs).astype(HALF))
    return pieces


def add_pieces(pieces):
    total = pieces[0].astype(WIDE)
    for by in (1, 2, 3):
        total = total + shift_y(pieces[by], by).astype(WIDE)
    return total


def sum_rows(value, yi, ci):
    parts = value.reshape(4, 2, OWN, value.shape[1])
    mine = lax.dynamic_index_in_dim(parts, ci, 1, keepdims=False)
    theirs = lax.dynamic_index_in_dim(parts, 1 - ci, 1, keepdims=False)
    return add_pieces(pair_pieces(mine, theirs, yi))


def sum_experts(value):
    rows, width = value.shape
    parts = spread(value.reshape(16, rows // 16, width), EX)
    return jnp.sum(parts.astype(WIDE), axis=0)


def spans(row_ids, seq_lengths, piece_starts):
    ends = jnp.cumsum(seq_lengths)
    starts = ends - seq_lengths
    member = (row_ids[:, None] >= starts[None, :]) & (row_ids[:, None] < ends[None, :])
    member = member.astype(jnp.int32)
    low = jnp.sum(member * starts[None, :], axis=1)
    end = jnp.sum(member * ends[None, :], axis=1)
    inside = (row_ids[:, None] >= piece_starts[None, :]) & (
        row_ids[:, None] < piece_starts[None, :] + PIECE
    )
    piece_last = jnp.max(jnp.where(inside, piece_starts[None, :] + (PIECE - 1), -1), axis=1)
    high = jnp.where(piece_last >= 0, jnp.minimum(piece_last, end - 1), row_ids)
    return row_ids - low, low, high


def head_query(q_ref, head):
    lane = lax.broadcasted_iota(jnp.int32, (ROWS, 128), 1)
    rot = q_ref[:, 256:384]
    rot = jnp.where((lane // 32) % 2 == head, rot, jnp.zeros_like(rot))
    return jnp.concatenate([q_ref[:, 128 * head : 128 * head + 128], rot], axis=1)


def attend_kernel(q_ref, kv_ref, rot_ref, low_ref, high_ref, p_ref, o_ref, s_ref):
    low = low_ref[...]
    high = high_ref[...]
    for head in range(H_DEV):
        query = head_query(q_ref, head)

        def scores_step(i, top):
            at = pl.multiple_of(i * CHUNK, CHUNK)
            key = jnp.concatenate(
                [
                    kv_ref[pl.ds(at, CHUNK), 128 * head : 128 * head + 128],
                    rot_ref[pl.ds(at, CHUNK), :],
                ],
                axis=1,
            )
            scores = dot_nt(key, query) * SCALE
            col = lax.broadcasted_iota(jnp.int32, (CHUNK, ROWS), 0) + at
            scores = jnp.where((col >= low) & (col <= high), scores, NEG)
            s_ref[pl.ds(at, CHUNK), :] = scores
            return jnp.maximum(top, jnp.max(scores.reshape(CHUNK // 8, 8, ROWS), axis=0))

        top = lax.fori_loop(
            0, KEYS // CHUNK, scores_step, jnp.full((8, ROWS), NEG, WIDE)
        )
        top = jnp.max(top, axis=0, keepdims=True)

        def exp_step(i, total):
            at = pl.multiple_of(i * CHUNK, CHUNK)
            weights = jnp.exp(s_ref[pl.ds(at, CHUNK), :] - top)
            s_ref[pl.ds(at, CHUNK), :] = weights
            return total + jnp.sum(weights.reshape(CHUNK // 8, 8, ROWS), axis=0)

        total = lax.fori_loop(0, KEYS // CHUNK, exp_step, jnp.zeros((8, ROWS), WIDE))
        inverse = 1.0 / jnp.sum(total, axis=0, keepdims=True)

        def value_step(i, acc):
            at = pl.multiple_of(i * CHUNK, CHUNK)
            probs = (s_ref[pl.ds(at, CHUNK), :] * inverse).astype(HALF)
            p_ref[head, pl.ds(at, CHUNK), :] = probs
            value = kv_ref[pl.ds(at, CHUNK), 256 + 128 * head : 384 + 128 * head]
            return acc + dot_tn(value, probs)

        out = lax.fori_loop(0, KEYS // CHUNK, value_step, jnp.zeros((DN, ROWS), WIDE))
        o_ref[:, 128 * head : 128 * head + 128] = out.T


def attend(queries, kv_all, rot_all, low, high):
    vmem = pl.BlockSpec(memory_space=pltpu.VMEM)
    return pl.pallas_call(
        attend_kernel,
        out_shape=(
            jax.ShapeDtypeStruct((H_DEV, KEYS, ROWS), HALF),
            jax.ShapeDtypeStruct((ROWS, H_DEV * DN), WIDE),
        ),
        in_specs=[vmem] * 5,
        out_specs=(vmem, vmem),
        scratch_shapes=[pltpu.VMEM((KEYS, ROWS), WIDE)],
        compiler_params=pltpu.CompilerParams(vmem_limit_bytes=40 * 1024 * 1024),
        cost_estimate=pl.CostEstimate(
            flops=2 * H_DEV * ROWS * KEYS * 384, bytes_accessed=12 << 20, transcendentals=2 << 20
        ),
    )(queries, kv_all, rot_all, low, high)


def attend_back_kernel(
    core_ref, q_ref, kv_ref, rot_ref, p_ref, dmid_ref, wot_ref, wkv_ref, o_ref,
    keep_ref, send_ref, dkv_ref, dq_ref, acc_ref, do_ref, delta_ref, qf_ref,
):
    step = pl.program_id(0)

    @pl.when(step == 0)
    def _():
        acc_ref[...] = jnp.zeros_like(acc_ref)
        d_heads = dot_nn(dmid_ref[...], wot_ref[...]).astype(HALF)
        do_ref[...] = d_heads
        product = d_heads.astype(WIDE) * o_ref[...]
        for head in range(H_DEV):
            delta_ref[8 * head : 8 * head + 8, :] = lax.dot_general(
                jnp.ones((8, 128), WIDE),
                product[:, 128 * head : 128 * head + 128],
                (((1,), (1,)), ((), ())),
                precision=lax.Precision.HIGHEST,
                preferred_element_type=WIDE,
            )
            qf_ref[head] = head_query(q_ref, head)

    rot = rot_ref[...]
    d_rot = jnp.zeros((CHUNK, 128), WIDE)
    for head in range(H_DEV):
        d_out = do_ref[:, 128 * head : 128 * head + 128]
        value = kv_ref[:, 256 + 128 * head : 384 + 128 * head]
        probs = p_ref[head]
        d_probs = dot_nt(value, d_out)
        d_scores = (
            probs.astype(WIDE) * (d_probs - delta_ref[8 * head : 8 * head + 1, :])
        ).astype(HALF)
        d_key = dot_nn(d_scores, qf_ref[head]) * SCALE
        dkv_ref[:, 128 * head : 128 * head + 128] = d_key[:, :128].astype(HALF)
        d_rot = d_rot + d_key[:, 128:]
        dkv_ref[:, 256 + 128 * head : 384 + 128 * head] = dot_nn(probs, d_out).astype(HALF)
        key = jnp.concatenate([kv_ref[:, 128 * head : 128 * head + 128], rot], axis=1)
        acc_ref[head] += dot_tn(key, d_scores)
    d_lat = dot_nt(dkv_ref[...], wkv_ref[...]).astype(HALF)
    d_rot = d_rot.astype(HALF)

    def write(target, core):
        for block in range(CHUNK // ROWS):
            for y in range(4):
                row = ROWS * block + OWN * (2 * y + core)
                target[y, block, :, :512] = d_lat[row : row + OWN]
                target[y, block, :, 512:] = d_rot[row : row + OWN]

    @pl.when(core_ref[0] == 0)
    def _():
        write(keep_ref, 0)
        write(send_ref, 1)

    @pl.when(core_ref[0] != 0)
    def _():
        write(keep_ref, 1)
        write(send_ref, 0)

    @pl.when(step == KEYS // CHUNK - 1)
    def _():
        lane = lax.broadcasted_iota(jnp.int32, (ROWS, 128), 1)
        d_q_rot = jnp.zeros((ROWS, 128), WIDE)
        for head in range(H_DEV):
            d_query = acc_ref[head].T * SCALE
            dq_ref[:, 128 * head : 128 * head + 128] = d_query[:, :128]
            d_q_rot = jnp.where((lane // 32) % 2 == head, d_query[:, 128:], d_q_rot)
        dq_ref[:, 256:384] = d_q_rot


def attend_back(ci, queries, kv_all, rot_all, probs, d_mid, wot, wkv, heads):
    def whole(*shape):
        return pl.BlockSpec(shape, lambda i, core: (0,) * len(shape))

    share = jax.ShapeDtypeStruct((4, 16, OWN, 640), HALF)
    share_spec = pl.BlockSpec((4, CHUNK // ROWS, OWN, 640), lambda i, core: (0, i, 0, 0))
    return pl.pallas_call(
        attend_back_kernel,
        out_shape=(
            share,
            share,
            jax.ShapeDtypeStruct((KEYS, 512), HALF),
            jax.ShapeDtypeStruct((ROWS, 384), WIDE),
        ),
        grid_spec=pltpu.PrefetchScalarGridSpec(
            num_scalar_prefetch=1,
            grid=(KEYS // CHUNK,),
            in_specs=[
                whole(ROWS, 384),
                pl.BlockSpec((CHUNK, 512), lambda i, core: (i, 0)),
                pl.BlockSpec((CHUNK, 128), lambda i, core: (i, 0)),
                pl.BlockSpec((H_DEV, CHUNK, ROWS), lambda i, core: (0, i, 0)),
                whole(ROWS, D),
                whole(D, 256),
                whole(KVL, 512),
                whole(ROWS, 256),
            ],
            out_specs=(
                share_spec,
                share_spec,
                pl.BlockSpec((CHUNK, 512), lambda i, core: (i, 0)),
                whole(ROWS, 384),
            ),
            scratch_shapes=[
                pltpu.VMEM((H_DEV, 256, ROWS), WIDE),
                pltpu.VMEM((ROWS, H_DEV * DV), HALF),
                pltpu.VMEM((8 * H_DEV, ROWS), WIDE),
                pltpu.VMEM((H_DEV, ROWS, 256), HALF),
            ],
        ),
        compiler_params=pltpu.CompilerParams(vmem_limit_bytes=32 * 1024 * 1024),
        cost_estimate=pl.CostEstimate(flops=1, bytes_accessed=1, transcendentals=0),
    )(ci.reshape(1), queries, kv_all, rot_all, probs, d_mid, wot, wkv, heads)


def expert_kernel(at_ref, x_ref, xo_ref, g_ref, go_ref, *rest):
    pieces = rest[:12]
    keep_in, send_in, keep_out, send_out = rest[12:16]
    saved = rest[16:20]
    wg_ref, wu_ref, wd_ref, dots_ref, x_out, dso_out, hid_out, dpre_out, sems = rest[20:]
    copies = []
    leaving = []

    def leave(i, source):
        copy = pltpu.make_async_copy(source, saved[i], sems.at[12 + i])
        copy.start()
        leaving.append(copy)

    for part, target in enumerate((wg_ref, wu_ref, wd_ref)):
        for k in range(4):
            copy = pltpu.make_async_copy(
                pieces[4 * part + k],
                target.at[pl.ds(FFS * k, FFS), :],
                sems.at[4 * part + k],
            )
            copy.start()
            copies.append(copy)
        target[FFH:, :] = jnp.zeros((FFP - FFH, D), HALF)
    first = at_ref[0] == 0
    half = D // 2
    own = x_ref[:, :half]
    other = xo_ref[:, :half]
    x_out[:, :half] = jnp.where(first, own, other)
    x_out[:, half:] = jnp.where(first, other, own)
    gate = x_ref[:, half : half + 1].astype(WIDE)
    own = (g_ref[...].astype(WIDE) * gate).astype(HALF)
    other = (go_ref[...].astype(WIDE) * gate).astype(HALF)
    dso_out[:, :half] = jnp.where(first, own, other)
    dso_out[:, half:] = jnp.where(first, other, own)
    leave(0, x_out)
    leave(1, dso_out)
    for copy in copies:
        copy.wait()

    def hidden_step(i, carry):
        at = pl.multiple_of(i * 256, 256)
        x = x_out[...]
        pre_gate = dot_nt(x, wg_ref[pl.ds(at, 256), :])
        pre_up = dot_nt(x, wu_ref[pl.ds(at, 256), :])
        d_hidden = dot_nt(dso_out[...], wd_ref[pl.ds(at, 256), :])
        sig = 1.0 / (1.0 + jnp.exp(-pre_gate))
        act = pre_gate * sig
        hid_out[:, pl.ds(at, 256)] = (act * pre_up).astype(HALF)
        slope = sig * (1.0 + pre_gate * (1.0 - sig))
        dpre_out[:, pl.ds(at, 256)] = (d_hidden * pre_up * slope).astype(HALF)
        dpre_out[:, pl.ds(pl.multiple_of(at + FFP, 256), 256)] = (d_hidden * act).astype(HALF)
        return carry

    lax.fori_loop(0, FFP // 256, hidden_step, 0)

    leave(2, hid_out)
    leave(3, dpre_out)
    dots_ref[...] = jnp.zeros_like(dots_ref)

    def output_step(i, carry):
        at = pl.multiple_of(i * 256, 256)
        to = pl.multiple_of((i % 4) * 256, 256)
        own_side = (i // 4) == at_ref[0]
        d_in = dot_nn(dpre_out[:, :FFP], wg_ref[:, pl.ds(at, 256)])
        d_in = d_in + dot_nn(dpre_out[:, FFP:], wu_ref[:, pl.ds(at, 256)])
        d_in = d_in.astype(HALF)
        out = dot_nn(hid_out[...], wd_ref[:, pl.ds(at, 256)])
        g = jnp.where(own_side, g_ref[:, pl.ds(to, 256)], go_ref[:, pl.ds(to, 256)])
        dots = out * g.astype(WIDE)
        dots_ref[...] += dots[:, :128] + dots[:, 128:]
        out = out.astype(HALF)

        @pl.when(own_side)
        def _():
            keep_in[:, pl.ds(to, 256)] = d_in
            keep_out[:, pl.ds(to, 256)] = out

        @pl.when(jnp.logical_not(own_side))
        def _():
            send_in[:, pl.ds(to, 256)] = d_in
            send_out[:, pl.ds(to, 256)] = out

        return carry

    lax.fori_loop(0, D // 256, output_step, 0)
    total = jnp.sum(dots_ref[...], axis=1, keepdims=True)
    keep_in[:, half:] = jnp.broadcast_to(total, (16 * SLOTS, 128)).astype(HALF)
    send_in[:, half:] = jnp.zeros((16 * SLOTS, 128), HALF)
    for copy in leaving:
        copy.wait()


def run_expert(ci, x_own, x_other, g_own, g_other, pieces):
    rows = 16 * SLOTS
    vmem = pl.BlockSpec(memory_space=pltpu.VMEM)
    return pl.pallas_call(
        expert_kernel,
        out_shape=(
            jax.ShapeDtypeStruct((rows, D // 2 + 128), HALF),
            jax.ShapeDtypeStruct((rows, D // 2 + 128), HALF),
            jax.ShapeDtypeStruct((rows, D // 2), HALF),
            jax.ShapeDtypeStruct((rows, D // 2), HALF),
            jax.ShapeDtypeStruct((rows, D), HALF),
            jax.ShapeDtypeStruct((rows, D), HALF),
            jax.ShapeDtypeStruct((rows, FFP), HALF),
            jax.ShapeDtypeStruct((rows, 2 * FFP), HALF),
        ),
        in_specs=[pl.BlockSpec(memory_space=pltpu.SMEM)]
        + [vmem] * 4
        + [pl.BlockSpec(memory_space=pl.ANY)] * 12,
        out_specs=(vmem,) * 4 + (pl.BlockSpec(memory_space=pl.ANY),) * 4,
        scratch_shapes=[pltpu.VMEM((FFP, D), HALF)] * 3
        + [
            pltpu.VMEM((rows, 128), WIDE),
            pltpu.VMEM((rows, D), HALF),
            pltpu.VMEM((rows, D), HALF),
            pltpu.VMEM((rows, FFP), HALF),
            pltpu.VMEM((rows, 2 * FFP), HALF),
            pltpu.SemaphoreType.DMA((16,)),
        ],
        compiler_params=pltpu.CompilerParams(vmem_limit_bytes=52 * 1024 * 1024),
        cost_estimate=pl.CostEstimate(
            flops=12 * rows * D * FFP, bytes_accessed=28 << 20, transcendentals=rows * FFP
        ),
    )(ci.reshape(1), x_own, x_other, g_own, g_other, *pieces)


def place_kernel(at_ref, *refs):
    out_ref = refs[4]
    step = pl.program_id(0)
    for k in range(4):

        @pl.when(step == k)
        def _():
            out_ref[0] = refs[k][...].astype(WIDE)


def place_pieces(yi, pieces, part):
    return pl.pallas_call(
        place_kernel,
        out_shape=jax.ShapeDtypeStruct((4, FFS, D), WIDE),
        grid_spec=pltpu.PrefetchScalarGridSpec(
            num_scalar_prefetch=1,
            grid=(4,),
            in_specs=[
                pl.BlockSpec((FFS, D), lambda k, at, i=i: (part if i == 2 else 0, 0))
                for i in range(4)
            ],
            out_specs=pl.BlockSpec((1, FFS, D), lambda k, at: ((at[0] + k) % 4, 0, 0)),
        ),
        compiler_params=pltpu.CompilerParams(vmem_limit_bytes=24 * 1024 * 1024),
        cost_estimate=pl.CostEstimate(flops=1, bytes_accessed=1, transcendentals=0),
    )(yi.reshape(1), *pieces)


def expert_grad_kernel(x_ref, dso_ref, hid_ref, dpre_ref, gate_ref, *rest):
    outs, far_ref = rest[:6], rest[6]
    targets, sems = rest[7:9], rest[9]
    copies = []

    def copy(source, target):
        moved = pltpu.make_async_copy(source, target, sems.at[len(copies)])
        moved.start()
        copies.append(moved)

    copy(gate_ref.at[pl.ds(2 * FFS, FFS), :], far_ref.at[pl.ds(0, FFS), :])
    for part, right in enumerate((x_ref, dso_ref)):
        target = targets[part]
        for c in range(FFP // 256):
            if part == 0:
                left = dpre_ref[:, FFP + 256 * c : FFP + 256 * c + 256]
            else:
                left = hid_ref[:, 256 * c : 256 * c + 256]
            target[256 * c : 256 * c + 256, :] = dot_tn(left, right[...]).astype(HALF)
        for i, k in enumerate((0, 1, 3)):
            copy(target.at[pl.ds(FFS * k, FFS), :], outs[3 * part + i])
        copy(target.at[pl.ds(2 * FFS, FFS), :], far_ref.at[pl.ds(FFS * (part + 1), FFS), :])
    for moved in copies:
        moved.wait()


def expert_grads(x_slots, d_slot_out, hidden, d_pre, grad_gate):
    vmem = pl.BlockSpec(memory_space=pltpu.VMEM)
    hbm = pl.BlockSpec(memory_space=pl.ANY)
    outs = pl.pallas_call(
        expert_grad_kernel,
        out_shape=(jax.ShapeDtypeStruct((FFS, D), HALF),) * 6
        + (jax.ShapeDtypeStruct((3 * FFS, D), HALF),),
        in_specs=[vmem] * 4 + [hbm],
        out_specs=(hbm,) * 7,
        scratch_shapes=[pltpu.VMEM((FFP, D), HALF)] * 2 + [pltpu.SemaphoreType.DMA((9,))],
        compiler_params=pltpu.CompilerParams(vmem_limit_bytes=40 * 1024 * 1024),
        cost_estimate=pl.CostEstimate(flops=1, bytes_accessed=1, transcendentals=0),
    )(x_slots, d_slot_out, hidden, d_pre, grad_gate)
    up_parts = [outs[0], outs[1], None, outs[2]]
    down_parts = [outs[3], outs[4], None, outs[5]]
    return up_parts, down_parts, outs[6]


def late_kernel(one_ref, so_ref, gated_ref, out_ref, core_ref, late_ref):
    late_ref[:, :D] = one_ref[...]
    routed = dot_tn(gated_ref[...], out_ref[...])
    half = D // 2
    first = (core_ref[0] == 0).astype(WIDE)
    late_ref[:, D : D + half] = (so_ref[:, :half] + routed * first).astype(HALF)
    late_ref[:, D + half :] = (so_ref[:, half:] + routed * (1.0 - first)).astype(HALF)


def late_products(ci, d_one, shared_out, gated, out_back):
    vmem = pl.BlockSpec(memory_space=pltpu.VMEM)
    return pl.pallas_call(
        late_kernel,
        out_shape=jax.ShapeDtypeStruct((ROWS, 2 * D), HALF),
        in_specs=[vmem] * 4 + [pl.BlockSpec(memory_space=pltpu.SMEM)],
        out_specs=vmem,
        compiler_params=pltpu.CompilerParams(vmem_limit_bytes=32 * 1024 * 1024),
        cost_estimate=pl.CostEstimate(flops=1, bytes_accessed=1, transcendentals=0),
    )(d_one, shared_out, gated, out_back, ci.reshape(1))


def rest_kernel(
    h_two_ref, dsp_ref, g_ref, sh_ref, h_one_ref, dq_ref, dmid_ref, heads_ref, c_ref, dkv_ref,
    wq_ref, norm_ref, out_ref, one_ref, gain_ref, kv_ref,
):
    d_one = dot_nt(dq_ref[...], wq_ref[...])
    one_ref[...] = d_one.astype(HALF)
    gain_ref[...] = jnp.sum(d_one * norm_ref[...], axis=0, keepdims=True)

    def step(i, carry):
        rows = pl.ds(pl.multiple_of(i * 256, 256), 256)
        out_ref[rows, 0:768] = dot_tn(h_two_ref[:, rows], dsp_ref[...]).astype(HALF)
        out_ref[rows, 768:1152] = dot_tn(g_ref[:, rows], sh_ref[...]).astype(HALF)
        out_ref[rows, 1152:1536] = dot_tn(h_one_ref[:, rows], dq_ref[...]).astype(HALF)
        out_ref[rows, 1536:1792] = dot_tn(dmid_ref[:, rows], heads_ref[...]).astype(HALF)
        return carry

    lax.fori_loop(0, D // 256, step, 0)
    kv_ref[...] = jnp.zeros_like(kv_ref)

    def kv_step(i, carry):
        rows = pl.ds(pl.multiple_of(i * CHUNK, CHUNK), CHUNK)
        kv_ref[...] += dot_tn(c_ref[rows, 0:KVL], dkv_ref[rows, :])
        return carry

    lax.fori_loop(0, KEYS // CHUNK, kv_step, 0)
    for e in range(16):
        for block in range(4):
            row = 128 * e + 32 * block
            out_ref[row : row + 32, 1792:1920] = kv_ref[
                32 * e : 32 * e + 32, 128 * block : 128 * block + 128
            ].astype(HALF)


def rest_products(*operands):
    vmem = pl.BlockSpec(memory_space=pltpu.VMEM)
    return pl.pallas_call(
        rest_kernel,
        out_shape=(
            jax.ShapeDtypeStruct((D, 1920), HALF),
            jax.ShapeDtypeStruct((ROWS, D), HALF),
            jax.ShapeDtypeStruct((1, D), WIDE),
        ),
        in_specs=[vmem] * 12,
        out_specs=(vmem,) * 3,
        scratch_shapes=[pltpu.VMEM((KVL, 512), WIDE)],
        compiler_params=pltpu.CompilerParams(vmem_limit_bytes=48 * 1024 * 1024),
        cost_estimate=pl.CostEstimate(flops=1, bytes_accessed=1, transcendentals=0),
    )(*operands)


def latent_kernel(
    parts_ref, cos_ref, sin_ref, norm_ref, scale_ref, gain_ref, blk_ref, one_ref, logits_ref,
    chip_ref, d_one_ref, gain_one_ref, gain_lat_ref,
):
    total = jnp.sum(parts_ref[...].astype(WIDE), axis=0)
    rope = total[:, KVL:]
    rope = rope * cos_ref[...] - jnp.concatenate([rope[:, 64:], rope[:, :64]], axis=1) * sin_ref[...]
    source = lax.broadcasted_iota(jnp.int32, (128, 128), 0)
    target = lax.broadcasted_iota(jnp.int32, (128, 128), 1)
    fold = (target == source % 32 + 32 * (source // 64)).astype(WIDE)
    rope = jnp.dot(
        rope, fold, precision=lax.Precision.HIGHEST, preferred_element_type=WIDE
    ).astype(HALF)
    grad = total[:, :KVL]
    normed = norm_ref[...]
    scaled = grad * gain_ref[...]
    inner = jnp.mean(scaled * normed, axis=-1, keepdims=True)
    d_lat = (scale_ref[...] * (scaled - normed * inner)).astype(HALF)
    gain_lat = jnp.sum(grad * normed, axis=0, keepdims=True)
    lane = lax.broadcasted_iota(jnp.int32, (1, 128), 1)
    for e in range(16):
        moved = pltpu.roll(gain_lat, (KVL - 32 * e) % KVL, axis=1)[:, :128]
        gain_lat_ref[:, 128 * e : 128 * e + 128] = jnp.where(lane < 32, moved, 0.0)
    chip_ref[:, :KVL] = d_lat
    chip_ref[:, KVL:] = rope + logits_ref[...]
    d_one = dot_nt(d_lat, blk_ref[:, :KVL]) + dot_nt(rope, blk_ref[:, KVL:])
    d_one_ref[...] = d_one
    gain_one_ref[...] = jnp.sum(d_one * one_ref[...], axis=0, keepdims=True)


def latent_back(*operands):
    vmem = pl.BlockSpec(memory_space=pltpu.VMEM)
    return pl.pallas_call(
        latent_kernel,
        out_shape=(
            jax.ShapeDtypeStruct((OWN, 640), HALF),
            jax.ShapeDtypeStruct((OWN, D), WIDE),
            jax.ShapeDtypeStruct((1, D), WIDE),
            jax.ShapeDtypeStruct((1, D), WIDE),
        ),
        in_specs=[vmem] * 9,
        out_specs=(vmem,) * 4,
        compiler_params=pltpu.CompilerParams(vmem_limit_bytes=24 * 1024 * 1024),
        cost_estimate=pl.CostEstimate(flops=1, bytes_accessed=1, transcendentals=0),
    )(*operands)


def last_kernel(
    core_ref, chip_ref, other_ref, h_one_ref, h_two_ref, one_a_ref, one_b_ref, two_ref, lat_ref,
    out_ref,
):
    core = core_ref[0]
    chip, other = chip_ref[...], other_ref[...]
    rows = jnp.concatenate(
        [jnp.where(core == 0, chip, other), jnp.where(core == 0, other, chip)], axis=0
    )
    source = lax.broadcasted_iota(jnp.int32, (640, 384), 0)
    target = lax.broadcasted_iota(jnp.int32, (640, 384), 1)
    wanted = jnp.where(
        target < 288,
        target + 288 * core,
        jnp.where(target < 320, target + 288 + 32 * core, -1),
    )
    picked = dot_nn(rows, (source == wanted).astype(HALF)).astype(HALF)
    lane = lax.broadcasted_iota(jnp.int32, (2 * OWN, 384), 1)
    zero = jnp.zeros_like(picked)
    out = dot_tn(h_one_ref[...], jnp.where(lane < 288, picked, zero))
    out = out + dot_tn(h_two_ref[...], jnp.where(lane < 288, zero, picked))
    row = lax.broadcasted_iota(jnp.int32, (8, D), 0)
    gains = jnp.where(row == 0, one_a_ref[...] + one_b_ref[...], 0.0)
    gains = gains + jnp.where(row == 1, two_ref[...], 0.0) + jnp.where(row == 2, lat_ref[...], 0.0)
    place = lax.broadcasted_iota(jnp.int32, (8, 384), 0) + 320
    place = (place == lax.broadcasted_iota(jnp.int32, (8, 384), 1)).astype(HALF)
    out_ref[...] = (out + dot_tn(gains.astype(HALF), place)).astype(HALF)


def last_products(ci, *operands):
    vmem = pl.BlockSpec(memory_space=pltpu.VMEM)
    return pl.pallas_call(
        last_kernel,
        out_shape=jax.ShapeDtypeStruct((D, 384), HALF),
        in_specs=[pl.BlockSpec(memory_space=pltpu.SMEM)] + [vmem] * 8,
        out_specs=vmem,
        compiler_params=pltpu.CompilerParams(vmem_limit_bytes=24 * 1024 * 1024),
        cost_estimate=pl.CostEstimate(flops=1, bytes_accessed=1, transcendentals=0),
    )(ci.reshape(1), *operands)


def last_sum_kernel(parts_ref, out_ref):
    out_ref[...] = jnp.sum(parts_ref[...].astype(WIDE), axis=0).astype(HALF)


def sum_last(parts):
    vmem = pl.BlockSpec(memory_space=pltpu.VMEM)
    return pl.pallas_call(
        last_sum_kernel,
        out_shape=jax.ShapeDtypeStruct(parts.shape[1:], HALF),
        in_specs=[vmem],
        out_specs=vmem,
        cost_estimate=pl.CostEstimate(flops=1, bytes_accessed=1, transcendentals=0),
    )(parts)


def finish_kernel(sum_ref, sg_ref, su_ref, sd_ref, wq_ref, wo_ref, uk_ref, uv_ref):
    sg_ref[...] = sum_ref[:, 0:352].astype(WIDE)
    su_ref[...] = sum_ref[:, SHP : SHP + 352].astype(WIDE)
    sd_ref[...] = sum_ref[:, 2 * SHP : 3 * SHP].astype(WIDE).T[:352, :]
    wo_ref[...] = sum_ref[:, 1536:1792].astype(WIDE).T
    source = lax.broadcasted_iota(jnp.int32, (384, 384), 0)
    target = lax.broadcasted_iota(jnp.int32, (384, 384), 1)
    head, place = target // 192, target % 192
    wanted = jnp.where(
        place < 128,
        128 * head + place,
        256 + 32 * head + 64 * ((place - 128) // 32) + (place - 128) % 32,
    )
    wq_ref[...] = dot_nn(sum_ref[:, 1152:1536], (source == wanted).astype(HALF))
    for block in range(2):
        lanes = slice(128 * block, 128 * block + 128)
        uk_ref[:, lanes] = sum_ref[32 * block : 32 * block + 32, 1792:1920].astype(WIDE)
        uv_ref[:, lanes] = sum_ref[64 + 32 * block : 96 + 32 * block, 1792:1920].astype(WIDE)


def finish(total):
    vmem = pl.BlockSpec(memory_space=pltpu.VMEM)
    shapes = ((128, 352), (128, 352), (352, 128), (128, 384), (256, 128), (32, 256), (32, 256))
    return pl.pallas_call(
        finish_kernel,
        out_shape=tuple(jax.ShapeDtypeStruct(shape, WIDE) for shape in shapes),
        in_specs=[vmem],
        out_specs=(vmem,) * 7,
        cost_estimate=pl.CostEstimate(flops=1, bytes_accessed=1, transcendentals=0),
    )(total)


def pack_query_columns(w):
    return jnp.concatenate(
        [w[:, 0:128], w[:, 192:320], w[:, 128:160], w[:, 320:352], w[:, 160:192], w[:, 352:384]],
        axis=1,
    )


def pad_cols(w, width):
    return jnp.pad(w, ((0, 0), (0, width - w.shape[1])))


def silu_parts(gate):
    sig = jax.nn.sigmoid(gate)
    return gate * sig, sig * (1.0 + gate * (1.0 - sig))


def body(
    inputs,
    gain_attn,
    w_q,
    w_dkv,
    gain_latent,
    w_uk,
    w_uv,
    w_o,
    gain_ffn,
    w_router,
    w_sg,
    w_su,
    w_sd,
    w_eg,
    w_eu,
    w_ed,
    routes,
    seq_lengths,
    piece_starts,
    out_grad,
):
    zi, xi, yi, ci = (lax.axis_index(name) for name in ("z", "x", "y", "c"))
    ei = zi * 4 + xi
    ti = yi * 2 + ci

    def half_cols(value):
        return lax.dynamic_slice_in_dim(value, ci * (D // 2), D // 2, value.ndim - 1)

    def place_half(value):
        zero = jnp.zeros_like(value)
        return jnp.concatenate(
            [jnp.where(ci == 0, value, zero), jnp.where(ci == 0, zero, value)], axis=1
        )

    def swap_halves(v):
        return jnp.concatenate([v[:, 64:], v[:, :64]], axis=1)

    def ordered_cores(mine, other, axis):
        return jnp.concatenate(
            [jnp.where(ci == 0, mine, other), jnp.where(ci == 0, other, mine)], axis=axis
        )

    def both_cores(value, axis):
        return ordered_cores(value, swap_core(value), axis)

    def own_rows(value):
        return lax.dynamic_slice_in_dim(value, ti * OWN, OWN, 0)

    def sent_pieces(weight):
        return [
            lax.dynamic_index_in_dim(weight, (yi + by) % 4, 0, keepdims=False).astype(HALF)
            for by in range(4)
        ]

    def moved_pieces(sent):
        return [sent[0]] + [shift_y(sent[by], by) for by in (1, 2, 3)]

    gain_cols = jnp.stack([gain_attn, gain_ffn, jnp.pad(gain_latent, (0, 96))], axis=1)
    w_router_perm = w_router.reshape(128, 16, 4).transpose(0, 2, 1).reshape(128, EXPERTS)
    first_pack = jnp.concatenate(
        [
            w_dkv,
            w_router_perm,
            jnp.concatenate([w_uk, w_uv], axis=1).reshape(128, 128),
            pad_cols(gain_cols, 128),
            pack_query_columns(w_q),
            w_o.T,
        ],
        axis=1,
    ).astype(HALF)
    first_all = lax.all_gather(first_pack, EX, axis=0, tiled=True)
    gate_sent, up_sent, down_sent = sent_pieces(w_eg), sent_pieces(w_eu), sent_pieces(w_ed)
    gate_sent, up_sent, inputs_b, out_grad_b = lax.optimization_barrier(
        (gate_sent, up_sent, inputs, out_grad)
    )
    gate_pieces = moved_pieces(gate_sent)
    in_rows = gather_rows(inputs_b, yi, ci)
    g_rows = gather_rows(out_grad_b, yi, ci)
    second_pack = jnp.concatenate(
        [pad_cols(w_sg, SHP), pad_cols(w_su, SHP), pad_cols(w_sd.T, SHP)], axis=1
    ).astype(HALF)

    row_ids = ei * ROWS + jnp.arange(ROWS, dtype=jnp.int32)
    position, low, high = spans(row_ids, seq_lengths, piece_starts)
    inv_freq = 10000.0 ** (-(2.0 * jnp.arange(DR // 2, dtype=WIDE)) / DR)
    angles = position.astype(WIDE)[:, None] * inv_freq[None, :]
    cosine, sine = jnp.cos(angles), jnp.sin(angles)
    cos4 = jnp.concatenate([cosine] * 4, axis=1)
    sin4 = jnp.concatenate([-sine, -sine, sine, sine], axis=1)

    routes_t = routes.T
    expert_ids = 4 * lax.broadcasted_iota(jnp.int32, (16, 1, ROWS), 0) + yi
    named = jnp.max((routes_t[None] == expert_ids).astype(WIDE), axis=1)
    earlier = (
        lax.broadcasted_iota(jnp.int32, (ROWS, ROWS), 0)
        < lax.broadcasted_iota(jnp.int32, (ROWS, ROWS), 1)
    ).astype(HALF)
    rank = dot_nn(named.astype(HALF), earlier)
    slot_ids = lax.broadcasted_iota(jnp.int32, (16, SLOTS, ROWS), 1).astype(WIDE)
    picked = (named[:, None, :] > 0.5) & (rank[:, None, :] == slot_ids)
    select = picked.astype(HALF).reshape(16 * SLOTS, ROWS)

    in_wide = in_rows.astype(WIDE)
    normed_in = in_wide * inv_rms(in_wide)
    first_all, gate_pieces, up_sent, down_sent, second_pack = lax.optimization_barrier(
        (first_all, gate_pieces, up_sent, down_sent, second_pack)
    )
    normed_in, cos4, sin4, select = lax.optimization_barrier((normed_in, cos4, sin4, select))

    blk_b = first_all[:, 0:640]
    wkv_b = first_all[:, 640:768]
    pick = jnp.eye(8, 128, dtype=HALF)
    gains = dot_nt(pick, first_all[:, 768:896])
    wq_b = first_all[:, 896:1280]
    wot_b = first_all[:, 1280:1536]
    gain_one = gains[0]
    gain_two = gains[1]
    gain_lat = gains[2].reshape(16, 128)[:, :32].reshape(KVL)
    h_one = (normed_in * gain_one).astype(HALF)
    latent_all = dot_nn(h_one, blk_b)
    lat_part = latent_all[:, :KVL]
    scale_lat = inv_rms(lat_part)
    normed_lat = lat_part * scale_lat
    c_norm = (normed_lat * gain_lat).astype(HALF)
    rope_a, rope_b = latent_all[:, 512:544], latent_all[:, 544:576]
    rope = jnp.concatenate([rope_a, rope_a, rope_b, rope_b], axis=1)
    k_rot = rope * cos4 + swap_halves(rope) * sin4
    c_local = jnp.concatenate([c_norm, k_rot.astype(HALF)], axis=1)
    g_half = half_cols(g_rows)
    g_sent = dot_nn(select, g_half).astype(HALF).reshape(16, SLOTS, D // 2)
    c_local, up_sent, down_sent, g_sent, wq_b, wkv_b = lax.optimization_barrier(
        (c_local, up_sent, down_sent, g_sent, wq_b, wkv_b)
    )
    g_recv = spread(g_sent, EX).reshape(16 * SLOTS, D // 2)
    c_all = lax.all_gather(c_local, EX, axis=0, tiled=True)
    up_pieces = moved_pieces(up_sent)
    down_first = [down_sent[0], shift_y(down_sent[1], 1), None, shift_y(down_sent[3], 3)]
    wkv_b = wkv_b.reshape(KVL, 512)
    q_raw = dot_nn(h_one, wq_b)
    q_rot = q_raw[:, 256:]
    q_rot = q_rot * cos4 + swap_halves(q_rot) * sin4
    queries = jnp.concatenate([q_raw[:, :256], q_rot], axis=1).astype(HALF)
    c_all, queries, wot_b, wkv_b, up_pieces, down_first, g_recv, second_pack, down_sent = (
        lax.optimization_barrier(
            (c_all, queries, wot_b, wkv_b, up_pieces, down_first, g_recv, second_pack, down_sent)
        )
    )

    second_all = lax.all_gather(second_pack, EX, axis=0, tiled=True)
    kv_all = dot_nn(c_all[:, :KVL], wkv_b).astype(HALF)
    rot_all = c_all[:, KVL:]
    probs, heads_wide = attend(queries, kv_all, rot_all, low[None, :], high[None, :])
    attn_heads = heads_wide.astype(HALF)
    attn_own = sum_rows(dot_nt(attn_heads, wot_b).astype(HALF), yi, ci)

    in_own = inputs.astype(WIDE)
    mid_own = in_own + attn_own
    scale_two = inv_rms(mid_own)
    normed_two = mid_own * scale_two
    h_two_own = (normed_two * gain_two).astype(HALF)
    h_two = gather_rows(h_two_own, yi, ci)

    rope_router_b = blk_b[:, 512:640]
    logits_t = lax.dot_general(
        rope_router_b, h_two, (((0,), (1,)), ((), ())), preferred_element_type=WIDE
    )[64:]
    probs_t = jax.nn.softmax(logits_t, axis=0)
    gate_t = lax.dynamic_slice_in_dim(probs_t, yi * 16, 16, 0).astype(HALF).astype(WIDE)
    gated = jnp.where(picked, gate_t[:, None, :], 0.0)
    slot_gate = jnp.sum(gated, axis=2)
    gated = gated.astype(HALF).reshape(16 * SLOTS, ROWS)
    x_sent = dot_nn(select, half_cols(h_two)).astype(HALF).reshape(16, SLOTS, D // 2)
    slot_gate = jnp.broadcast_to(slot_gate[:, :, None], (16, SLOTS, 128)).astype(HALF)
    x_sent = jnp.concatenate([x_sent, slot_gate], axis=2)
    x_sent, g_own, down_sent, h_two = lax.optimization_barrier((x_sent, g_recv, down_sent, h_two))
    x_own = spread(x_sent, EX).reshape(16 * SLOTS, D // 2 + 128)
    g_other = swap_core(g_own)
    down_pieces = [down_first[0], down_first[1], shift_y(down_sent[2], 2), down_first[3]]

    wgu_b = second_all[:, : 2 * SHP]
    wsdt_b = second_all[:, 2 * SHP :]
    shared_pre = dot_nn(h_two, wgu_b)
    shared_gate, shared_up = shared_pre[:, :SHP], shared_pre[:, SHP:]
    shared_silu, shared_slope = silu_parts(shared_gate)
    shared_hidden = (shared_silu * shared_up).astype(HALF)
    shared_out = dot_nt(shared_hidden, wsdt_b)
    d_shared_hidden = dot_nn(g_rows, wsdt_b)
    d_shared_pre = jnp.concatenate(
        [d_shared_hidden * shared_up * shared_slope, d_shared_hidden * shared_silu], axis=1
    ).astype(HALF)
    d_shared_in = dot_nt(d_shared_pre, wgu_b)
    x_own, g_other, down_pieces, shared_out, d_shared_in, d_shared_pre, shared_hidden = (
        lax.optimization_barrier(
            (x_own, g_other, down_pieces, shared_out, d_shared_in, d_shared_pre, shared_hidden)
        )
    )

    x_other = swap_core(x_own)
    keep_in, send_in, keep_out, send_out, x_slots, d_slot_out, expert_hidden, d_expert_pre = (
        run_expert(
            ci, x_own, x_other, g_own, g_other, gate_pieces + up_pieces + down_pieces
        )
    )

    def pair(keep, send):
        return (keep.astype(WIDE) + swap_core(send).astype(WIDE)).astype(HALF)

    in_sent = pair(keep_in, send_in)
    grad_gate = dot_tn(d_expert_pre[:, :FFP], x_slots).astype(HALF)
    in_sent, grad_gate, keep_out, send_out, d_slot_out, expert_hidden, d_expert_pre = (
        lax.optimization_barrier(
            (in_sent, grad_gate, keep_out, send_out, d_slot_out, expert_hidden, d_expert_pre)
        )
    )
    in_recv = spread(in_sent.reshape(16, SLOTS, D // 2 + 128), EX)
    gate_back = [
        grad_gate[:FFS],
        shift_y(grad_gate[FFS : 2 * FFS], -1),
        None,
        shift_y(grad_gate[3 * FFS : FFH], -3),
    ]
    out_sent = pair(keep_out, send_out)
    up_parts, down_parts, far_parts = expert_grads(
        x_slots, d_slot_out, expert_hidden, d_expert_pre, grad_gate
    )
    in_recv, gate_back, up_parts, down_parts, far_parts = lax.optimization_barrier(
        (in_recv, gate_back, up_parts, down_parts, far_parts)
    )

    in_back = in_recv[:, :, : D // 2].reshape(16 * SLOTS, D // 2)
    slot_dots = in_recv[:, :, D // 2 : D // 2 + 1].astype(WIDE)
    d_route_t = jnp.sum(jnp.where(picked, slot_dots, 0.0), axis=1).astype(HALF)
    lane_at = (
        lax.broadcasted_iota(jnp.int32, (16, 128), 0) + yi * 16
        == lax.broadcasted_iota(jnp.int32, (16, 128), 1)
    ).astype(HALF)
    d_route_part = dot_tn(d_route_t, lane_at)
    d_h_part = d_shared_in + place_half(dot_tn(select, in_back))
    back_part = jnp.concatenate([d_h_part, d_route_part], axis=1).astype(HALF)
    back_own = sum_rows(back_part, yi, ci)

    logits_own = dot_nn(h_two_own, rope_router_b)[:, 64:]
    probs_own = jax.nn.softmax(logits_own, axis=-1)
    d_route = back_own[:, D : D + EXPERTS]
    d_logits = (
        probs_own * (d_route - jnp.sum(probs_own * d_route, axis=-1, keepdims=True))
    ).astype(HALF)
    d_logits_pad = jnp.pad(d_logits, ((0, 0), (64, 0)))
    d_h_two = back_own[:, :D] + dot_nt(d_logits_pad, rope_router_b)
    d_mid_norm, gain_two_part = norm_back(d_h_two, normed_two, scale_two, gain_two)
    d_mid_own = d_mid_norm + out_grad.astype(WIDE)
    d_attn_b = gather_rows(d_mid_own.astype(HALF), yi, ci)
    d_attn_b, up_parts = lax.optimization_barrier((d_attn_b, up_parts))

    up_back = [up_parts[0], shift_y(up_parts[1], -1), None, shift_y(up_parts[3], -3)]
    lat_keep, lat_send, d_kv, d_q = attend_back(
        ci, queries, kv_all, rot_all, probs, d_attn_b, wot_b, wkv_b, heads_wide
    )
    lat_keep, lat_send, d_kv, d_q, up_back = lax.optimization_barrier(
        (lat_keep, lat_send, d_kv, d_q, up_back)
    )
    lat_pieces = pair_pieces(lat_keep, lat_send, yi)
    lat_pieces, d_kv, d_q, d_attn_b, out_sent = lax.optimization_barrier(
        (lat_pieces, d_kv, d_q, d_attn_b, out_sent)
    )
    out_back = spread(out_sent.reshape(16, SLOTS, D // 2), EX).reshape(16 * SLOTS, D // 2)
    lat_total = add_pieces(lat_pieces)

    d_q_rot = d_q[:, 256:]
    d_q_rot = d_q_rot * cos4 - swap_halves(d_q_rot) * sin4
    d_queries = jnp.concatenate([d_q[:, :256], d_q_rot], axis=1).astype(HALF)
    rest_grads, d_one, gain_one_late = rest_products(
        h_two, d_shared_pre, g_rows, shared_hidden, h_one, d_queries, d_attn_b, attn_heads,
        c_all, d_kv, wq_b, normed_in,
    )
    lat_total, out_back, down_parts, rest_grads = lax.optimization_barrier(
        (lat_total.astype(HALF), out_back, down_parts, rest_grads)
    )
    rest_sum = lax.psum_scatter(rest_grads, EX, scatter_dimension=0, tiled=True)
    lat_parts = spread(lat_total, EX)
    down_back = [down_parts[0], shift_y(down_parts[1], -1), None, shift_y(down_parts[3], -3)]
    scale_one = inv_rms(in_own)
    normed_one = in_own * scale_one
    lat_own = (
        own_rows(cos4), own_rows(sin4), own_rows(normed_lat), own_rows(scale_lat), gain_lat[None]
    )
    lat_parts, down_back, far_parts, lat_own, normed_one = lax.optimization_barrier(
        (lat_parts, down_back, far_parts, lat_own, normed_one)
    )
    far_back = shift_y(far_parts, -2)
    chip, d_lat_one, gain_one_lat, gain_lat_wide = latent_back(
        lat_parts, *lat_own, blk_b, normed_one, d_logits_pad
    )
    chip, d_one, out_back = lax.optimization_barrier((chip, d_one, out_back))
    late_parts = late_products(ci, d_one, shared_out, gated, out_back).reshape(4, 2, OWN, 2 * D)
    late_pieces = pair_pieces(
        lax.dynamic_index_in_dim(late_parts, ci, 1, keepdims=False),
        lax.dynamic_index_in_dim(late_parts, 1 - ci, 1, keepdims=False),
        yi,
    )

    def chip_rows(value):
        return lax.dynamic_slice_in_dim(value, yi * 2 * OWN, 2 * OWN, 0)

    last_part = last_products(
        ci, chip, swap_core(chip), chip_rows(h_one), chip_rows(h_two),
        gain_one_late, gain_one_lat, gain_two_part[None], gain_lat_wide,
    )
    last_parts = spread(last_part.reshape(16, 128, 384), EX)
    last_parts, far_back, late_pieces = lax.optimization_barrier(
        (last_parts, far_back, late_pieces)
    )
    last_sum = sum_last(last_parts)
    last_sum = add_pieces([last_sum] * 4).astype(HALF)
    late_own = add_pieces(late_pieces)
    up_back[2] = gate_back[2] = down_back[2] = far_back
    grad_eg = place_pieces(yi, gate_back, 0)
    grad_eu = place_pieces(yi, up_back, 1)
    grad_ed = place_pieces(yi, down_back, 2)
    last_sum, late_own, grad_eg, grad_eu, grad_ed = lax.optimization_barrier(
        (last_sum, late_own, grad_eg, grad_eu, grad_ed)
    )
    last_other = swap_core(last_sum)
    sum_dkv = ordered_cores(last_sum[:, :288], last_other[:, :288], 1).astype(WIDE)
    sum_router = ordered_cores(last_sum[:, 288:320], last_other[:, 288:320], 1)
    sum_router = sum_router.reshape(128, 4, 16).transpose(0, 2, 1).reshape(128, EXPERTS).astype(WIDE)
    gain_sums = last_sum[:, 320:323].astype(WIDE) + last_other[:, 320:323].astype(WIDE)
    layer_out = (mid_own + late_own[:, D:]).astype(HALF)
    d_in_norm, _ = norm_back(late_own[:, :D] + d_lat_one, normed_one, scale_one, gain_one)
    grad_inputs = (d_mid_own + d_in_norm).astype(HALF)
    sum_sg, sum_su, sum_sd, sum_q, sum_o, sum_uk, sum_uv = finish(rest_sum)
    return (
        layer_out,
        grad_inputs,
        gain_sums[:, 0],
        sum_q,
        sum_dkv,
        gain_sums[:32, 2],
        sum_uk,
        sum_uv,
        sum_o,
        gain_sums[:, 1],
        sum_router,
        sum_sg,
        sum_su,
        sum_sd,
        grad_eg,
        grad_eu,
        grad_ed,
    )


def solution(mesh):
    grid = Mesh(mesh.devices.reshape(4, 4, 4, 2), ("z", "x", "y", "c"))
    ten = ("y", "c")
    rows = P(("z", "x", "y", "c"), None)
    wide = P(EX, ten)
    tall = P(ten, EX)
    expert = P(EX, ten, None)
    return jax.shard_map(
        body,
        mesh=grid,
        in_specs=(
            rows,
            P(EX),
            wide,
            P(EX, None),
            P(EX),
            wide,
            wide,
            tall,
            P(EX),
            P(EX, None),
            wide,
            wide,
            tall,
            expert,
            expert,
            expert,
            P(EX, None),
            P(),
            P(),
            rows,
        ),
        out_specs=(
            rows,
            rows,
            P(EX),
            wide,
            P(EX, None),
            P(EX),
            wide,
            wide,
            tall,
            P(EX),
            P(EX, None),
            wide,
            wide,
            tall,
            expert,
            expert,
            expert,
        ),
        check_vma=False,
    )
```

```python
import jax
import jax.numpy as jnp
from jax import lax
from jax.experimental import pallas as pl
from jax.experimental.layout import Layout, with_layout_constraint
from jax.experimental.pallas import tpu as pltpu
from jax.sharding import Mesh, PartitionSpec as P

D = 2048
H_DEV = 2
DN = 128
DV = 128
DR = 64
KVL = 512
PIECE = 256
EXPERTS = 64
ROWS = 256
OWN = 32
SLOTS = 40
FFH = 704
FFS = 176
FFP = 768
SHP = 384
KEYS = 4096
CHUNK = 512
EPS = 1e-06
NEG = -1e30
SCALE = (DN + DR) ** (-0.5)
EX = ("z", "x")
HALF = jnp.bfloat16
WIDE = jnp.float32


def dot_nn(left, right):
    return jnp.dot(left, right, preferred_element_type=WIDE)


def dot_nt(left, right):
    return lax.dot_general(left, right, (((1,), (1,)), ((), ())), preferred_element_type=WIDE)


def dot_tn(left, right):
    return lax.dot_general(left, right, (((0,), (0,)), ((), ())), preferred_element_type=WIDE)


def inv_rms(values):
    return lax.rsqrt(jnp.mean(values * values, axis=-1, keepdims=True) + EPS)


def norm_back(grad, normed, row_scale, gain):
    scaled = grad * gain
    inner_mean = jnp.mean(scaled * normed, axis=-1, keepdims=True)
    return (row_scale * (scaled - normed * inner_mean), jnp.sum(grad * normed, axis=0))


def row_major(value):
    return with_layout_constraint(value, Layout(major_to_minor=(0, 1)))


def swap_core(value):
    return lax.ppermute(value, "c", [(0, 1), (1, 0)])


def shift_y(value, by):
    return lax.ppermute(value, "y", [(i, (i + by) % 4) for i in range(4)])


def spread(value, axes):
    return lax.all_to_all(value, axes, split_axis=0, concat_axis=0, tiled=True)


def gather_rows(value, yi, ci):
    n = value.shape[1]
    block = jnp.zeros((4, OWN, n), value.dtype)
    block = lax.dynamic_update_slice(block, value[None], (yi, 0, 0))
    for by in (1, 2, 3):
        block = lax.dynamic_update_slice(block, shift_y(value, by)[None], ((yi - by) % 4, 0, 0))
    other = swap_core(block)
    first = jnp.where(ci == 0, block, other)
    second = jnp.where(ci == 0, other, block)
    return jnp.stack([first, second], axis=1).reshape(ROWS, n)


def pair_pieces(keep, send, yi):
    other = swap_core(send)
    pieces = []
    for by in range(4):
        at = (yi + by) % 4
        mine = lax.dynamic_index_in_dim(keep, at, 0, keepdims=False).astype(WIDE)
        theirs = lax.dynamic_index_in_dim(other, at, 0, keepdims=False).astype(WIDE)
        pieces.append((mine + theirs).astype(HALF))
    return pieces


def add_pieces(pieces):
    total = pieces[0].astype(WIDE)
    for by in (1, 2, 3):
        total = total + shift_y(pieces[by], by).astype(WIDE)
    return total


def sum_rows(value, yi, ci):
    parts = value.reshape(4, 2, OWN, value.shape[1])
    mine = lax.dynamic_index_in_dim(parts, ci, 1, keepdims=False)
    theirs = lax.dynamic_index_in_dim(parts, 1 - ci, 1, keepdims=False)
    return add_pieces(pair_pieces(mine, theirs, yi))


def sum_experts(value):
    rows, width = value.shape
    parts = spread(value.reshape(16, rows // 16, width), EX)
    return jnp.sum(parts.astype(WIDE), axis=0)


def spans(row_ids, seq_lengths, piece_starts):
    ends = jnp.cumsum(seq_lengths)
    starts = ends - seq_lengths
    member = (row_ids[:, None] >= starts[None, :]) & (row_ids[:, None] < ends[None, :])
    member = member.astype(jnp.int32)
    low = jnp.sum(member * starts[None, :], axis=1)
    end = jnp.sum(member * ends[None, :], axis=1)
    inside = (row_ids[:, None] >= piece_starts[None, :]) & (
        row_ids[:, None] < piece_starts[None, :] + PIECE
    )
    piece_last = jnp.max(jnp.where(inside, piece_starts[None, :] + (PIECE - 1), -1), axis=1)
    high = jnp.where(piece_last >= 0, jnp.minimum(piece_last, end - 1), row_ids)
    return row_ids - low, low, high


def head_query(q_ref, head):
    lane = lax.broadcasted_iota(jnp.int32, (ROWS, 128), 1)
    rot = q_ref[:, 256:384]
    rot = jnp.where((lane // 32) % 2 == head, rot, jnp.zeros_like(rot))
    return jnp.concatenate([q_ref[:, 128 * head : 128 * head + 128], rot], axis=1)


def attend_kernel(q_ref, kv_ref, rot_ref, low_ref, high_ref, p_ref, o_ref, s_ref):
    low = low_ref[...]
    high = high_ref[...]
    for head in range(H_DEV):
        query = head_query(q_ref, head)

        def scores_step(i, top):
            at = pl.multiple_of(i * CHUNK, CHUNK)
            key = jnp.concatenate(
                [
                    kv_ref[pl.ds(at, CHUNK), 128 * head : 128 * head + 128],
                    rot_ref[pl.ds(at, CHUNK), :],
                ],
                axis=1,
            )
            scores = dot_nt(key, query) * SCALE
            col = lax.broadcasted_iota(jnp.int32, (CHUNK, ROWS), 0) + at
            scores = jnp.where((col >= low) & (col <= high), scores, NEG)
            s_ref[pl.ds(at, CHUNK), :] = scores
            return jnp.maximum(top, jnp.max(scores.reshape(CHUNK // 8, 8, ROWS), axis=0))

        top = lax.fori_loop(
            0, KEYS // CHUNK, scores_step, jnp.full((8, ROWS), NEG, WIDE)
        )
        top = jnp.max(top, axis=0, keepdims=True)

        def exp_step(i, total):
            at = pl.multiple_of(i * CHUNK, CHUNK)
            weights = jnp.exp(s_ref[pl.ds(at, CHUNK), :] - top)
            s_ref[pl.ds(at, CHUNK), :] = weights
            return total + jnp.sum(weights.reshape(CHUNK // 8, 8, ROWS), axis=0)

        total = lax.fori_loop(0, KEYS // CHUNK, exp_step, jnp.zeros((8, ROWS), WIDE))
        inverse = 1.0 / jnp.sum(total, axis=0, keepdims=True)

        def value_step(i, acc):
            at = pl.multiple_of(i * CHUNK, CHUNK)
            probs = (s_ref[pl.ds(at, CHUNK), :] * inverse).astype(HALF)
            p_ref[head, pl.ds(at, CHUNK), :] = probs
            value = kv_ref[pl.ds(at, CHUNK), 256 + 128 * head : 384 + 128 * head]
            return acc + dot_tn(value, probs)

        out = lax.fori_loop(0, KEYS // CHUNK, value_step, jnp.zeros((DN, ROWS), WIDE))
        o_ref[:, 128 * head : 128 * head + 128] = out.T


def attend(queries, kv_all, rot_all, low, high):
    vmem = pl.BlockSpec(memory_space=pltpu.VMEM)
    return pl.pallas_call(
        attend_kernel,
        out_shape=(
            jax.ShapeDtypeStruct((H_DEV, KEYS, ROWS), HALF),
            jax.ShapeDtypeStruct((ROWS, H_DEV * DN), WIDE),
        ),
        in_specs=[vmem] * 5,
        out_specs=(vmem, vmem),
        scratch_shapes=[pltpu.VMEM((KEYS, ROWS), WIDE)],
        compiler_params=pltpu.CompilerParams(vmem_limit_bytes=40 * 1024 * 1024),
        cost_estimate=pl.CostEstimate(
            flops=2 * H_DEV * ROWS * KEYS * 384, bytes_accessed=12 << 20, transcendentals=2 << 20
        ),
    )(queries, kv_all, rot_all, low, high)


def attend_back_kernel(
    core_ref, q_ref, kv_ref, rot_ref, p_ref, dmid_ref, wot_ref, wkv_ref, o_ref,
    keep_ref, send_ref, dkv_ref, dq_ref, acc_ref, do_ref, delta_ref, qf_ref,
):
    step = pl.program_id(0)

    @pl.when(step == 0)
    def _():
        acc_ref[...] = jnp.zeros_like(acc_ref)
        d_heads = dot_nn(dmid_ref[...], wot_ref[...]).astype(HALF)
        do_ref[...] = d_heads
        product = d_heads.astype(WIDE) * o_ref[...]
        for head in range(H_DEV):
            delta_ref[8 * head : 8 * head + 8, :] = lax.dot_general(
                jnp.ones((8, 128), WIDE),
                product[:, 128 * head : 128 * head + 128],
                (((1,), (1,)), ((), ())),
                precision=lax.Precision.HIGHEST,
                preferred_element_type=WIDE,
            )
            qf_ref[head] = head_query(q_ref, head)

    rot = rot_ref[...]
    d_rot = jnp.zeros((CHUNK, 128), WIDE)
    for head in range(H_DEV):
        d_out = do_ref[:, 128 * head : 128 * head + 128]
        value = kv_ref[:, 256 + 128 * head : 384 + 128 * head]
        probs = p_ref[head]
        d_probs = dot_nt(value, d_out)
        d_scores = (
            probs.astype(WIDE) * (d_probs - delta_ref[8 * head : 8 * head + 1, :])
        ).astype(HALF)
        d_key = dot_nn(d_scores, qf_ref[head]) * SCALE
        dkv_ref[:, 128 * head : 128 * head + 128] = d_key[:, :128].astype(HALF)
        d_rot = d_rot + d_key[:, 128:]
        dkv_ref[:, 256 + 128 * head : 384 + 128 * head] = dot_nn(probs, d_out).astype(HALF)
        key = jnp.concatenate([kv_ref[:, 128 * head : 128 * head + 128], rot], axis=1)
        acc_ref[head] += dot_tn(key, d_scores)
    d_lat = dot_nt(dkv_ref[...], wkv_ref[...]).astype(HALF)
    d_rot = d_rot.astype(HALF)

    def write(target, core):
        for block in range(CHUNK // ROWS):
            for y in range(4):
                row = ROWS * block + OWN * (2 * y + core)
                target[y, block, :, :512] = d_lat[row : row + OWN]
                target[y, block, :, 512:] = d_rot[row : row + OWN]

    @pl.when(core_ref[0] == 0)
    def _():
        write(keep_ref, 0)
        write(send_ref, 1)

    @pl.when(core_ref[0] != 0)
    def _():
        write(keep_ref, 1)
        write(send_ref, 0)

    @pl.when(step == KEYS // CHUNK - 1)
    def _():
        lane = lax.broadcasted_iota(jnp.int32, (ROWS, 128), 1)
        d_q_rot = jnp.zeros((ROWS, 128), WIDE)
        for head in range(H_DEV):
            d_query = acc_ref[head].T * SCALE
            dq_ref[:, 128 * head : 128 * head + 128] = d_query[:, :128]
            d_q_rot = jnp.where((lane // 32) % 2 == head, d_query[:, 128:], d_q_rot)
        dq_ref[:, 256:384] = d_q_rot


def attend_back(ci, queries, kv_all, rot_all, probs, d_mid, wot, wkv, heads):
    def whole(*shape):
        return pl.BlockSpec(shape, lambda i, core: (0,) * len(shape))

    share = jax.ShapeDtypeStruct((4, 16, OWN, 640), HALF)
    share_spec = pl.BlockSpec((4, CHUNK // ROWS, OWN, 640), lambda i, core: (0, i, 0, 0))
    return pl.pallas_call(
        attend_back_kernel,
        out_shape=(
            share,
            share,
            jax.ShapeDtypeStruct((KEYS, 512), HALF),
            jax.ShapeDtypeStruct((ROWS, 384), WIDE),
        ),
        grid_spec=pltpu.PrefetchScalarGridSpec(
            num_scalar_prefetch=1,
            grid=(KEYS // CHUNK,),
            in_specs=[
                whole(ROWS, 384),
                pl.BlockSpec((CHUNK, 512), lambda i, core: (i, 0)),
                pl.BlockSpec((CHUNK, 128), lambda i, core: (i, 0)),
                pl.BlockSpec((H_DEV, CHUNK, ROWS), lambda i, core: (0, i, 0)),
                whole(ROWS, D),
                whole(D, 256),
                whole(KVL, 512),
                whole(ROWS, 256),
            ],
            out_specs=(
                share_spec,
                share_spec,
                pl.BlockSpec((CHUNK, 512), lambda i, core: (i, 0)),
                whole(ROWS, 384),
            ),
            scratch_shapes=[
                pltpu.VMEM((H_DEV, 256, ROWS), WIDE),
                pltpu.VMEM((ROWS, H_DEV * DV), HALF),
                pltpu.VMEM((8 * H_DEV, ROWS), WIDE),
                pltpu.VMEM((H_DEV, ROWS, 256), HALF),
            ],
        ),
        compiler_params=pltpu.CompilerParams(vmem_limit_bytes=32 * 1024 * 1024),
        cost_estimate=pl.CostEstimate(flops=1, bytes_accessed=1, transcendentals=0),
    )(ci.reshape(1), queries, kv_all, rot_all, probs, d_mid, wot, wkv, heads)


def expert_kernel(at_ref, x_ref, xo_ref, g_ref, go_ref, *rest):
    pieces = rest[:12]
    keep_in, send_in, keep_out, send_out = rest[12:16]
    saved = rest[16:20]
    wg_ref, wu_ref, wd_ref, dots_ref, x_out, dso_out, hid_out, dpre_out, sems = rest[20:]
    copies = []
    leaving = []

    def leave(i, source):
        copy = pltpu.make_async_copy(source, saved[i], sems.at[12 + i])
        copy.start()
        leaving.append(copy)

    for part, target in enumerate((wg_ref, wu_ref, wd_ref)):
        for k in range(4):
            copy = pltpu.make_async_copy(
                pieces[4 * part + k],
                target.at[pl.ds(FFS * k, FFS), :],
                sems.at[4 * part + k],
            )
            copy.start()
            copies.append(copy)
        target[FFH:, :] = jnp.zeros((FFP - FFH, D), HALF)
    first = at_ref[0] == 0
    half = D // 2
    own = x_ref[:, :half]
    other = xo_ref[:, :half]
    x_out[:, :half] = jnp.where(first, own, other)
    x_out[:, half:] = jnp.where(first, other, own)
    gate = x_ref[:, half : half + 1].astype(WIDE)
    own = (g_ref[...].astype(WIDE) * gate).astype(HALF)
    other = (go_ref[...].astype(WIDE) * gate).astype(HALF)
    dso_out[:, :half] = jnp.where(first, own, other)
    dso_out[:, half:] = jnp.where(first, other, own)
    leave(0, x_out)
    leave(1, dso_out)
    for copy in copies:
        copy.wait()

    def hidden_step(i, carry):
        at = pl.multiple_of(i * 256, 256)
        x = x_out[...]
        pre_gate = dot_nt(x, wg_ref[pl.ds(at, 256), :])
        pre_up = dot_nt(x, wu_ref[pl.ds(at, 256), :])
        d_hidden = dot_nt(dso_out[...], wd_ref[pl.ds(at, 256), :])
        sig = 1.0 / (1.0 + jnp.exp(-pre_gate))
        act = pre_gate * sig
        hid_out[:, pl.ds(at, 256)] = (act * pre_up).astype(HALF)
        slope = sig * (1.0 + pre_gate * (1.0 - sig))
        dpre_out[:, pl.ds(at, 256)] = (d_hidden * pre_up * slope).astype(HALF)
        dpre_out[:, pl.ds(pl.multiple_of(at + FFP, 256), 256)] = (d_hidden * act).astype(HALF)
        return carry

    lax.fori_loop(0, FFP // 256, hidden_step, 0)

    leave(2, hid_out)
    leave(3, dpre_out)
    dots_ref[...] = jnp.zeros_like(dots_ref)

    def output_step(i, carry):
        at = pl.multiple_of(i * 256, 256)
        to = pl.multiple_of((i % 4) * 256, 256)
        own_side = (i // 4) == at_ref[0]
        d_in = dot_nn(dpre_out[:, :FFP], wg_ref[:, pl.ds(at, 256)])
        d_in = d_in + dot_nn(dpre_out[:, FFP:], wu_ref[:, pl.ds(at, 256)])
        d_in = d_in.astype(HALF)
        out = dot_nn(hid_out[...], wd_ref[:, pl.ds(at, 256)])
        g = jnp.where(own_side, g_ref[:, pl.ds(to, 256)], go_ref[:, pl.ds(to, 256)])
        dots = out * g.astype(WIDE)
        dots_ref[...] += dots[:, :128] + dots[:, 128:]
        out = out.astype(HALF)

        @pl.when(own_side)
        def _():
            keep_in[:, pl.ds(to, 256)] = d_in
            keep_out[:, pl.ds(to, 256)] = out

        @pl.when(jnp.logical_not(own_side))
        def _():
            send_in[:, pl.ds(to, 256)] = d_in
            send_out[:, pl.ds(to, 256)] = out

        return carry

    lax.fori_loop(0, D // 256, output_step, 0)
    total = jnp.sum(dots_ref[...], axis=1, keepdims=True)
    keep_in[:, half:] = jnp.broadcast_to(total, (16 * SLOTS, 128)).astype(HALF)
    send_in[:, half:] = jnp.zeros((16 * SLOTS, 128), HALF)
    for copy in leaving:
        copy.wait()


def run_expert(ci, x_own, x_other, g_own, g_other, pieces):
    rows = 16 * SLOTS
    vmem = pl.BlockSpec(memory_space=pltpu.VMEM)
    return pl.pallas_call(
        expert_kernel,
        out_shape=(
            jax.ShapeDtypeStruct((rows, D // 2 + 128), HALF),
            jax.ShapeDtypeStruct((rows, D // 2 + 128), HALF),
            jax.ShapeDtypeStruct((rows, D // 2), HALF),
            jax.ShapeDtypeStruct((rows, D // 2), HALF),
            jax.ShapeDtypeStruct((rows, D), HALF),
            jax.ShapeDtypeStruct((rows, D), HALF),
            jax.ShapeDtypeStruct((rows, FFP), HALF),
            jax.ShapeDtypeStruct((rows, 2 * FFP), HALF),
        ),
        in_specs=[pl.BlockSpec(memory_space=pltpu.SMEM)]
        + [vmem] * 4
        + [pl.BlockSpec(memory_space=pl.ANY)] * 12,
        out_specs=(vmem,) * 4 + (pl.BlockSpec(memory_space=pl.ANY),) * 4,
        scratch_shapes=[pltpu.VMEM((FFP, D), HALF)] * 3
        + [
            pltpu.VMEM((rows, 128), WIDE),
            pltpu.VMEM((rows, D), HALF),
            pltpu.VMEM((rows, D), HALF),
            pltpu.VMEM((rows, FFP), HALF),
            pltpu.VMEM((rows, 2 * FFP), HALF),
            pltpu.SemaphoreType.DMA((16,)),
        ],
        compiler_params=pltpu.CompilerParams(vmem_limit_bytes=52 * 1024 * 1024),
        cost_estimate=pl.CostEstimate(
            flops=12 * rows * D * FFP, bytes_accessed=28 << 20, transcendentals=rows * FFP
        ),
    )(ci.reshape(1), x_own, x_other, g_own, g_other, *pieces)


def place_kernel(at_ref, *refs):
    out_ref = refs[4]
    step = pl.program_id(0)
    for k in range(4):

        @pl.when(step == k)
        def _():
            out_ref[0] = refs[k][...].astype(WIDE)


def place_pieces(yi, pieces, part):
    return pl.pallas_call(
        place_kernel,
        out_shape=jax.ShapeDtypeStruct((4, FFS, D), WIDE),
        grid_spec=pltpu.PrefetchScalarGridSpec(
            num_scalar_prefetch=1,
            grid=(4,),
            in_specs=[
                pl.BlockSpec((FFS, D), lambda k, at, i=i: (part if i == 2 else 0, 0))
                for i in range(4)
            ],
            out_specs=pl.BlockSpec((1, FFS, D), lambda k, at: ((at[0] + k) % 4, 0, 0)),
        ),
        compiler_params=pltpu.CompilerParams(vmem_limit_bytes=24 * 1024 * 1024),
        cost_estimate=pl.CostEstimate(flops=1, bytes_accessed=1, transcendentals=0),
    )(yi.reshape(1), *pieces)


def expert_grad_kernel(x_ref, dso_ref, hid_ref, dpre_ref, gate_ref, *rest):
    outs, far_ref = rest[:6], rest[6]
    targets, sems = rest[7:9], rest[9]
    copies = []

    def copy(source, target):
        moved = pltpu.make_async_copy(source, target, sems.at[len(copies)])
        moved.start()
        copies.append(moved)

    copy(gate_ref.at[pl.ds(2 * FFS, FFS), :], far_ref.at[pl.ds(0, FFS), :])
    for part, right in enumerate((x_ref, dso_ref)):
        target = targets[part]
        for c in range(FFP // 256):
            if part == 0:
                left = dpre_ref[:, FFP + 256 * c : FFP + 256 * c + 256]
            else:
                left = hid_ref[:, 256 * c : 256 * c + 256]
            target[256 * c : 256 * c + 256, :] = dot_tn(left, right[...]).astype(HALF)
        for i, k in enumerate((0, 1, 3)):
            copy(target.at[pl.ds(FFS * k, FFS), :], outs[3 * part + i])
        copy(target.at[pl.ds(2 * FFS, FFS), :], far_ref.at[pl.ds(FFS * (part + 1), FFS), :])
    for moved in copies:
        moved.wait()


def expert_grads(x_slots, d_slot_out, hidden, d_pre, grad_gate):
    vmem = pl.BlockSpec(memory_space=pltpu.VMEM)
    hbm = pl.BlockSpec(memory_space=pl.ANY)
    outs = pl.pallas_call(
        expert_grad_kernel,
        out_shape=(jax.ShapeDtypeStruct((FFS, D), HALF),) * 6
        + (jax.ShapeDtypeStruct((3 * FFS, D), HALF),),
        in_specs=[vmem] * 4 + [hbm],
        out_specs=(hbm,) * 7,
        scratch_shapes=[pltpu.VMEM((FFP, D), HALF)] * 2 + [pltpu.SemaphoreType.DMA((9,))],
        compiler_params=pltpu.CompilerParams(vmem_limit_bytes=40 * 1024 * 1024),
        cost_estimate=pl.CostEstimate(flops=1, bytes_accessed=1, transcendentals=0),
    )(x_slots, d_slot_out, hidden, d_pre, grad_gate)
    up_parts = [outs[0], outs[1], None, outs[2]]
    down_parts = [outs[3], outs[4], None, outs[5]]
    return up_parts, down_parts, outs[6]


def late_kernel(one_ref, so_ref, gated_ref, out_ref, core_ref, late_ref):
    late_ref[:, :D] = one_ref[...]
    routed = dot_tn(gated_ref[...], out_ref[...])
    half = D // 2
    first = (core_ref[0] == 0).astype(WIDE)
    late_ref[:, D : D + half] = (so_ref[:, :half] + routed * first).astype(HALF)
    late_ref[:, D + half :] = (so_ref[:, half:] + routed * (1.0 - first)).astype(HALF)


def late_products(ci, d_one, shared_out, gated, out_back):
    vmem = pl.BlockSpec(memory_space=pltpu.VMEM)
    return pl.pallas_call(
        late_kernel,
        out_shape=jax.ShapeDtypeStruct((ROWS, 2 * D), HALF),
        in_specs=[vmem] * 4 + [pl.BlockSpec(memory_space=pltpu.SMEM)],
        out_specs=vmem,
        compiler_params=pltpu.CompilerParams(vmem_limit_bytes=32 * 1024 * 1024),
        cost_estimate=pl.CostEstimate(flops=1, bytes_accessed=1, transcendentals=0),
    )(d_one, shared_out, gated, out_back, ci.reshape(1))


def rest_kernel(
    h_two_ref, dsp_ref, g_ref, sh_ref, h_one_ref, dq_ref, dmid_ref, heads_ref, c_ref, dkv_ref,
    wq_ref, norm_ref, out_ref, one_ref, gain_ref, kv_ref,
):
    d_one = dot_nt(dq_ref[...], wq_ref[...])
    one_ref[...] = d_one.astype(HALF)
    gain_ref[...] = jnp.sum(d_one * norm_ref[...], axis=0, keepdims=True)

    def step(i, carry):
        rows = pl.ds(pl.multiple_of(i * 256, 256), 256)
        out_ref[rows, 0:768] = dot_tn(h_two_ref[:, rows], dsp_ref[...]).astype(HALF)
        out_ref[rows, 768:1152] = dot_tn(g_ref[:, rows], sh_ref[...]).astype(HALF)
        out_ref[rows, 1152:1536] = dot_tn(h_one_ref[:, rows], dq_ref[...]).astype(HALF)
        out_ref[rows, 1536:1792] = dot_tn(dmid_ref[:, rows], heads_ref[...]).astype(HALF)
        return carry

    lax.fori_loop(0, D // 256, step, 0)
    kv_ref[...] = jnp.zeros_like(kv_ref)

    def kv_step(i, carry):
        rows = pl.ds(pl.multiple_of(i * CHUNK, CHUNK), CHUNK)
        kv_ref[...] += dot_tn(c_ref[rows, 0:KVL], dkv_ref[rows, :])
        return carry

    lax.fori_loop(0, KEYS // CHUNK, kv_step, 0)
    for e in range(16):
        for block in range(4):
            row = 128 * e + 32 * block
            out_ref[row : row + 32, 1792:1920] = kv_ref[
                32 * e : 32 * e + 32, 128 * block : 128 * block + 128
            ].astype(HALF)


def rest_products(*operands):
    vmem = pl.BlockSpec(memory_space=pltpu.VMEM)
    return pl.pallas_call(
        rest_kernel,
        out_shape=(
            jax.ShapeDtypeStruct((D, 1920), HALF),
            jax.ShapeDtypeStruct((ROWS, D), HALF),
            jax.ShapeDtypeStruct((1, D), WIDE),
        ),
        in_specs=[vmem] * 12,
        out_specs=(vmem,) * 3,
        scratch_shapes=[pltpu.VMEM((KVL, 512), WIDE)],
        compiler_params=pltpu.CompilerParams(vmem_limit_bytes=48 * 1024 * 1024),
        cost_estimate=pl.CostEstimate(flops=1, bytes_accessed=1, transcendentals=0),
    )(*operands)


def latent_kernel(
    parts_ref, cos_ref, sin_ref, norm_ref, scale_ref, gain_ref, blk_ref, one_ref, logits_ref,
    chip_ref, d_one_ref, gain_one_ref, gain_lat_ref,
):
    total = jnp.sum(parts_ref[...].astype(WIDE), axis=0)
    rope = total[:, KVL:]
    rope = rope * cos_ref[...] - jnp.concatenate([rope[:, 64:], rope[:, :64]], axis=1) * sin_ref[...]
    source = lax.broadcasted_iota(jnp.int32, (128, 128), 0)
    target = lax.broadcasted_iota(jnp.int32, (128, 128), 1)
    fold = (target == source % 32 + 32 * (source // 64)).astype(WIDE)
    rope = jnp.dot(
        rope, fold, precision=lax.Precision.HIGHEST, preferred_element_type=WIDE
    ).astype(HALF)
    grad = total[:, :KVL]
    normed = norm_ref[...]
    scaled = grad * gain_ref[...]
    inner = jnp.mean(scaled * normed, axis=-1, keepdims=True)
    d_lat = (scale_ref[...] * (scaled - normed * inner)).astype(HALF)
    gain_lat = jnp.sum(grad * normed, axis=0, keepdims=True)
    lane = lax.broadcasted_iota(jnp.int32, (1, 128), 1)
    for e in range(16):
        moved = pltpu.roll(gain_lat, (KVL - 32 * e) % KVL, axis=1)[:, :128]
        gain_lat_ref[:, 128 * e : 128 * e + 128] = jnp.where(lane < 32, moved, 0.0)
    chip_ref[:, :KVL] = d_lat
    chip_ref[:, KVL:] = rope + logits_ref[...]
    d_one = dot_nt(d_lat, blk_ref[:, :KVL]) + dot_nt(rope, blk_ref[:, KVL:])
    d_one_ref[...] = d_one
    gain_one_ref[...] = jnp.sum(d_one * one_ref[...], axis=0, keepdims=True)


def latent_back(*operands):
    vmem = pl.BlockSpec(memory_space=pltpu.VMEM)
    return pl.pallas_call(
        latent_kernel,
        out_shape=(
            jax.ShapeDtypeStruct((OWN, 640), HALF),
            jax.ShapeDtypeStruct((OWN, D), WIDE),
            jax.ShapeDtypeStruct((1, D), WIDE),
            jax.ShapeDtypeStruct((1, D), WIDE),
        ),
        in_specs=[vmem] * 9,
        out_specs=(vmem,) * 4,
        compiler_params=pltpu.CompilerParams(vmem_limit_bytes=24 * 1024 * 1024),
        cost_estimate=pl.CostEstimate(flops=1, bytes_accessed=1, transcendentals=0),
    )(*operands)


def last_kernel(
    core_ref, chip_ref, other_ref, h_one_ref, h_two_ref, one_a_ref, one_b_ref, two_ref, lat_ref,
    out_ref,
):
    core = core_ref[0]
    chip, other = chip_ref[...], other_ref[...]
    rows = jnp.concatenate(
        [jnp.where(core == 0, chip, other), jnp.where(core == 0, other, chip)], axis=0
    )
    source = lax.broadcasted_iota(jnp.int32, (640, 384), 0)
    target = lax.broadcasted_iota(jnp.int32, (640, 384), 1)
    wanted = jnp.where(
        target < 288,
        target + 288 * core,
        jnp.where(target < 320, target + 288 + 32 * core, -1),
    )
    picked = dot_nn(rows, (source == wanted).astype(HALF)).astype(HALF)
    lane = lax.broadcasted_iota(jnp.int32, (2 * OWN, 384), 1)
    zero = jnp.zeros_like(picked)
    out = dot_tn(h_one_ref[...], jnp.where(lane < 288, picked, zero))
    out = out + dot_tn(h_two_ref[...], jnp.where(lane < 288, zero, picked))
    row = lax.broadcasted_iota(jnp.int32, (8, D), 0)
    gains = jnp.where(row == 0, one_a_ref[...] + one_b_ref[...], 0.0)
    gains = gains + jnp.where(row == 1, two_ref[...], 0.0) + jnp.where(row == 2, lat_ref[...], 0.0)
    place = lax.broadcasted_iota(jnp.int32, (8, 384), 0) + 320
    place = (place == lax.broadcasted_iota(jnp.int32, (8, 384), 1)).astype(HALF)
    out_ref[...] = (out + dot_tn(gains.astype(HALF), place)).astype(HALF)


def last_products(ci, *operands):
    vmem = pl.BlockSpec(memory_space=pltpu.VMEM)
    return pl.pallas_call(
        last_kernel,
        out_shape=jax.ShapeDtypeStruct((D, 384), HALF),
        in_specs=[pl.BlockSpec(memory_space=pltpu.SMEM)] + [vmem] * 8,
        out_specs=vmem,
        compiler_params=pltpu.CompilerParams(vmem_limit_bytes=24 * 1024 * 1024),
        cost_estimate=pl.CostEstimate(flops=1, bytes_accessed=1, transcendentals=0),
    )(ci.reshape(1), *operands)


def last_sum_kernel(parts_ref, out_ref):
    out_ref[...] = jnp.sum(parts_ref[...].astype(WIDE), axis=0).astype(HALF)


def sum_last(parts):
    vmem = pl.BlockSpec(memory_space=pltpu.VMEM)
    return pl.pallas_call(
        last_sum_kernel,
        out_shape=jax.ShapeDtypeStruct(parts.shape[1:], HALF),
        in_specs=[vmem],
        out_specs=vmem,
        cost_estimate=pl.CostEstimate(flops=1, bytes_accessed=1, transcendentals=0),
    )(parts)


def finish_kernel(sum_ref, sg_ref, su_ref, sd_ref, wq_ref, wo_ref, uk_ref, uv_ref):
    sg_ref[...] = sum_ref[:, 0:352].astype(WIDE)
    su_ref[...] = sum_ref[:, SHP : SHP + 352].astype(WIDE)
    sd_ref[...] = sum_ref[:, 2 * SHP : 3 * SHP].astype(WIDE).T[:352, :]
    wo_ref[...] = sum_ref[:, 1536:1792].astype(WIDE).T
    source = lax.broadcasted_iota(jnp.int32, (384, 384), 0)
    target = lax.broadcasted_iota(jnp.int32, (384, 384), 1)
    head, place = target // 192, target % 192
    wanted = jnp.where(
        place < 128,
        128 * head + place,
        256 + 32 * head + 64 * ((place - 128) // 32) + (place - 128) % 32,
    )
    wq_ref[...] = dot_nn(sum_ref[:, 1152:1536], (source == wanted).astype(HALF))
    for block in range(2):
        lanes = slice(128 * block, 128 * block + 128)
        uk_ref[:, lanes] = sum_ref[32 * block : 32 * block + 32, 1792:1920].astype(WIDE)
        uv_ref[:, lanes] = sum_ref[64 + 32 * block : 96 + 32 * block, 1792:1920].astype(WIDE)


def finish(total):
    vmem = pl.BlockSpec(memory_space=pltpu.VMEM)
    shapes = ((128, 352), (128, 352), (352, 128), (128, 384), (256, 128), (32, 256), (32, 256))
    return pl.pallas_call(
        finish_kernel,
        out_shape=tuple(jax.ShapeDtypeStruct(shape, WIDE) for shape in shapes),
        in_specs=[vmem],
        out_specs=(vmem,) * 7,
        cost_estimate=pl.CostEstimate(flops=1, bytes_accessed=1, transcendentals=0),
    )(total)


def spots(rows, cols, wanted):
    source = lax.broadcasted_iota(jnp.int32, (rows, cols), 0)
    target = lax.broadcasted_iota(jnp.int32, (rows, cols), 1)
    return (source == wanted(target)).astype(HALF)


def pack_kernel(dkv_ref, router_ref, uk_ref, uv_ref, gains_ref, wq_ref, wo_ref, out_ref):
    out_ref[:, 0:512] = dkv_ref[0:512, :].T.astype(HALF)
    rope = dot_tn(dkv_ref[512:576, :].astype(HALF), spots(64, 128, lambda j: j))
    router = dot_tn(
        router_ref[...].astype(HALF),
        spots(64, 128, lambda j: jnp.where(j < 64, -1, 4 * (j % 16) + (j - 64) // 16)),
    )
    out_ref[:, 512:640] = (rope + router).astype(HALF)
    for block in range(2):
        lanes = slice(128 * block, 128 * block + 128)
        out_ref[32 * block : 32 * block + 32, 640:768] = uk_ref[:, lanes].astype(HALF)
        out_ref[64 + 32 * block : 96 + 32 * block, 640:768] = uv_ref[:, lanes].astype(HALF)
    out_ref[:, 768:896] = dot_tn(gains_ref[...].astype(HALF), spots(8, 128, lambda j: j)).astype(HALF)

    def query_column(j):
        rot = j - 256
        return jnp.where(
            j < 256,
            j + 64 * (j // 128),
            128 + 192 * ((rot // 32) % 2) + 32 * (rot // 64) + rot % 32,
        )

    out_ref[:, 896:1280] = dot_nn(
        wq_ref[...].astype(HALF), spots(384, 384, query_column)
    ).astype(HALF)
    out_ref[:, 1280:1536] = wo_ref[...].T.astype(HALF)


def pack_first(*operands):
    vmem = pl.BlockSpec(memory_space=pltpu.VMEM)
    return pl.pallas_call(
        pack_kernel,
        out_shape=jax.ShapeDtypeStruct((128, 1536), HALF),
        in_specs=[vmem] * 7,
        out_specs=vmem,
        cost_estimate=pl.CostEstimate(flops=1, bytes_accessed=1, transcendentals=0),
    )(*operands)


def pad_cols(w, width):
    return jnp.pad(w, ((0, 0), (0, width - w.shape[1])))


def silu_parts(gate):
    sig = jax.nn.sigmoid(gate)
    return gate * sig, sig * (1.0 + gate * (1.0 - sig))


def body(
    inputs,
    gain_attn,
    w_q,
    w_dkv,
    gain_latent,
    w_uk,
    w_uv,
    w_o,
    gain_ffn,
    w_router,
    w_sg,
    w_su,
    w_sd,
    w_eg,
    w_eu,
    w_ed,
    routes,
    seq_lengths,
    piece_starts,
    out_grad,
):
    zi, xi, yi, ci = (lax.axis_index(name) for name in ("z", "x", "y", "c"))
    ei = zi * 4 + xi
    ti = yi * 2 + ci

    def half_cols(value):
        return lax.dynamic_slice_in_dim(value, ci * (D // 2), D // 2, value.ndim - 1)

    def place_half(value):
        zero = jnp.zeros_like(value)
        return jnp.concatenate(
            [jnp.where(ci == 0, value, zero), jnp.where(ci == 0, zero, value)], axis=1
        )

    def swap_halves(v):
        return jnp.concatenate([v[:, 64:], v[:, :64]], axis=1)

    def ordered_cores(mine, other, axis):
        return jnp.concatenate(
            [jnp.where(ci == 0, mine, other), jnp.where(ci == 0, other, mine)], axis=axis
        )

    def both_cores(value, axis):
        return ordered_cores(value, swap_core(value), axis)

    def own_rows(value):
        return lax.dynamic_slice_in_dim(value, ti * OWN, OWN, 0)

    def sent_pieces(weight):
        return [
            lax.dynamic_index_in_dim(weight, (yi + by) % 4, 0, keepdims=False).astype(HALF)
            for by in range(4)
        ]

    def moved_pieces(sent):
        return [sent[0]] + [shift_y(sent[by], by) for by in (1, 2, 3)]

    gain_own = jnp.stack([gain_attn, gain_ffn, jnp.pad(gain_latent, (0, 96))], axis=0)
    first_pack = pack_first(
        w_dkv.T, w_router.T, w_uk, w_uv, jnp.pad(gain_own, ((0, 5), (0, 0))), w_q, w_o
    )
    first_all = lax.all_gather(first_pack, EX, axis=0, tiled=True)
    gate_sent, up_sent, down_sent = sent_pieces(w_eg), sent_pieces(w_eu), sent_pieces(w_ed)
    gate_sent, up_sent, inputs_b, out_grad_b = lax.optimization_barrier(
        (gate_sent, up_sent, inputs, out_grad)
    )
    gate_pieces = moved_pieces(gate_sent)
    in_rows = gather_rows(inputs_b, yi, ci)
    g_rows = gather_rows(out_grad_b, yi, ci)
    second_pack = jnp.concatenate(
        [pad_cols(w_sg, SHP), pad_cols(w_su, SHP), pad_cols(w_sd.T, SHP)], axis=1
    ).astype(HALF)

    row_ids = ei * ROWS + jnp.arange(ROWS, dtype=jnp.int32)
    position, low, high = spans(row_ids, seq_lengths, piece_starts)
    inv_freq = 10000.0 ** (-(2.0 * jnp.arange(DR // 2, dtype=WIDE)) / DR)
    angles = position.astype(WIDE)[:, None] * inv_freq[None, :]
    cosine, sine = jnp.cos(angles), jnp.sin(angles)
    cos4 = jnp.concatenate([cosine] * 4, axis=1)
    sin4 = jnp.concatenate([-sine, -sine, sine, sine], axis=1)

    routes_t = routes.T
    expert_ids = 4 * lax.broadcasted_iota(jnp.int32, (16, 1, ROWS), 0) + yi
    named = jnp.max((routes_t[None] == expert_ids).astype(WIDE), axis=1)
    earlier = (
        lax.broadcasted_iota(jnp.int32, (ROWS, ROWS), 0)
        < lax.broadcasted_iota(jnp.int32, (ROWS, ROWS), 1)
    ).astype(HALF)
    rank = dot_nn(named.astype(HALF), earlier)
    slot_ids = lax.broadcasted_iota(jnp.int32, (16, SLOTS, ROWS), 1).astype(WIDE)
    picked = (named[:, None, :] > 0.5) & (rank[:, None, :] == slot_ids)
    select = picked.astype(HALF).reshape(16 * SLOTS, ROWS)

    in_wide = in_rows.astype(WIDE)
    normed_in = in_wide * inv_rms(in_wide)
    first_all, gate_pieces, up_sent, down_sent, second_pack = lax.optimization_barrier(
        (first_all, gate_pieces, up_sent, down_sent, second_pack)
    )
    normed_in, cos4, sin4, select = lax.optimization_barrier((normed_in, cos4, sin4, select))

    blk_b = first_all[:, 0:640]
    wkv_b = first_all[:, 640:768]
    pick = jnp.eye(8, 128, dtype=HALF)
    gains = dot_nt(pick, first_all[:, 768:896])
    wq_b = first_all[:, 896:1280]
    wot_b = first_all[:, 1280:1536]
    gain_one = gains[0]
    gain_two = gains[1]
    gain_lat = gains[2].reshape(16, 128)[:, :32].reshape(KVL)
    h_one = (normed_in * gain_one).astype(HALF)
    latent_all = dot_nn(h_one, blk_b)
    lat_part = latent_all[:, :KVL]
    scale_lat = inv_rms(lat_part)
    normed_lat = lat_part * scale_lat
    c_norm = (normed_lat * gain_lat).astype(HALF)
    rope_a, rope_b = latent_all[:, 512:544], latent_all[:, 544:576]
    rope = jnp.concatenate([rope_a, rope_a, rope_b, rope_b], axis=1)
    k_rot = rope * cos4 + swap_halves(rope) * sin4
    c_local = jnp.concatenate([c_norm, k_rot.astype(HALF)], axis=1)
    g_half = half_cols(g_rows)
    g_sent = dot_nn(select, g_half).astype(HALF).reshape(16, SLOTS, D // 2)
    c_local, up_sent, down_sent, g_sent, wq_b, wkv_b = lax.optimization_barrier(
        (c_local, up_sent, down_sent, g_sent, wq_b, wkv_b)
    )
    g_recv = spread(g_sent, EX).reshape(16 * SLOTS, D // 2)
    c_all = lax.all_gather(c_local, EX, axis=0, tiled=True)
    up_pieces = moved_pieces(up_sent)
    down_first = [down_sent[0], shift_y(down_sent[1], 1), None, shift_y(down_sent[3], 3)]
    wkv_b = wkv_b.reshape(16, 4, 32, 128).transpose(0, 2, 1, 3).reshape(KVL, 512)
    q_raw = dot_nn(h_one, wq_b)
    q_rot = q_raw[:, 256:]
    q_rot = q_rot * cos4 + swap_halves(q_rot) * sin4
    queries = jnp.concatenate([q_raw[:, :256], q_rot], axis=1).astype(HALF)
    c_all, queries, wot_b, wkv_b, up_pieces, down_first, g_recv, second_pack, down_sent = (
        lax.optimization_barrier(
            (c_all, queries, wot_b, wkv_b, up_pieces, down_first, g_recv, second_pack, down_sent)
        )
    )

    second_all = lax.all_gather(second_pack, EX, axis=0, tiled=True)
    kv_all = dot_nn(c_all[:, :KVL], wkv_b).astype(HALF)
    rot_all = c_all[:, KVL:]
    probs, heads_wide = attend(queries, kv_all, rot_all, low[None, :], high[None, :])
    attn_heads = heads_wide.astype(HALF)
    attn_own = sum_rows(dot_nt(attn_heads, wot_b).astype(HALF), yi, ci)

    in_own = inputs.astype(WIDE)
    mid_own = in_own + attn_own
    scale_two = inv_rms(mid_own)
    normed_two = mid_own * scale_two
    h_two_own = (normed_two * gain_two).astype(HALF)
    h_two = gather_rows(h_two_own, yi, ci)

    rope_router_b = blk_b[:, 512:640]
    logits_t = lax.dot_general(
        rope_router_b, h_two, (((0,), (1,)), ((), ())), preferred_element_type=WIDE
    )[64:]
    probs_t = jax.nn.softmax(logits_t, axis=0)
    gate_t = lax.dynamic_slice_in_dim(probs_t, yi * 16, 16, 0).astype(HALF).astype(WIDE)
    gated = jnp.where(picked, gate_t[:, None, :], 0.0)
    slot_gate = jnp.sum(gated, axis=2)
    gated = gated.astype(HALF).reshape(16 * SLOTS, ROWS)
    x_sent = dot_nn(select, half_cols(h_two)).astype(HALF).reshape(16, SLOTS, D // 2)
    slot_gate = jnp.broadcast_to(slot_gate[:, :, None], (16, SLOTS, 128)).astype(HALF)
    x_sent = jnp.concatenate([x_sent, slot_gate], axis=2)
    x_sent, g_own, down_sent, h_two = lax.optimization_barrier((x_sent, g_recv, down_sent, h_two))
    x_own = spread(x_sent, EX).reshape(16 * SLOTS, D // 2 + 128)
    g_other = swap_core(g_own)
    down_pieces = [down_first[0], down_first[1], shift_y(down_sent[2], 2), down_first[3]]

    wgu_b = second_all[:, : 2 * SHP]
    wsdt_b = second_all[:, 2 * SHP :]
    shared_pre = dot_nn(h_two, wgu_b)
    shared_gate, shared_up = shared_pre[:, :SHP], shared_pre[:, SHP:]
    shared_silu, shared_slope = silu_parts(shared_gate)
    shared_hidden = (shared_silu * shared_up).astype(HALF)
    shared_out = dot_nt(shared_hidden, wsdt_b)
    d_shared_hidden = dot_nn(g_rows, wsdt_b)
    d_shared_pre = jnp.concatenate(
        [d_shared_hidden * shared_up * shared_slope, d_shared_hidden * shared_silu], axis=1
    ).astype(HALF)
    d_shared_in = dot_nt(d_shared_pre, wgu_b)
    x_own, g_other, down_pieces, shared_out, d_shared_in, d_shared_pre, shared_hidden = (
        lax.optimization_barrier(
            (x_own, g_other, down_pieces, shared_out, d_shared_in, d_shared_pre, shared_hidden)
        )
    )

    x_other = swap_core(x_own)
    keep_in, send_in, keep_out, send_out, x_slots, d_slot_out, expert_hidden, d_expert_pre = (
        run_expert(
            ci, x_own, x_other, g_own, g_other, gate_pieces + up_pieces + down_pieces
        )
    )

    def pair(keep, send):
        return (keep.astype(WIDE) + swap_core(send).astype(WIDE)).astype(HALF)

    in_sent = pair(keep_in, send_in)
    grad_gate = dot_tn(d_expert_pre[:, :FFP], x_slots).astype(HALF)
    in_sent, grad_gate, keep_out, send_out, d_slot_out, expert_hidden, d_expert_pre = (
        lax.optimization_barrier(
            (in_sent, grad_gate, keep_out, send_out, d_slot_out, expert_hidden, d_expert_pre)
        )
    )
    in_recv = spread(in_sent.reshape(16, SLOTS, D // 2 + 128), EX)
    gate_back = [
        grad_gate[:FFS],
        shift_y(grad_gate[FFS : 2 * FFS], -1),
        None,
        shift_y(grad_gate[3 * FFS : FFH], -3),
    ]
    out_sent = pair(keep_out, send_out)
    up_parts, down_parts, far_parts = expert_grads(
        x_slots, d_slot_out, expert_hidden, d_expert_pre, grad_gate
    )
    in_recv, gate_back, up_parts, down_parts, far_parts = lax.optimization_barrier(
        (in_recv, gate_back, up_parts, down_parts, far_parts)
    )

    in_back = in_recv[:, :, : D // 2].reshape(16 * SLOTS, D // 2)
    slot_dots = in_recv[:, :, D // 2 : D // 2 + 1].astype(WIDE)
    d_route_t = jnp.sum(jnp.where(picked, slot_dots, 0.0), axis=1).astype(HALF)
    lane_at = (
        lax.broadcasted_iota(jnp.int32, (16, 128), 0) + yi * 16
        == lax.broadcasted_iota(jnp.int32, (16, 128), 1)
    ).astype(HALF)
    d_route_part = dot_tn(d_route_t, lane_at)
    d_h_part = d_shared_in + place_half(dot_tn(select, in_back))
    back_part = jnp.concatenate([d_h_part, d_route_part], axis=1).astype(HALF)
    back_own = sum_rows(back_part, yi, ci)

    logits_own = dot_nn(h_two_own, rope_router_b)[:, 64:]
    probs_own = jax.nn.softmax(logits_own, axis=-1)
    d_route = back_own[:, D : D + EXPERTS]
    d_logits = (
        probs_own * (d_route - jnp.sum(probs_own * d_route, axis=-1, keepdims=True))
    ).astype(HALF)
    d_logits_pad = jnp.pad(d_logits, ((0, 0), (64, 0)))
    d_h_two = back_own[:, :D] + dot_nt(d_logits_pad, rope_router_b)
    d_mid_norm, gain_two_part = norm_back(d_h_two, normed_two, scale_two, gain_two)
    d_mid_own = d_mid_norm + out_grad.astype(WIDE)
    d_attn_b = gather_rows(d_mid_own.astype(HALF), yi, ci)
    d_attn_b, up_parts = lax.optimization_barrier((d_attn_b, up_parts))

    up_back = [up_parts[0], shift_y(up_parts[1], -1), None, shift_y(up_parts[3], -3)]
    lat_keep, lat_send, d_kv, d_q = attend_back(
        ci, queries, kv_all, rot_all, probs, d_attn_b, wot_b, wkv_b, heads_wide
    )
    lat_keep, lat_send, d_kv, d_q, up_back = lax.optimization_barrier(
        (lat_keep, lat_send, d_kv, d_q, up_back)
    )
    lat_pieces = pair_pieces(lat_keep, lat_send, yi)
    lat_pieces, d_kv, d_q, d_attn_b, out_sent = lax.optimization_barrier(
        (lat_pieces, d_kv, d_q, d_attn_b, out_sent)
    )
    out_back = spread(out_sent.reshape(16, SLOTS, D // 2), EX).reshape(16 * SLOTS, D // 2)
    lat_total = add_pieces(lat_pieces)

    d_q_rot = d_q[:, 256:]
    d_q_rot = d_q_rot * cos4 - swap_halves(d_q_rot) * sin4
    d_queries = jnp.concatenate([d_q[:, :256], d_q_rot], axis=1).astype(HALF)
    rest_grads, d_one, gain_one_late = rest_products(
        h_two, d_shared_pre, g_rows, shared_hidden, h_one, d_queries, d_attn_b, attn_heads,
        c_all, d_kv, wq_b, normed_in,
    )
    lat_total, out_back, down_parts, rest_grads = lax.optimization_barrier(
        (lat_total.astype(HALF), out_back, down_parts, rest_grads)
    )
    rest_sum = lax.psum_scatter(rest_grads, EX, scatter_dimension=0, tiled=True)
    lat_parts = spread(lat_total, EX)
    down_back = [down_parts[0], shift_y(down_parts[1], -1), None, shift_y(down_parts[3], -3)]
    scale_one = inv_rms(in_own)
    normed_one = in_own * scale_one
    lat_own = (
        own_rows(cos4), own_rows(sin4), own_rows(normed_lat), own_rows(scale_lat), gain_lat[None]
    )
    lat_parts, down_back, far_parts, lat_own, normed_one = lax.optimization_barrier(
        (lat_parts, down_back, far_parts, lat_own, normed_one)
    )
    far_back = shift_y(far_parts, -2)
    chip, d_lat_one, gain_one_lat, gain_lat_wide = latent_back(
        lat_parts, *lat_own, blk_b, normed_one, d_logits_pad
    )
    chip, d_one, out_back = lax.optimization_barrier((chip, d_one, out_back))
    late_parts = late_products(ci, d_one, shared_out, gated, out_back).reshape(4, 2, OWN, 2 * D)
    late_pieces = pair_pieces(
        lax.dynamic_index_in_dim(late_parts, ci, 1, keepdims=False),
        lax.dynamic_index_in_dim(late_parts, 1 - ci, 1, keepdims=False),
        yi,
    )

    def chip_rows(value):
        return lax.dynamic_slice_in_dim(value, yi * 2 * OWN, 2 * OWN, 0)

    last_part = last_products(
        ci, chip, swap_core(chip), chip_rows(h_one), chip_rows(h_two),
        gain_one_late, gain_one_lat, gain_two_part[None], gain_lat_wide,
    )
    last_parts = spread(last_part.reshape(16, 128, 384), EX)
    last_parts, far_back, late_pieces = lax.optimization_barrier(
        (last_parts, far_back, late_pieces)
    )
    last_sum = sum_last(last_parts)
    last_sum = add_pieces([last_sum] * 4).astype(HALF)
    late_own = add_pieces(late_pieces)
    up_back[2] = gate_back[2] = down_back[2] = far_back
    grad_eg = place_pieces(yi, gate_back, 0)
    grad_eu = place_pieces(yi, up_back, 1)
    grad_ed = place_pieces(yi, down_back, 2)
    last_sum, late_own, grad_eg, grad_eu, grad_ed = lax.optimization_barrier(
        (last_sum, late_own, grad_eg, grad_eu, grad_ed)
    )
    last_other = swap_core(last_sum)
    sum_dkv = ordered_cores(last_sum[:, :288], last_other[:, :288], 1).astype(WIDE)
    sum_router = ordered_cores(last_sum[:, 288:320], last_other[:, 288:320], 1)
    sum_router = sum_router.reshape(128, 4, 16).transpose(0, 2, 1).reshape(128, EXPERTS).astype(WIDE)
    gain_sums = last_sum[:, 320:323].astype(WIDE) + last_other[:, 320:323].astype(WIDE)
    layer_out = (mid_own + late_own[:, D:]).astype(HALF)
    d_in_norm, _ = norm_back(late_own[:, :D] + d_lat_one, normed_one, scale_one, gain_one)
    grad_inputs = (d_mid_own + d_in_norm).astype(HALF)
    sum_sg, sum_su, sum_sd, sum_q, sum_o, sum_uk, sum_uv = finish(rest_sum)
    return (
        layer_out,
        grad_inputs,
        gain_sums[:, 0],
        sum_q,
        sum_dkv,
        gain_sums[:32, 2],
        sum_uk,
        sum_uv,
        sum_o,
        gain_sums[:, 1],
        sum_router,
        sum_sg,
        sum_su,
        sum_sd,
        grad_eg,
        grad_eu,
        grad_ed,
    )


def solution(mesh):
    grid = Mesh(mesh.devices.reshape(4, 4, 4, 2), ("z", "x", "y", "c"))
    ten = ("y", "c")
    rows = P(("z", "x", "y", "c"), None)
    wide = P(EX, ten)
    tall = P(ten, EX)
    expert = P(EX, ten, None)
    return jax.shard_map(
        body,
        mesh=grid,
        in_specs=(
            rows,
            P(EX),
            wide,
            P(EX, None),
            P(EX),
            wide,
            wide,
            tall,
            P(EX),
            P(EX, None),
            wide,
            wide,
            tall,
            expert,
            expert,
            expert,
            P(EX, None),
            P(),
            P(),
            rows,
        ),
        out_specs=(
            rows,
            rows,
            P(EX),
            wide,
            P(EX, None),
            P(EX),
            wide,
            wide,
            tall,
            P(EX),
            P(EX, None),
            wide,
            wide,
            tall,
            expert,
            expert,
            expert,
        ),
        check_vma=False,
    )
```
